128 devices in a mesh: wide: 16 (over z, x_lo, core), narrow: 8 (over y, x_hi).
Axes of the slice: x: 4 (x_hi: 2, x_lo: 2; x = x_hi * 2 + x_lo), y: 4, z: 4, core: 2. Of those that a mesh axis runs over, the one named last changes fastest.
Arguments:
- signal: bfloat16 [4, 8388608], P(None, ('wide', 'narrow')), may hold values from -6 to 6
- gate: bfloat16 [4, 8388608], P(None, ('wide', 'narrow')), may hold values from -6 to 6
- skip: float32 [4], replicated, may hold values from 0.5 to 2
- spectrum: float32 [2, 4, 256, 256, 256], P(None, None, ('wide', 'narrow')), may hold values from -6 to 6
Outputs:
- mixed: bfloat16 [4, 8388608], P(None, ('wide', 'narrow'))
The draws below stay inside these ranges and needn't reach their ends.
All inputs are finite; a program needn't handle non-finite values.
Results may differ from the reference program's by a relative error of at most 0.001.
Values may be sent and summed in bfloat16 or wider, within the bound.
No kernel may reach another device: no remote copies, remote signals or barrier semaphores. Data moves between devices by JAX's collectives and lax.ppermute only.
A program may use at most 320 MiB of HBM per device.

```python
import math
import jax
import jax.numpy as jnp
from jax import lax

F1 = 256
F2 = 256
F3 = 256
CH = 4
NFFT = 16777216
SEG = 8388608


def level_of(key, extent, cuts, low, high):
    gain, own = 1.0, jax.random.fold_in(key, 6)
    for dim, shards_of in cuts:
        steps = jnp.exp(jax.random.uniform(jax.random.fold_in(own, dim), (shards_of,), jnp.float32, low / len(cuts), high / len(cuts)))
        gain = gain * jnp.repeat(steps, extent[dim] // shards_of).reshape([-1 if axis == dim else 1 for axis in range(len(extent))])
    return gain


def bell_draw(own_key, extent, spread, reach, pieces=(), dtype=jnp.bfloat16):
    drawn = jax.random.normal(own_key, extent, jnp.float32) * spread
    if len(pieces) > 0:
        drawn = level_of(own_key, extent, pieces, -0.22, 0.18) * drawn
    return jnp.clip(drawn, min=-reach, max=reach).astype(dtype)


def setup_inputs(seed: int = 0) -> dict:
    key_list = jax.random.split(jax.random.key(seed), 5)
    return {
        "signal": bell_draw(key_list[0], (CH, SEG), 1.0, 6.0, ((1, 128),)),
        "gate": bell_draw(key_list[1], (CH, SEG), 1.0, 6.0, ((1, 128),)),
        "skip": jnp.clip(jnp.exp(jax.random.uniform(key_list[2], (CH,), jnp.float32, math.log(0.5), math.log(2.0))), 0.5, 2.0),
        "spectrum": bell_draw(key_list[3], (2, CH, F1, F2, F3), 1.0, 6.0, ((2, 128),), jnp.float32),
    }


def reference(signal, gate, skip, spectrum):
    def one_channel(items):
        row, filt_real, filt_imag = items
        padded = jnp.concatenate([row.astype(jnp.float32), jnp.zeros((SEG,), jnp.float32)])
        freq = jnp.fft.fft(padded)
        filt = lax.complex(filt_real, filt_imag)
        natural = jnp.transpose(filt, (2, 1, 0)).reshape(NFFT)
        return jnp.real(jnp.fft.ifft(freq * natural))[:SEG]

    conv = lax.map(one_channel, (signal, spectrum[0], spectrum[1]))
    mixed = gate.astype(jnp.float32) * (conv + skip[:, None] * signal.astype(jnp.float32))
    return mixed.astype(jnp.bfloat16)
```

```python
import jax
import jax.numpy as jnp
import ml_dtypes
import numpy as np
from jax import lax
from jax.experimental import pallas as pl
from jax.experimental.pallas import tpu as pltpu
from jax.sharding import PartitionSpec as P

F = 256
ND = 128
HALF = 32768
AXES = ("wide", "narrow")
bf16 = jnp.bfloat16
f32 = jnp.float32

OFFSET = 120.0 * np.log(2.0)
SPAN = 240.0
FIELD_CODE = (2.0**-8, 15.1)
FILTERED_CODE = (2.0**-11, 22.2)
CONV_CODE = (2.0**-7, 21.7)


def split_np(x):
    hi = x.astype(ml_dtypes.bfloat16)
    lo = (x - hi.astype(np.float64)).astype(ml_dtypes.bfloat16)
    return hi, lo


def outer_forward_table():
    k1 = np.arange(F).reshape(ND, 2)
    n = np.arange(ND)
    ang = 2 * np.pi * (k1[:, :, None] * n % F) / F
    t = np.zeros((ND, 2, 2, 2, 2, ND))
    for c in range(2):
        t[:, :, c, 0, c, :] = np.cos(ang)
        t[:, :, c, 1, c, :] = -np.sin(ang)
    return np.concatenate(split_np(t.reshape(ND * 8, 2 * ND)), axis=1)


def outer_inverse_table():
    k1 = np.arange(F).reshape(ND, 2)
    n = np.arange(ND)
    ang = 2 * np.pi * (n[:, None, None] * k1[None] % F) / F
    t = np.zeros((2, ND, ND, 2, 2, 2))
    for c in range(2):
        t[c, :, :, :, c, 0] = np.cos(ang)
        t[c, :, :, :, c, 1] = -np.sin(ang)
    return np.concatenate(split_np(t.reshape(2 * ND, ND * 8)), axis=1)


def inner_tables():
    i = np.arange(F)
    ang = 2 * np.pi * (i[:, None] * i[None] % F) / F
    c, s = np.cos(ang), np.sin(ang)
    fwd = np.block([[c, -s], [s, c]])
    inv = np.block([[c, s], [-s, c]]) / F
    return np.concatenate(split_np(fwd), axis=0), np.concatenate(split_np(inv), axis=0)


def base_tables():
    i = np.arange(F)
    a0 = 2 * np.pi * (i[:, None] * i[None] % F) / F
    a1 = 2 * np.pi * (i[:, None] * i[None]) / (F * F)
    return np.stack([np.cos(a0), np.sin(a0), np.cos(a1), np.sin(a1)]).astype(np.float32)


def peak_of(peak_ref):
    return jnp.maximum(jnp.max(peak_ref[...], keepdims=True), 1e-30)


def encode(x, peak, code):
    knee, octaves = code
    beta = SPAN / octaves
    z = jnp.abs(x) * (1.0 / (peak * knee))
    y = jnp.exp(jnp.minimum(beta * jnp.log(1.0 + z) - OFFSET, OFFSET))
    return jnp.where(x < 0, -y, y)


def decode(y, peak, code):
    knee, octaves = code
    beta = SPAN / octaves
    z = jnp.exp(jnp.log(jnp.abs(y)) * (1.0 / beta) + OFFSET / beta) - 1.0
    z = z * (peak * knee)
    return jnp.where(y < 0, -z, z)


def split(x):
    hi = x.astype(bf16)
    return hi, (x - hi.astype(f32)).astype(bf16)


def dot(a, b):
    return jnp.dot(a, b, preferred_element_type=f32)


def pack_kernel(sig_ref, out_ref, peak_ref, buf):
    peak_ref[...] = jnp.zeros((8, 128), f32)
    top = jnp.zeros((4, 128), f32)
    for q in range(ND):
        for i in range(4):
            x = sig_ref[:, pl.ds((i // 2) * HALF + q * F + (i % 2) * 128, 128)].astype(f32)
            top = jnp.maximum(top, jnp.abs(x))
            buf[pl.ds(q * 16 + i * 4, 4), :] = x
    peak_ref[pl.ds(0, 4), :] = top
    out_ref[...] = buf[...].reshape(ND, 16, 128).astype(bf16)


def outer_kernel(x_ref, table_ref, peak_ref, out0_ref, out1_ref, buf):
    peak = peak_of(peak_ref)
    buf[...] = x_ref[...].astype(f32).reshape(ND * 16, 128)
    for pair, out_ref in enumerate((out0_ref, out1_ref)):
        rows = []
        for c in range(2):
            parts = [buf[pl.ds(i * 4 + pair * 2 + c, ND, stride=16), :] for i in range(4)]
            rows.append(jnp.concatenate(parts, axis=1).astype(bf16))
        x = jnp.concatenate(rows, axis=0)
        for m in range(4):
            t = table_ref[pl.ds(m * 256, 256), :]
            res = dot(t[:, :256], x) + dot(t[:, 256:], x)
            res = encode(res, peak, FIELD_CODE)
            low = res[:, :F].reshape(32, 8, F)
            high = res[:, F:].reshape(32, 8, F)
            out_ref[pl.ds(m * 32, 32)] = jnp.concatenate([low, high], axis=1).astype(bf16)


def table_kernel(base_ref, lane_ref, sub_ref, mf_ref, mi_ref, cross_ref):
    c0, s0, c1, s1 = (base_ref[i] for i in range(4))
    for r in range(2):
        cb, sb = lane_ref[r, 0], lane_ref[r, 1]
        c, s = c0 * cb - s0 * sb, s0 * cb + c0 * sb
        (ch, cl), (sh, sl) = split(c), split(s)
        for part, (cc, ss) in enumerate(((ch, sh), (cl, sl))):
            lo = part * 512
            mf_ref[r, 0:256, lo : lo + 256] = cc
            mf_ref[r, 0:256, lo + 256 : lo + 512] = ss
            mf_ref[r, 256:512, lo : lo + 256] = -ss
            mf_ref[r, 256:512, lo + 256 : lo + 512] = cc
        cb, sb = sub_ref[r, 0], sub_ref[r, 1]
        c, s = (c0 * cb - s0 * sb) * (1.0 / F), (s0 * cb + c0 * sb) * (1.0 / F)
        (ch, cl), (sh, sl) = split(c), split(s)
        for part, (cc, ss) in enumerate(((ch, sh), (cl, sl))):
            lo = part * 512
            mi_ref[r, 0:256, lo : lo + 256] = cc
            mi_ref[r, 0:256, lo + 256 : lo + 512] = -ss
            mi_ref[r, 256:512, lo : lo + 256] = ss
            mi_ref[r, 256:512, lo + 256 : lo + 512] = cc
        cb, sb = lane_ref[r, 2], lane_ref[r, 3]
        cross_ref[r, 0] = c1 * cb - s1 * sb
        cross_ref[r, 1] = s1 * cb + c1 * sb


def middle_kernel(pair, y_ref, peak_ref, mf_ref, mi_ref, cross_ref, fwd_ref, inv_ref, filt_ref, out_ref, buf, obuf):
    peak = peak_of(peak_ref)
    for m in range(4):
        y = decode(y_ref[pl.ds(m * 32, 32)].astype(f32), peak, FIELD_CODE)
        y = y.reshape(512, F)
        for g in range(2):
            buf[g, pl.ds(m * 512, 512), :] = y[:, g * 128 : (g + 1) * 128]

    for r in range(2):
        cosine, sine = cross_ref[r, 0], cross_ref[r, 1]
        cols = []
        for c in range(2):
            cols.append(
                jnp.concatenate(
                    [
                        jnp.concatenate(
                            [buf[g, pl.ds(h * 8 + r * 4 + c * 2 + ri, ND, stride=16), :] for g in range(2)], axis=1
                        )
                        for ri in range(2)
                        for h in range(2)
                    ],
                    axis=0,
                )
            )
        hi, lo = split(jnp.concatenate(cols, axis=1))
        mf = mf_ref[r]
        z = dot(mf[:, :512], hi) + dot(mf[:, :512], lo) + dot(mf[:, 512:], hi)
        rows = []
        for c in range(2):
            zr, zi = z[:256, c * F : (c + 1) * F], z[256:, c * F : (c + 1) * F]
            rows.append(jnp.concatenate([zr * cosine + zi * sine, zi * cosine - zr * sine], axis=1))
        hi, lo = split(jnp.concatenate(rows, axis=0))
        fh, fl = fwd_ref[0:512, :], fwd_ref[512:1024, :]
        z = dot(hi, fh) + dot(lo, fh) + dot(hi, fl)
        rows = []
        for c in range(2):
            zr, zi = z[c * F : (c + 1) * F, :256], z[c * F : (c + 1) * F, 256:]
            fr, fi = filt_ref[0, c, r], filt_ref[1, c, r]
            rows.append(jnp.concatenate([zr * fr - zi * fi, zi * fr + zr * fi], axis=1))
        hi, lo = split(jnp.concatenate(rows, axis=0))
        fh, fl = inv_ref[0:512, :], inv_ref[512:1024, :]
        z = dot(hi, fh) + dot(lo, fh) + dot(hi, fl)
        cosine, sine = cosine * (1.0 / F), sine * (1.0 / F)
        cols = []
        for c in range(2):
            zr, zi = z[c * F : (c + 1) * F, :256], z[c * F : (c + 1) * F, 256:]
            cols.append(jnp.concatenate([zr * cosine - zi * sine, zi * cosine + zr * sine], axis=0))
        hi, lo = split(jnp.concatenate(cols, axis=1))
        mi = mi_ref[r]
        z = dot(mi[:, :512], hi) + dot(mi[:, :512], lo) + dot(mi[:, 512:], hi)
        for c in range(2):
            for ri in range(2):
                for h in range(2):
                    for g in range(2):
                        obuf[g, pl.ds(h * 8 + r * 4 + c * 2 + ri, ND, stride=16), :] = z[
                            ri * 256 + h * 128 : ri * 256 + (h + 1) * 128, c * F + g * 128 : c * F + (g + 1) * 128
                        ]
    for m in range(4):
        y = jnp.concatenate([obuf[g, pl.ds(m * 512, 512), :] for g in range(2)], axis=1)
        y = encode(y, peak, FILTERED_CODE)
        out_ref[pl.ds(m * 32, 32)] = y.reshape(32, 16, F).astype(bf16)


def last_kernel(y_ref, table_ref, peak_ref, out_ref, buf):
    peak = peak_of(peak_ref)
    for h in range(2):
        acc = jnp.zeros((256, F), f32)
        for m in range(4):
            y = y_ref[pl.ds(m * 32, 32)].astype(f32)[:, h * 8 : (h + 1) * 8, :]
            hi, lo = split(decode(y.reshape(256, F), peak, FILTERED_CODE))
            th = table_ref[:, m * 256 : (m + 1) * 256]
            tl = table_ref[:, 1024 + m * 256 : 1024 + (m + 1) * 256]
            acc = acc + dot(th, hi) + dot(th, lo) + dot(tl, hi)
        for c in range(2):
            for b in range(2):
                buf[pl.ds(h * 4 + b * 2 + c, ND, stride=8), :] = acc[
                    c * ND : (c + 1) * ND, b * 128 : (b + 1) * 128
                ]
    out_ref[...] = encode(buf[...], peak, CONV_CODE).reshape(ND, 8, 128).astype(bf16)


def finish_kernel(y0_ref, y1_ref, sig_ref, gate_ref, skip_ref, peak_ref, out_ref, buf0, buf1, conv):
    peak = peak_of(peak_ref)
    for y_ref, buf in ((y0_ref, buf0), (y1_ref, buf1)):
        buf[...] = decode(y_ref[...].astype(f32).reshape(ND * 8, 128), peak, CONV_CODE)
    for q in range(ND):
        for i in range(4):
            at = pl.ds((i // 2) * HALF + q * F + (i % 2) * 128, 128)
            conv[pl.ds(0, 2), at] = buf0[pl.ds(q * 8 + i * 2, 2), :]
            conv[pl.ds(2, 2), at] = buf1[pl.ds(q * 8 + i * 2, 2), :]
    skip = skip_ref[...]
    for i in range(16):
        at = pl.ds(i * 4096, 4096)
        total = conv[:, at] + skip * sig_ref[:, at].astype(f32)
        out_ref[:, at] = (gate_ref[:, at].astype(f32) * total).astype(bf16)


VMEM = pl.BlockSpec(memory_space=pltpu.VMEM)


def call(kernel, ins, outs, scratch, name, flops=0, limit=48):
    size = sum(int(np.prod(x.shape)) * x.dtype.itemsize for x in (*ins, *outs))
    return pl.pallas_call(
        kernel,
        in_specs=[VMEM] * len(ins),
        out_specs=[VMEM] * len(outs),
        out_shape=outs,
        scratch_shapes=[pltpu.VMEM(s, f32) for s in scratch],
        compiler_params=pltpu.CompilerParams(vmem_limit_bytes=limit * 2**20),
        cost_estimate=pl.CostEstimate(flops=flops, bytes_accessed=size, transcendentals=0),
        name=name,
    )(*ins)


def exchange(x):
    return lax.all_to_all(x, AXES, split_axis=0, concat_axis=0, tiled=True)


def shape(*dims, dtype=bf16):
    return jax.ShapeDtypeStruct(dims, dtype)


def per_device(signal, gate, skip, spectrum):
    place = lax.axis_index("wide") * lax.axis_size("narrow") + lax.axis_index("narrow")
    packed, peak = call(
        pack_kernel, (signal,), [shape(ND, 16, 128), shape(8, 128, dtype=f32)], [(ND * 16, 128)], "pack"
    )
    spread = exchange(packed)
    peak = lax.pmax(peak, AXES)

    k1 = (place * 2 + jnp.arange(2, dtype=jnp.int32))[:, None] * jnp.arange(F, dtype=jnp.int32)
    mid = (2 * np.pi / (F * F)) * (k1 % (F * F)).astype(f32)
    fine = (2 * np.pi / (F * F * F)) * k1.astype(f32)
    lane = jnp.stack([jnp.cos(mid), jnp.sin(mid), jnp.cos(fine), jnp.sin(fine)], axis=1)
    mf, mi, cross = call(
        table_kernel,
        (jnp.asarray(base_tables()), lane[:, :, None, :], lane[:, :2, :, None]),
        [shape(2, 512, 1024), shape(2, 512, 1024), shape(2, 2, F, F, dtype=f32)],
        [],
        "tables",
    )
    inner_fwd, inner_inv = (jnp.asarray(t) for t in inner_tables())

    field = call(
        outer_kernel,
        (spread, jnp.asarray(outer_forward_table()), peak),
        [shape(ND, 16, F)] * 2,
        [(ND * 16, 128)],
        "outer",
        flops=2**30,
    )
    field = [exchange(y) for y in field]
    table = jnp.asarray(outer_inverse_table())
    conv = []
    for pair in range(2):
        (filtered,) = call(
            lambda *refs, pair=pair: middle_kernel(pair, *refs),
            (field[pair], peak, mf, mi, cross, inner_fwd, inner_inv, spectrum[:, 2 * pair : 2 * pair + 2]),
            [shape(ND, 16, F)],
            [(2, ND * 16, 128)] * 2,
            "middle",
            flops=6 * 2**30,
        )
        filtered = exchange(filtered)
        (part,) = call(last_kernel, (filtered, table, peak), [shape(ND, 8, 128)], [(ND * 8, 128)], "last", flops=2**29)
        conv.append(exchange(part))
    (mixed,) = call(
        finish_kernel,
        (*conv, signal, gate, skip[:, None], peak),
        [shape(4, 65536)],
        [(ND * 8, 128), (ND * 8, 128), (4, 65536)],
        "finish",
    )
    return mixed


def solution(mesh):
    split_spec = P(None, AXES)
    return jax.shard_map(
        per_device,
        mesh=mesh,
        in_specs=(split_spec, split_spec, P(), P(None, None, AXES, None, None)),
        out_specs=split_spec,
        check_vma=False,
    )
```

```python
import jax
import jax.numpy as jnp
import ml_dtypes
import numpy as np
from jax import lax
from jax.experimental import pallas as pl
from jax.experimental.pallas import tpu as pltpu
from jax.sharding import PartitionSpec as P

F = 256
ND = 128
STEPS = 4
ROWS = ND // STEPS
AXES = ("wide", "narrow")
bf16 = jnp.bfloat16
f32 = jnp.float32

OFFSET = 120.0 * np.log(2.0)
SPAN = 240.0
FIELD_CODE = (2.0**-8, 15.1)
FILTERED_CODE = (2.0**-11, 22.2)
CONV_CODE = (2.0**-7, 21.7)


def split_np(x):
    hi = x.astype(ml_dtypes.bfloat16)
    lo = (x - hi.astype(np.float64)).astype(ml_dtypes.bfloat16)
    return hi, lo


def outer_forward_table():
    k1 = np.arange(F).reshape(ND, 2)
    n = np.arange(ND)
    ang = 2 * np.pi * (k1[:, :, None] * n % F) / F
    t = np.zeros((ND, 2, 2, 2, 2, ND))
    for c in range(2):
        t[:, :, c, 0, c, :] = np.cos(ang)
        t[:, :, c, 1, c, :] = -np.sin(ang)
    return np.concatenate(split_np(t.reshape(ND * 8, 2 * ND)), axis=1)


def outer_inverse_table():
    k1 = np.arange(F).reshape(ND, 2)
    n = np.arange(ND)
    ang = 2 * np.pi * (n[:, None, None] * k1[None] % F) / F
    t = np.zeros((2, ND, ND, 2, 2, 2))
    for c in range(2):
        t[c, :, :, :, c, 0] = np.cos(ang)
        t[c, :, :, :, c, 1] = -np.sin(ang)
    hi, lo = (x.reshape(2 * ND, STEPS, -1) for x in split_np(t.reshape(2 * ND, ND * 8)))
    return np.ascontiguousarray(np.concatenate([hi, hi, lo], axis=2).transpose(1, 0, 2))


def inner_tables():
    i = np.arange(F)
    ang = 2 * np.pi * (i[:, None] * i[None] % F) / F
    c, s = np.cos(ang), np.sin(ang)
    fwd = split_np(np.block([[c, -s], [s, c]]))
    inv = split_np(np.block([[c, s], [-s, c]]) / F)
    return tuple(np.concatenate([hi, hi, lo], axis=0) for hi, lo in (fwd, inv))


def base_tables():
    i = np.arange(F)
    half = np.arange(ND)
    a0 = 2 * np.pi * (half[:, None] * half[None] % ND) / ND
    a1 = 2 * np.pi * (i[:, None] * i[None]) / (F * F)
    return (
        np.stack([np.cos(a0), np.sin(a0)]).astype(np.float32),
        np.stack([np.cos(a1), np.sin(a1)]).astype(np.float32),
    )


def peak_of(peak_ref):
    return jnp.maximum(jnp.max(peak_ref[...], keepdims=True), 1e-30)


def encode(x, peak, code):
    knee, octaves = code
    beta = SPAN / octaves
    z = jnp.abs(x) * (1.0 / (peak * knee))
    y = jnp.exp(jnp.minimum(beta * jnp.log(1.0 + z) - OFFSET, OFFSET))
    return jnp.where(x < 0, -y, y)


def decode(y, peak, code):
    knee, octaves = code
    beta = SPAN / octaves
    z = jnp.exp(jnp.log(jnp.abs(y)) * (1.0 / beta) + OFFSET / beta) - 1.0
    z = z * (peak * knee)
    return jnp.where(y < 0, -z, z)


def split(x):
    hi = x.astype(bf16)
    return hi, (x - hi.astype(f32)).astype(bf16)


def dot(a, b):
    return jnp.dot(a, b, preferred_element_type=f32)


def twice(hi, lo, axis):
    return jnp.concatenate([hi, lo, hi], axis=axis)


def pack_kernel(sig_ref, out_ref):
    top = jnp.zeros((4, 128), f32)
    for q in range(ND):
        x = sig_ref[:, pl.ds(q * 512, 512)]
        out_ref[q, :, pl.ds(0, 512)] = x
        x = jnp.abs(x.astype(f32))
        for i in range(4):
            top = jnp.maximum(top, x[:, i * 128 : (i + 1) * 128])
    top = top.astype(bf16)
    for q in range(ND):
        out_ref[q, :, pl.ds(512, 128)] = top


def outer_kernel(x_ref, table_ref, out_ref, peak_ref, buf, xs):
    @pl.when(pl.program_id(0) == 0)
    def _():
        top = jnp.zeros((4, 128), f32)
        for n in range(ND):
            x = x_ref[n].astype(f32)
            top = jnp.maximum(top, x[:, 512:640])
            for i in range(4):
                buf[i, pl.ds(n * 8, 4), :] = x[:, i * 128 : (i + 1) * 128]
        peak_ref[...] = jnp.broadcast_to(jnp.maximum(jnp.max(top, keepdims=True), 1e-30), (8, 128))
        for c in range(4):
            parts = [buf[i, pl.ds(c, ND, stride=8), :] for i in range(4)]
            xs[pl.ds(c * ND, ND), :] = jnp.concatenate(parts, axis=1).astype(bf16)

    peak = peak_ref[0:1, 0:1]
    t = table_ref[...]
    outs = []
    for pair in range(2):
        x = xs[pl.ds(pair * 256, 256), :]
        res = encode(dot(t, jnp.concatenate([x, x], axis=0)), peak, FIELD_CODE)
        outs.append(res[:, :F].reshape(ROWS, 8, F))
        outs.append(res[:, F:].reshape(ROWS, 8, F))
    out_ref[...] = jnp.concatenate(outs, axis=1).astype(bf16)


def table_kernel(base_ref, cross_base_ref, lane_ref, cross_lane_ref, sub_ref, mf_ref, mi_ref, cross_ref):
    c0, s0 = base_ref[0], base_ref[1]
    c1, s1 = cross_base_ref[0], cross_base_ref[1]
    for r in range(2):
        for out_ref, vec_ref, sign in ((mf_ref, lane_ref, 1.0), (mi_ref, sub_ref, -1.0)):
            cb, sb = vec_ref[r, 0], vec_ref[r, 1]
            c, s = c0 * cb - s0 * sb, (s0 * cb + c0 * sb) * sign
            if sign < 0:
                c, s = c * (1.0 / F), s * (1.0 / F)
            (ch, cl), (sh, sl) = split(c), split(s)
            for part, (cc, ss) in enumerate(((ch, sh), (ch, sh), (cl, sl))):
                at = part * 256
                out_ref[r, 0:128, at : at + 128] = cc
                out_ref[r, 0:128, at + 128 : at + 256] = ss
                out_ref[r, 128:256, at : at + 128] = -ss
                out_ref[r, 128:256, at + 128 : at + 256] = cc
        cb, sb = cross_lane_ref[r, 0], cross_lane_ref[r, 1]
        cross_ref[r, 0] = c1 * cb - s1 * sb
        cross_ref[r, 1] = s1 * cb + c1 * sb


def middle_kernel(y_ref, peak_ref, mf_ref, mi_ref, cross_ref, turn_ref, fwd_ref, inv_ref, filt_ref, out_ref, buf, obuf):
    peak = peak_ref[0:1, 0:1]
    for m in range(STEPS):
        y = decode(y_ref[pl.ds(m * ROWS, ROWS)].astype(f32), peak, FIELD_CODE).reshape(ROWS * 16, F)
        for g in range(2):
            buf[g, pl.ds(m * ROWS * 16, ROWS * 16), :] = y[:, g * 128 : (g + 1) * 128]

    for r in range(2):
        tc, ts = turn_ref[r, 0], turn_ref[r, 1]
        parts = []
        for ri in range(2):
            parts.append(
                jnp.concatenate(
                    [
                        buf[g, pl.ds(h * 8 + r * 4 + c * 2 + ri, ND, stride=16), :]
                        for c in range(2)
                        for h in range(2)
                        for g in range(2)
                    ],
                    axis=1,
                )
            )
        hi, lo = split(jnp.concatenate(parts, axis=0))
        z = dot(mf_ref[r], twice(hi, lo, 0))
        rows = []
        for c in range(2):
            at = c * 512
            dr, di = z[:128, at : at + 256], z[128:, at : at + 256]
            er, ei = z[:128, at + 256 : at + 512], z[128:, at + 256 : at + 512]
            pr, pi = er * tc + ei * ts, ei * tc - er * ts
            for zr, zi, e in ((dr + pr, di + pi, 0), (dr - pr, di - pi, 128)):
                cosine, sine = cross_ref[r, 0, e : e + 128], cross_ref[r, 1, e : e + 128]
                rows.append(jnp.concatenate([zr * cosine + zi * sine, zi * cosine - zr * sine], axis=1))
        hi, lo = split(jnp.concatenate(rows, axis=0))
        z = dot(twice(hi, lo, 1), fwd_ref[...])
        rows = []
        for c in range(2):
            zr, zi = z[c * F : (c + 1) * F, :256], z[c * F : (c + 1) * F, 256:]
            fr, fi = filt_ref[0, c, r], filt_ref[1, c, r]
            rows.append(jnp.concatenate([zr * fr - zi * fi, zi * fr + zr * fi], axis=1))
        hi, lo = split(jnp.concatenate(rows, axis=0))
        z = dot(twice(hi, lo, 1), inv_ref[...])
        tops, bottoms = [], []
        for c in range(2):
            both = []
            for e in (0, 128):
                at = c * F + e
                zr, zi = z[at : at + 128, :256], z[at : at + 128, 256:]
                cosine = cross_ref[r, 0, e : e + 128] * (1.0 / F)
                sine = cross_ref[r, 1, e : e + 128] * (1.0 / F)
                both.append((zr * cosine - zi * sine, zi * cosine + zr * sine))
            (ar, ai), (br, bi) = both
            ur, ui = ar - br, ai - bi
            tops += [ar + br, ur * tc - ui * ts]
            bottoms += [ai + bi, ui * tc + ur * ts]
        hi, lo = split(jnp.concatenate([jnp.concatenate(tops, axis=1), jnp.concatenate(bottoms, axis=1)], axis=0))
        z = dot(mi_ref[r], twice(hi, lo, 0))
        for c in range(2):
            for ri in range(2):
                for h in range(2):
                    for g in range(2):
                        at = c * 512 + h * 256 + g * 128
                        obuf[g, pl.ds(h * 8 + r * 4 + c * 2 + ri, ND, stride=16), :] = z[
                            ri * 128 : (ri + 1) * 128, at : at + 128
                        ]
    for m in range(STEPS):
        y = jnp.concatenate([obuf[g, pl.ds(m * ROWS * 16, ROWS * 16), :] for g in range(2)], axis=1)
        out_ref[pl.ds(m * ROWS, ROWS)] = encode(y, peak, FILTERED_CODE).reshape(ROWS, 16, F).astype(bf16)


def last_kernel(y_ref, table_ref, peak_ref, out_ref, acc, buf):
    peak = peak_ref[0:1, 0:1]
    step = pl.program_id(0)

    @pl.when(step == 0)
    def _():
        acc[...] = jnp.zeros(acc.shape, f32)

    y = decode(y_ref[...].astype(f32), peak, FILTERED_CODE)
    t = table_ref[0]
    for pair in range(2):
        for h in range(2):
            at = pair * 16 + h * 8
            hi, lo = split(y[:, at : at + 8, :].reshape(ROWS * 8, F))
            acc[pair, h] += dot(t, twice(hi, lo, 0))

    @pl.when(step == STEPS - 1)
    def _():
        for pair in range(2):
            for h in range(2):
                for c in range(2):
                    for g in range(2):
                        buf[pl.ds(h * 8 + g * 4 + pair * 2 + c, ND, stride=16), :] = acc[
                            pair, h, c * ND : (c + 1) * ND, g * 128 : (g + 1) * 128
                        ]
        out_ref[...] = encode(buf[...], peak, CONV_CODE).reshape(ND, 16, 128).astype(bf16)


def finish_kernel(y_ref, sig_ref, gate_ref, skip_ref, peak_ref, out_ref, buf):
    peak = peak_ref[0:1, 0:1]
    buf[...] = decode(y_ref[...].astype(f32).reshape(ND * 16, 128), peak, CONV_CODE)
    skip = skip_ref[...]
    for q in range(ND):
        at = pl.ds(q * 512, 512)
        conv = jnp.concatenate([buf[pl.ds(q * 16 + i * 4, 4), :] for i in range(4)], axis=1)
        total = conv + skip * sig_ref[:, at].astype(f32)
        out_ref[:, at] = (gate_ref[:, at].astype(f32) * total).astype(bf16)


VMEM = pl.BlockSpec(memory_space=pltpu.VMEM)


def call(kernel, ins, outs, scratch, name, flops=0, limit=48, grid=(), in_specs=None, out_specs=None):
    size = sum(int(np.prod(x.shape)) * x.dtype.itemsize for x in (*ins, *outs))
    return pl.pallas_call(
        kernel,
        grid=grid,
        in_specs=in_specs or [VMEM] * len(ins),
        out_specs=out_specs or [VMEM] * len(outs),
        out_shape=outs,
        scratch_shapes=[pltpu.VMEM(s, d) for s, d in scratch],
        compiler_params=pltpu.CompilerParams(vmem_limit_bytes=limit * 2**20),
        cost_estimate=pl.CostEstimate(flops=flops, bytes_accessed=size, transcendentals=0),
        name=name,
    )(*ins)


def exchange(x):
    return lax.all_to_all(x, AXES, split_axis=0, concat_axis=0, tiled=True)


def shape(*dims, dtype=bf16):
    return jax.ShapeDtypeStruct(dims, dtype)


def per_device(signal, gate, skip, spectrum):
    place = lax.axis_index("wide") * lax.axis_size("narrow") + lax.axis_index("narrow")
    (packed,) = call(pack_kernel, (signal,), [shape(ND, 4, 640)], [], "pack")
    spread = exchange(packed)

    k1 = place * 2 + jnp.arange(2, dtype=jnp.int32)[:, None]
    half = jnp.arange(ND, dtype=jnp.int32)

    def wave(index, period):
        angle = (2 * np.pi / period) * (index % period).astype(f32)
        return jnp.stack([jnp.cos(angle), jnp.sin(angle)], axis=1)

    mid = wave(k1 * half, F * ND)
    fine = wave(k1 * jnp.arange(F, dtype=jnp.int32), F**3)
    turn = wave(k1 + F * half, F * F)
    base, cross_base = (jnp.asarray(t) for t in base_tables())
    mf, mi, cross = call(
        table_kernel,
        (base, cross_base, mid[:, :, None, :], fine[:, :, None, :], mid[:, :, :, None]),
        [shape(2, 256, 768), shape(2, 256, 768), shape(2, 2, F, F, dtype=f32)],
        [],
        "tables",
    )
    inner_fwd, inner_inv = (jnp.asarray(t) for t in inner_tables())

    field, peak = call(
        outer_kernel,
        (spread, jnp.asarray(outer_forward_table())),
        [shape(ND, 32, F), shape(8, 128, dtype=f32)],
        [((4, ND * 8, 128), f32), ((ND * 4, 512), bf16)],
        "outer",
        flops=2**30,
        grid=(STEPS,),
        in_specs=[VMEM, pl.BlockSpec((ROWS * 8, 512), lambda i: (i, 0))],
        out_specs=[pl.BlockSpec((ROWS, 32, F), lambda i: (i, 0, 0)), pl.BlockSpec((8, 128), lambda i: (0, 0))],
    )
    field = exchange(field)
    pair_spec = pl.BlockSpec((ND, 16, F), lambda i: (0, i, 0))
    (filtered,) = call(
        middle_kernel,
        (field, peak, mf, mi, cross, turn[:, :, :, None], inner_fwd, inner_inv, spectrum),
        [shape(ND, 32, F)],
        [((2, ND * 16, 128), f32)] * 2,
        "middle",
        flops=9 * 2**30,
        grid=(2,),
        in_specs=[pair_spec] + [VMEM] * 7 + [pl.BlockSpec((2, 2, 2, F, F), lambda i: (0, i, 0, 0, 0))],
        out_specs=[pair_spec],
    )
    filtered = exchange(filtered)
    (conv,) = call(
        last_kernel,
        (filtered, jnp.asarray(outer_inverse_table()), peak),
        [shape(ND, 16, 128)],
        [((2, 2, 2 * ND, F), f32), ((ND * 16, 128), f32)],
        "last",
        flops=2**30,
        grid=(STEPS,),
        in_specs=[
            pl.BlockSpec((ROWS, 32, F), lambda i: (i, 0, 0)),
            pl.BlockSpec((1, 2 * ND, ROWS * 24), lambda i: (i, 0, 0)),
            VMEM,
        ],
        out_specs=[VMEM],
    )
    conv = exchange(conv)
    (mixed,) = call(
        finish_kernel,
        (conv, signal, gate, skip[:, None], peak),
        [shape(4, 65536)],
        [((ND * 16, 128), f32)],
        "finish",
    )
    return mixed


def solution(mesh):
    split_spec = P(None, AXES)
    return jax.shard_map(
        per_device,
        mesh=mesh,
        in_specs=(split_spec, split_spec, P(), P(None, None, AXES, None, None)),
        out_specs=split_spec,
        check_vma=False,
    )
```

```python
import jax
import jax.numpy as jnp
import ml_dtypes
import numpy as np
from jax import lax
from jax.experimental import pallas as pl
from jax.experimental.pallas import tpu as pltpu
from jax.sharding import PartitionSpec as P

F = 256
ND = 128
STEPS = 4
ROWS = ND // STEPS
AXES = ("wide", "narrow")
bf16 = jnp.bfloat16
f32 = jnp.float32

OFFSET = 120.0 * np.log(2.0)
SPAN = 240.0
FIELD_CODE = (2.0**-8, 15.1)
FILTERED_CODE = (2.0**-11, 22.2)
CONV_CODE = (2.0**-7, 21.7)
FILTER_TOP = 6.02


def split_np(x):
    hi = x.astype(ml_dtypes.bfloat16)
    lo = (x - hi.astype(np.float64)).astype(ml_dtypes.bfloat16)
    return hi, lo


def outer_waves():
    k1 = np.arange(F).reshape(ND, 2)
    ang = 2 * np.pi * (k1[:, :, None] * np.arange(ND) % F) / F
    wave = np.stack([np.cos(ang), -np.sin(ang)], axis=2)
    for p in (0, ND // 2):
        wave[p, 0, 1] = np.cos(np.pi * (1 - p // (ND // 2)) * np.arange(ND))
    return wave


def outer_forward_table():
    t = np.zeros((ND, 2, 2, 2, 2, ND))
    for c in range(2):
        t[:, :, c, :, c, :] = outer_waves()
    return np.concatenate(split_np(t.reshape(ND * 8, 2 * ND)), axis=1)


def outer_inverse_table():
    t = np.zeros((2, ND, ND, 2, 2, 2))
    for c in range(2):
        t[c, :, :, :, c, :] = outer_waves().transpose(3, 0, 1, 2)
    hi, lo = (x.reshape(2 * ND, STEPS, -1) for x in split_np(t.reshape(2 * ND, ND * 8)))
    return np.ascontiguousarray(np.concatenate([hi, hi, lo], axis=2).transpose(1, 0, 2))


def inner_tables():
    low = np.arange(ND)
    out = []
    for odd in range(2):
        ang = 2 * np.pi * (low[:, None] * (2 * low[None] + odd) % F) / F
        c, s = np.cos(ang), np.sin(ang)
        fwd = split_np(np.block([[c, -s], [s, c]]))
        inv = split_np(np.block([[c.T, s.T], [-s.T, c.T]]) / F)
        out.append([np.concatenate([hi, hi, lo], axis=0) for hi, lo in (fwd, inv)])
    return np.stack([out[0][0], out[1][0]]), np.stack([out[0][1], out[1][1]])


def order_tables():
    eye = np.eye(F)
    even_odd = np.concatenate([np.arange(0, F, 2), np.arange(1, F, 2)])
    plain = np.stack([eye, eye[:, even_odd]])
    back = np.stack([eye[::-1], eye[:, 255 - even_odd]])
    return plain.astype(ml_dtypes.bfloat16), back.astype(ml_dtypes.bfloat16)


def base_tables():
    i = np.arange(F)
    half = np.arange(ND)
    a0 = 2 * np.pi * (half[:, None] * half[None] % ND) / ND
    a1 = 2 * np.pi * (i[:, None] * i[None]) / (F * F)
    return (
        np.stack([np.cos(a0), np.sin(a0)]).astype(np.float32),
        np.stack([np.cos(a1), np.sin(a1)]).astype(np.float32),
    )


def peak_of(peak_ref):
    return jnp.maximum(jnp.max(peak_ref[...], keepdims=True), 1e-30)


def encode(x, peak, code):
    knee, octaves = code
    beta = SPAN / octaves
    z = jnp.abs(x) * (1.0 / (peak * knee))
    y = jnp.exp(jnp.minimum(beta * jnp.log(1.0 + z) - OFFSET, OFFSET))
    return jnp.where(x < 0, -y, y)


def decode(y, peak, code):
    knee, octaves = code
    beta = SPAN / octaves
    z = jnp.exp(jnp.log(jnp.abs(y)) * (1.0 / beta) + OFFSET / beta) - 1.0
    z = z * (peak * knee)
    return jnp.where(y < 0, -z, z)


def encode_filter(x):
    y = jnp.exp(jnp.abs(x) * (SPAN * np.log(2.0) / FILTER_TOP) - OFFSET)
    return jnp.where(x < 0, -y, y)


def decode_filter(y):
    z = (jnp.log(jnp.abs(y)) + OFFSET) * (FILTER_TOP / (SPAN * np.log(2.0)))
    return jnp.where(y < 0, -z, z)


def split(x):
    hi = x.astype(bf16)
    return hi, (x - hi.astype(f32)).astype(bf16)


def dot(a, b):
    return jnp.dot(a, b, preferred_element_type=f32)


def twice(hi, lo, axis):
    return jnp.concatenate([hi, lo, hi], axis=axis)


def pack_kernel(sig_ref, out_ref):
    top = jnp.zeros((4, 128), f32)
    for q in range(ND):
        x = sig_ref[:, pl.ds(q * 512, 512)]
        out_ref[q, :, pl.ds(0, 512)] = x
        x = jnp.abs(x.astype(f32))
        for i in range(4):
            top = jnp.maximum(top, x[:, i * 128 : (i + 1) * 128])
    top = top.astype(bf16)
    for q in range(ND):
        out_ref[q, :, pl.ds(512, 128)] = top


def outer_kernel(x_ref, table_ref, out_ref, peak_ref, buf, xs):
    @pl.when(pl.program_id(0) == 0)
    def _():
        top = jnp.zeros((4, 128), f32)
        for n in range(ND):
            x = x_ref[n].astype(f32)
            top = jnp.maximum(top, x[:, 512:640])
            for i in range(4):
                buf[i, pl.ds(n * 8, 4), :] = x[:, i * 128 : (i + 1) * 128]
        peak_ref[...] = jnp.broadcast_to(jnp.maximum(jnp.max(top, keepdims=True), 1e-30), (8, 128))
        for c in range(4):
            parts = [buf[i, pl.ds(c, ND, stride=8), :] for i in range(4)]
            xs[pl.ds(c * ND, ND), :] = jnp.concatenate(parts, axis=1).astype(bf16)

    x = xs[pl.ds(pl.program_id(0) // (STEPS // 2) * 256, 256), :]
    res = encode(dot(table_ref[...], jnp.concatenate([x, x], axis=0)), peak_ref[0:1, 0:1], FIELD_CODE)
    parts = [res[:, h * F : (h + 1) * F].reshape(ROWS, 8, F) for h in range(2)]
    out_ref[...] = jnp.concatenate(parts, axis=1).astype(bf16)


def table_kernel(base_ref, cross_base_ref, lane_ref, cross_lane_ref, sub_ref, mf_ref, mi_ref, cross_ref):
    c0, s0 = base_ref[0], base_ref[1]
    c1, s1 = cross_base_ref[0], cross_base_ref[1]
    for r in range(3):
        for out_ref, vec_ref, sign in ((mf_ref, lane_ref, 1.0), (mi_ref, sub_ref, -1.0)):
            cb, sb = vec_ref[r, 0], vec_ref[r, 1]
            c, s = c0 * cb - s0 * sb, (s0 * cb + c0 * sb) * sign
            if sign < 0:
                c, s = c * (1.0 / F), s * (1.0 / F)
            (ch, cl), (sh, sl) = split(c), split(s)
            for part, (cc, ss) in enumerate(((ch, sh), (ch, sh), (cl, sl))):
                at = part * 256
                out_ref[r, 0:128, at : at + 128] = cc
                out_ref[r, 0:128, at + 128 : at + 256] = ss
                out_ref[r, 128:256, at : at + 128] = -ss
                out_ref[r, 128:256, at + 128 : at + 256] = cc
        cb, sb = cross_lane_ref[r, 0], cross_lane_ref[r, 1]
        cross_ref[r, 0] = c1 * cb - s1 * sb
        cross_ref[r, 1] = s1 * cb + c1 * sb


def give_kernel(half_ref, filt_ref, order_ref, sign_ref, out0_ref, out1_ref):
    del half_ref
    for r, out_ref in enumerate((out0_ref, out1_ref)):
        left, right = order_ref[r, 0], order_ref[r, 1]
        for ri in range(2):
            for c in range(2):
                hi, lo = split(filt_ref[ri, c, r])
                hi, lo = split(dot(hi, right) + dot(lo, right))
                x = dot(left, hi) + dot(left, lo)
                if ri:
                    x = x * sign_ref[r]
                out_ref[ri * 2 + c] = encode_filter(x).astype(bf16)


def combine_kernel(half_ref, filt_ref, order_ref, got0_ref, got1_ref, generic_ref, out_ref, other_ref):
    del half_ref
    for r, got_ref in enumerate((got0_ref, got1_ref)):
        for ri in range(2):
            for c in range(2):
                got = decode_filter(got_ref[ri * 2 + c].astype(f32))
                if r == 0:
                    other_ref[ri, c] = got
                    got = got * generic_ref[0]
                hi, lo = split(filt_ref[ri, c, r])
                out_ref[r, ri, c] = dot(hi, order_ref[1]) + dot(lo, order_ref[1]) + got


def transform(re, im, table, mf_ref, mi_ref, cross_ref, turn_ref, fwd_ref, inv_ref, filt):
    tc, ts = turn_ref[table, 0], turn_ref[table, 1]
    hi, lo = split(jnp.concatenate([re, im], axis=0))
    z = dot(mf_ref[table], twice(hi, lo, 0))
    sums, diffs = [], []
    for c in range(2):
        at = c * 512
        dr, di = z[:128, at : at + 256], z[128:, at : at + 256]
        er, ei = z[:128, at + 256 : at + 512], z[128:, at + 256 : at + 512]
        pr, pi = er * tc + ei * ts, ei * tc - er * ts
        for zr, zi, e in ((dr + pr, di + pi, 0), (dr - pr, di - pi, 128)):
            cosine, sine = cross_ref[table, 0, e : e + 128], cross_ref[table, 1, e : e + 128]
            zr, zi = zr * cosine + zi * sine, zi * cosine - zr * sine
            sums.append(jnp.concatenate([zr[:, :128] + zr[:, 128:], zi[:, :128] + zi[:, 128:]], axis=1))
            diffs.append(jnp.concatenate([zr[:, :128] - zr[:, 128:], zi[:, :128] - zi[:, 128:]], axis=1))
    back = []
    for odd, rows in enumerate((sums, diffs)):
        hi, lo = split(jnp.concatenate(rows, axis=0))
        z = dot(twice(hi, lo, 1), fwd_ref[odd])
        rows = []
        for c in range(2):
            zr, zi = z[c * F : (c + 1) * F, :128], z[c * F : (c + 1) * F, 128:]
            fr, fi = filt(0, c, odd), filt(1, c, odd)
            rows.append(jnp.concatenate([zr * fr - zi * fi, zi * fr + zr * fi], axis=1))
        hi, lo = split(jnp.concatenate(rows, axis=0))
        back.append(dot(twice(hi, lo, 1), inv_ref[odd]))
    even, odd = back
    tops, bottoms = [], []
    for c in range(2):
        both = []
        for e in (0, 128):
            at = c * F + e
            er, ei = even[at : at + 128, :128], even[at : at + 128, 128:]
            dr, di = odd[at : at + 128, :128], odd[at : at + 128, 128:]
            zr = jnp.concatenate([er + dr, er - dr], axis=1)
            zi = jnp.concatenate([ei + di, ei - di], axis=1)
            cosine = cross_ref[table, 0, e : e + 128] * (1.0 / F)
            sine = cross_ref[table, 1, e : e + 128] * (1.0 / F)
            both.append((zr * cosine - zi * sine, zi * cosine + zr * sine))
        (ar, ai), (br, bi) = both
        ur, ui = ar - br, ai - bi
        tops += [ar + br, ur * tc - ui * ts]
        bottoms += [ai + bi, ui * tc + ur * ts]
    hi, lo = split(jnp.concatenate([jnp.concatenate(tops, axis=1), jnp.concatenate(bottoms, axis=1)], axis=0))
    return dot(mi_ref[table], twice(hi, lo, 0))


def middle_kernel(
    y_ref, peak_ref, mf_ref, mi_ref, cross_ref, turn_ref, fwd_ref, inv_ref, filt_ref, other_ref, generic_ref, out_ref, buf, obuf
):
    peak = peak_ref[0:1, 0:1]
    tables = (mf_ref, mi_ref, cross_ref, turn_ref, fwd_ref, inv_ref)
    for m in range(STEPS):
        y = decode(y_ref[pl.ds(m * ROWS, ROWS)].astype(f32), peak, FIELD_CODE).reshape(ROWS * 16, F)
        for g in range(2):
            buf[g, pl.ds(m * ROWS * 16, ROWS * 16), :] = y[:, g * 128 : (g + 1) * 128]

    def field(r, ri):
        return jnp.concatenate(
            [
                buf[g, pl.ds(h * 8 + r * 4 + c * 2 + ri, ND, stride=16), :]
                for c in range(2)
                for h in range(2)
                for g in range(2)
            ],
            axis=1,
        )

    def put(z, r, ri, part):
        for c in range(2):
            for h in range(2):
                for g in range(2):
                    at = c * 512 + h * 256 + g * 128
                    obuf[g, pl.ds(h * 8 + r * 4 + c * 2 + ri, ND, stride=16), :] = z[
                        part * 128 : (part + 1) * 128, at : at + 128
                    ]

    def filt_of(r):
        return lambda ri, c, odd: filt_ref[r, ri, c, :, odd * 128 : (odd + 1) * 128]

    for r in range(2):
        im = field(r, 1)
        if r == 0:
            im = im * generic_ref[0]
        z = transform(field(r, 0), im, r, *tables, filt_of(r))
        put(z, r, 0, 0)
        put(z, r, 1, 1)

    @pl.when(generic_ref[0] < 0.5)
    def _():
        re = field(0, 1)
        z = transform(
            re, jnp.zeros_like(re), 2, *tables, lambda ri, c, odd: other_ref[ri, c, :, odd * 128 : (odd + 1) * 128]
        )
        put(z, 0, 1, 0)

    for m in range(STEPS):
        y = jnp.concatenate([obuf[g, pl.ds(m * ROWS * 16, ROWS * 16), :] for g in range(2)], axis=1)
        out_ref[pl.ds(m * ROWS, ROWS)] = encode(y, peak, FILTERED_CODE).reshape(ROWS, 16, F).astype(bf16)


def last_kernel(y_ref, table_ref, peak_ref, out_ref, acc, buf):
    peak = peak_ref[0:1, 0:1]
    step = pl.program_id(0)

    y = decode(y_ref[...].astype(f32), peak, FILTERED_CODE)
    t = table_ref[0]
    pair = step // (STEPS // 2)
    first = step % (STEPS // 2) == 0
    for h in range(2):
        hi, lo = split(y[:, h * 8 : h * 8 + 8, :].reshape(ROWS * 8, F))
        res = dot(t, twice(hi, lo, 0))
        acc[pair, h] = jnp.where(first, res, acc[pair, h] + res)

    @pl.when(step == STEPS - 1)
    def _():
        for pair in range(2):
            for h in range(2):
                for c in range(2):
                    for g in range(2):
                        buf[pl.ds(h * 8 + g * 4 + pair * 2 + c, ND, stride=16), :] = acc[
                            pair, h, c * ND : (c + 1) * ND, g * 128 : (g + 1) * 128
                        ]
        out_ref[...] = encode(buf[...], peak, CONV_CODE).reshape(ND, 16, 128).astype(bf16)


def finish_kernel(y_ref, sig_ref, gate_ref, skip_ref, peak_ref, out_ref, buf):
    peak = peak_ref[0:1, 0:1]
    buf[...] = decode(y_ref[...].astype(f32).reshape(ND * 16, 128), peak, CONV_CODE)
    skip = skip_ref[...]
    for q in range(ND):
        at = pl.ds(q * 512, 512)
        conv = jnp.concatenate([buf[pl.ds(q * 16 + i * 4, 4), :] for i in range(4)], axis=1)
        total = conv + skip * sig_ref[:, at].astype(f32)
        out_ref[:, at] = (gate_ref[:, at].astype(f32) * total).astype(bf16)


VMEM = pl.BlockSpec(memory_space=pltpu.VMEM)
SMEM = pl.BlockSpec(memory_space=pltpu.SMEM)


def call(kernel, ins, outs, scratch, name, flops=0, limit=16, grid=(), in_specs=None, out_specs=None, scalars=0):
    size = sum(int(np.prod(x.shape)) * x.dtype.itemsize for x in (*ins, *outs))
    return pl.pallas_call(
        kernel,
        grid_spec=pltpu.PrefetchScalarGridSpec(
            num_scalar_prefetch=scalars,
            grid=grid,
            in_specs=in_specs or [VMEM] * len(ins),
            out_specs=out_specs or [VMEM] * len(outs),
            scratch_shapes=[pltpu.VMEM(s, d) for s, d in scratch],
        ),
        out_shape=outs,
        compiler_params=pltpu.CompilerParams(vmem_limit_bytes=limit * 2**20),
        cost_estimate=pl.CostEstimate(flops=flops, bytes_accessed=size, transcendentals=0),
        name=name,
    )(*ins)


def exchange(x):
    return lax.all_to_all(x, AXES, split_axis=0, concat_axis=0, tiled=True)


def shape(*dims, dtype=bf16):
    return jax.ShapeDtypeStruct(dims, dtype)


def per_device(signal, gate, skip, spectrum):
    place = lax.axis_index("wide") * lax.axis_size("narrow") + lax.axis_index("narrow")
    (packed,) = call(pack_kernel, (signal,), [shape(ND, 4, 640)], [], "pack")
    spread = exchange(packed)

    upper = (place >= ND // 2).astype(jnp.int32)
    special = place % (ND // 2) == 0
    generic = jnp.where(special, 0.0, 1.0).astype(f32)[None]
    plain, back = (jnp.asarray(t) for t in order_tables())
    order = jnp.stack([jnp.where(place == 0, plain, back), back])
    sign = jnp.stack([jnp.where(place == 0, 1.0, -1.0), -1.0]).astype(f32)
    block = (2, 2, 2, F, F)
    given = call(
        give_kernel,
        ((1 - upper)[None], spectrum, order, sign),
        [shape(4, F, F)] * 2,
        [],
        "give",
        flops=2**30,
        grid=(1,),
        in_specs=[pl.BlockSpec(block, lambda i, half: (0, half[0], 0, 0, 0)), VMEM, SMEM],
        out_specs=[pl.BlockSpec((4, F, F), lambda i, half: (0, 0, 0))] * 2,
        scalars=1,
    )
    mirror = [(p, (ND // 2 - p) if p % (ND // 2) == 0 else ND - p) for p in range(ND)]
    got = [
        lax.ppermute(given[0], AXES, mirror),
        lax.ppermute(given[1], AXES, [(p, ND - 1 - p) for p in range(ND)]),
    ]

    k1 = jnp.stack([place * 2, place * 2 + 1, ND - place * 2])[:, None] % F
    half = jnp.arange(ND, dtype=jnp.int32)

    def wave(index, period):
        angle = (2 * np.pi / period) * (index % period).astype(f32)
        return jnp.stack([jnp.cos(angle), jnp.sin(angle)], axis=1)

    mid = wave(k1 * half, F * ND)
    fine = wave(k1 * jnp.arange(F, dtype=jnp.int32), F**3)
    turn = wave(k1 + F * half, F * F)
    base, cross_base = (jnp.asarray(t) for t in base_tables())
    mf, mi, cross = call(
        table_kernel,
        (base, cross_base, mid[:, :, None, :], fine[:, :, None, :], mid[:, :, :, None]),
        [shape(3, 256, 768), shape(3, 256, 768), shape(3, 2, F, F, dtype=f32)],
        [],
        "tables",
    )
    inner_fwd, inner_inv = (jnp.asarray(t) for t in inner_tables())

    field, peak = call(
        outer_kernel,
        (spread, jnp.asarray(outer_forward_table())),
        [shape(ND, 16, F), shape(8, 128, dtype=f32)],
        [((4, ND * 8, 128), f32), ((ND * 4, 512), bf16)],
        "outer",
        flops=2**29,
        grid=(STEPS,),
        in_specs=[VMEM, pl.BlockSpec((ROWS * 8, 512), lambda i: (i, 0))],
        out_specs=[pl.BlockSpec((ROWS, 16, F), lambda i: (i, 0, 0)), pl.BlockSpec((8, 128), lambda i: (0, 0))],
    )
    field = exchange(field)
    filt, other = call(
        combine_kernel,
        (upper[None], spectrum, plain, *got, generic),
        [shape(2, 2, 2, F, F, dtype=f32), shape(2, 2, F, F, dtype=f32)],
        [],
        "combine",
        flops=2**29,
        grid=(1,),
        in_specs=[pl.BlockSpec(block, lambda i, half: (0, half[0], 0, 0, 0)), VMEM, VMEM, VMEM, SMEM],
        out_specs=[
            pl.BlockSpec((2, 2, 2, F, F), lambda i, half: (0, 0, 0, 0, 0)),
            pl.BlockSpec((2, 2, F, F), lambda i, half: (0, 0, 0, 0)),
        ],
        scalars=1,
    )
    (filtered,) = call(
        middle_kernel,
        (field, peak, mf, mi, cross, turn[:, :, :, None], inner_fwd, inner_inv, filt, other, generic),
        [shape(ND, 16, F)],
        [((2, ND * 16, 128), f32)] * 2,
        "middle",
        flops=4 * 2**30,
        limit=24,
        in_specs=[VMEM] * 10 + [SMEM],
    )
    filtered = exchange(filtered)
    (conv,) = call(
        last_kernel,
        (filtered, jnp.asarray(outer_inverse_table()), peak),
        [shape(ND, 16, 128)],
        [((2, 2, 2 * ND, F), f32), ((ND * 16, 128), f32)],
        "last",
        flops=2**29,
        grid=(STEPS,),
        in_specs=[
            pl.BlockSpec((ROWS, 16, F), lambda i: (i, 0, 0)),
            pl.BlockSpec((1, 2 * ND, ROWS * 24), lambda i: (i, 0, 0)),
            VMEM,
        ],
        out_specs=[VMEM],
    )
    conv = exchange(conv)
    (mixed,) = call(
        finish_kernel,
        (conv, signal, gate, skip[:, None], peak),
        [shape(4, 65536)],
        [((ND * 16, 128), f32)],
        "finish",
    )
    return mixed


def solution(mesh):
    split_spec = P(None, AXES)
    return jax.shard_map(
        per_device,
        mesh=mesh,
        in_specs=(split_spec, split_spec, P(), P(None, None, AXES, None, None)),
        out_specs=split_spec,
        check_vma=False,
    )
```

```python
import jax
import jax.numpy as jnp
import ml_dtypes
import numpy as np
from jax import lax
from jax.experimental import pallas as pl
from jax.experimental.pallas import tpu as pltpu
from jax.sharding import PartitionSpec as P

F = 256
ND = 128
STEPS = 4
ROWS = ND // STEPS
AXES = ("wide", "narrow")
bf16 = jnp.bfloat16
f32 = jnp.float32

OFFSET = 120.0 * np.log(2.0)
SPAN = 240.0
FIELD_CODE = (2.0**-8, 15.1)
FILTERED_CODE = (2.0**-11, 22.2)
CONV_CODE = (2.0**-7, 21.7)
FILTER_TOP = 6.02


def split_np(x):
    hi = x.astype(ml_dtypes.bfloat16)
    lo = (x - hi.astype(np.float64)).astype(ml_dtypes.bfloat16)
    return hi, lo


def outer_waves():
    k1 = np.arange(F).reshape(ND, 2)
    ang = 2 * np.pi * (k1[:, :, None] * np.arange(ND) % F) / F
    wave = np.stack([np.cos(ang), -np.sin(ang)], axis=2)
    for p in (0, ND // 2):
        wave[p, 0, 1] = np.cos(np.pi * (1 - p // (ND // 2)) * np.arange(ND))
    return wave


def outer_forward_table():
    t = np.zeros((ND, 2, 2, 2, 2, ND))
    for c in range(2):
        t[:, :, c, :, c, :] = outer_waves()
    return np.concatenate(split_np(t.reshape(ND * 8, 2 * ND)), axis=1)


def outer_inverse_table():
    t = np.zeros((2, ND, ND, 2, 2, 2))
    for c in range(2):
        t[c, :, :, :, c, :] = outer_waves().transpose(3, 0, 1, 2)
    hi, lo = (x.reshape(2 * ND, STEPS, -1) for x in split_np(t.reshape(2 * ND, ND * 8)))
    return np.ascontiguousarray(np.concatenate([hi, hi, lo], axis=2).transpose(1, 0, 2))


def inner_tables():
    low = np.arange(ND)
    out = []
    for odd in range(2):
        ang = 2 * np.pi * (low[:, None] * (2 * low[None] + odd) % F) / F
        c, s = np.cos(ang), np.sin(ang)
        fwd = split_np(np.block([[c, -s], [s, c]]))
        inv = split_np(np.block([[c.T, s.T], [-s.T, c.T]]) / F)
        out.append([np.concatenate(x, axis=0) for x in (fwd, inv)])
    return np.stack([out[0][0], out[1][0]]), np.stack([out[0][1], out[1][1]])


def order_tables():
    eye = np.eye(F)
    even_odd = np.concatenate([np.arange(0, F, 2), np.arange(1, F, 2)])
    plain = np.stack([eye, eye[:, even_odd]])
    back = np.stack([eye[::-1], eye[:, 255 - even_odd]])
    return plain.astype(ml_dtypes.bfloat16), back.astype(ml_dtypes.bfloat16)


def base_tables():
    i = np.arange(F)
    half = np.arange(ND)
    a0 = 2 * np.pi * (half[:, None] * half[None] % ND) / ND
    a1 = 2 * np.pi * (i[:, None] * i[None]) / (F * F)
    return (
        np.stack([np.cos(a0), np.sin(a0)]).astype(np.float32),
        np.stack([np.cos(a1), np.sin(a1)]).astype(np.float32),
    )


def peak_of(peak_ref):
    return jnp.maximum(jnp.max(peak_ref[...], keepdims=True), 1e-30)


def encode(x, peak, code):
    knee, octaves = code
    beta = SPAN / octaves
    z = jnp.abs(x) * (1.0 / (peak * knee))
    y = jnp.exp(jnp.minimum(beta * jnp.log(1.0 + z) - OFFSET, OFFSET))
    return jnp.where(x < 0, -y, y)


def decode(y, peak, code):
    knee, octaves = code
    beta = SPAN / octaves
    z = jnp.exp(jnp.log(jnp.abs(y)) * (1.0 / beta) + OFFSET / beta) - 1.0
    z = z * (peak * knee)
    return jnp.where(y < 0, -z, z)


def encode_filter(x):
    y = jnp.exp(jnp.abs(x) * (SPAN * np.log(2.0) / FILTER_TOP) - OFFSET)
    return jnp.where(x < 0, -y, y)


def decode_filter(y):
    z = (jnp.log(jnp.abs(y)) + OFFSET) * (FILTER_TOP / (SPAN * np.log(2.0)))
    return jnp.where(y < 0, -z, z)


def split(x):
    hi = x.astype(bf16)
    return hi, (x - hi.astype(f32)).astype(bf16)


def dot(a, b):
    return jnp.dot(a, b, preferred_element_type=f32)


def twice(hi, lo, axis):
    return jnp.concatenate([hi, lo, hi], axis=axis)


def wide_table(t, axis):
    hi, lo = jnp.split(t, 2, axis=axis)
    return jnp.concatenate([hi, hi, lo], axis=axis)


def pack_kernel(sig_ref, out_ref):
    top = jnp.zeros((4, 128), f32)
    for q in range(ND):
        x = sig_ref[:, pl.ds(q * 512, 512)]
        out_ref[q, :, pl.ds(0, 512)] = x
        x = jnp.abs(x.astype(f32))
        for i in range(4):
            top = jnp.maximum(top, x[:, i * 128 : (i + 1) * 128])
    top = top.astype(bf16)
    for q in range(ND):
        out_ref[q, :, pl.ds(512, 128)] = top


def outer_kernel(x_ref, table_ref, out_ref, peak_ref, buf, xs):
    @pl.when(pl.program_id(0) == 0)
    def _():
        top = jnp.zeros((4, 128), f32)
        for n in range(ND):
            x = x_ref[n].astype(f32)
            top = jnp.maximum(top, x[:, 512:640])
            for i in range(4):
                buf[i, pl.ds(n * 8, 4), :] = x[:, i * 128 : (i + 1) * 128]
        peak_ref[...] = jnp.broadcast_to(jnp.maximum(jnp.max(top, keepdims=True), 1e-30), (8, 128))
        for c in range(4):
            parts = [buf[i, pl.ds(c, ND, stride=8), :] for i in range(4)]
            xs[pl.ds(c * ND, ND), :] = jnp.concatenate(parts, axis=1).astype(bf16)

    x = xs[pl.ds(pl.program_id(0) // (STEPS // 2) * 256, 256), :]
    res = encode(dot(table_ref[...], jnp.concatenate([x, x], axis=0)), peak_ref[0:1, 0:1], FIELD_CODE)
    parts = [res[:, h * F : (h + 1) * F].reshape(ROWS, 8, F) for h in range(2)]
    out_ref[...] = jnp.concatenate(parts, axis=1).astype(bf16)


def fill_tables(table, base_ref, cross_base_ref, wave_ref, mf_ref, mi_ref, cross_ref, turn_ref):
    def wave(row, lanes):
        return wave_ref[table, row : row + 1, 0:lanes]

    cb, sb = wave(0, ND), wave(1, ND)
    c0, s0 = base_ref[0], base_ref[1]
    c, s = c0 * cb - s0 * sb, s0 * cb + c0 * sb
    for out_ref, c, s in ((mf_ref, c, s), (mi_ref, c.T * (1.0 / F), s.T * (-1.0 / F))):
        (ch, cl), (sh, sl) = split(c), split(s)
        for part, (cc, ss) in enumerate(((ch, sh), (cl, sl))):
            at = part * 256
            out_ref[table, 0:128, at : at + 128] = cc
            out_ref[table, 0:128, at + 128 : at + 256] = ss
            out_ref[table, 128:256, at : at + 128] = -ss
            out_ref[table, 128:256, at + 128 : at + 256] = cc
    cb, sb = wave(2, F), wave(3, F)
    c1, s1 = cross_base_ref[0], cross_base_ref[1]
    cross_ref[table, 0] = c1 * cb - s1 * sb
    cross_ref[table, 1] = s1 * cb + c1 * sb
    for i in range(2):
        turn_ref[table, i] = jnp.broadcast_to(wave(4 + i, ND), (ND, ND)).T


def give_kernel(flag_ref, filt_ref, order_ref, out0_ref, out1_ref):
    first = flag_ref[1]
    for r, out_ref in enumerate((out0_ref, out1_ref)):
        kind = first if r == 0 else 0
        left, right = order_ref[kind, 0], order_ref[kind, 1]
        sign = (2 * kind - 1) * jnp.float32(1.0)
        for ri in range(2):
            for c in range(2):
                hi, lo = split(filt_ref[ri, c, r])
                hi, lo = split(dot(hi, right) + dot(lo, right))
                x = dot(left, hi) + dot(left, lo)
                if ri:
                    x = x * sign
                out_ref[ri * 2 + c] = encode_filter(x).astype(bf16)


def combine_kernel(half_ref, filt_ref, order_ref, got0_ref, got1_ref, generic_ref, out_ref, other_ref):
    del half_ref
    for r, got_ref in enumerate((got0_ref, got1_ref)):
        for ri in range(2):
            for c in range(2):
                got = decode_filter(got_ref[ri * 2 + c].astype(f32))
                if r == 0:
                    other_ref[ri, c] = got
                    got = got * generic_ref[0]
                hi, lo = split(filt_ref[ri, c, r])
                out_ref[r, ri, c] = dot(hi, order_ref[1]) + dot(lo, order_ref[1]) + got


def transform(re, im, table, mf_ref, mi_ref, cross_ref, turn_ref, fwd_ref, inv_ref, filt, arrive):
    tc, ts = (jnp.concatenate([turn_ref[table, i]] * 2, axis=1) for i in range(2))
    if im is None:
        hi, lo = split(re)
        t = jnp.concatenate([mf_ref[table, :, 0:128], mf_ref[table, :, 256:384]], axis=1)
    else:
        hi, lo = split(jnp.concatenate([re, im], axis=0))
        t = mf_ref[table]
    z = dot(wide_table(t, 1), twice(hi, lo, 0))
    yield
    sums, diffs = [], []
    for c in range(2):
        at = c * 512
        dr, di = z[:128, at : at + 256], z[128:, at : at + 256]
        er, ei = z[:128, at + 256 : at + 512], z[128:, at + 256 : at + 512]
        pr, pi = er * tc + ei * ts, ei * tc - er * ts
        for zr, zi, e in ((dr + pr, di + pi, 0), (dr - pr, di - pi, 128)):
            cosine, sine = cross_ref[table, 0, e : e + 128], cross_ref[table, 1, e : e + 128]
            zr, zi = zr * cosine + zi * sine, zi * cosine - zr * sine
            sums.append(jnp.concatenate([zr[:, :128] + zr[:, 128:], zi[:, :128] + zi[:, 128:]], axis=1))
            diffs.append(jnp.concatenate([zr[:, :128] - zr[:, 128:], zi[:, :128] - zi[:, 128:]], axis=1))
    arrive("fwd")
    spectra = []
    for odd, rows in enumerate((sums, diffs)):
        hi, lo = split(jnp.concatenate(rows, axis=0))
        spectra.append(dot(twice(hi, lo, 1), wide_table(fwd_ref[odd], 0)))
    yield
    arrive(("filt", table))
    arrive("inv")
    back = []
    for odd, z in enumerate(spectra):
        rows = []
        for c in range(2):
            zr, zi = z[c * F : (c + 1) * F, :128], z[c * F : (c + 1) * F, 128:]
            fr, fi = filt(0, c, odd), filt(1, c, odd)
            rows.append(jnp.concatenate([zr * fr - zi * fi, zi * fr + zr * fi], axis=1))
        hi, lo = split(jnp.concatenate(rows, axis=0))
        back.append(dot(twice(hi, lo, 1), wide_table(inv_ref[odd], 0)))
    yield
    even, odd = back
    tops, bottoms = [], []
    for c in range(2):
        both = []
        for e in (0, 128):
            at = c * F + e
            er, ei = even[at : at + 128, :128], even[at : at + 128, 128:]
            dr, di = odd[at : at + 128, :128], odd[at : at + 128, 128:]
            zr = jnp.concatenate([er + dr, er - dr], axis=1)
            zi = jnp.concatenate([ei + di, ei - di], axis=1)
            cosine = cross_ref[table, 0, e : e + 128] * (1.0 / F)
            sine = cross_ref[table, 1, e : e + 128] * (1.0 / F)
            both.append((zr * cosine - zi * sine, zi * cosine + zr * sine))
        (ar, ai), (br, bi) = both
        ur, ui = ar - br, ai - bi
        tops += [ar + br, ur * tc - ui * ts]
        bottoms += [ai + bi, ui * tc + ur * ts]
    hi, lo = split(jnp.concatenate([jnp.concatenate(tops, axis=1), jnp.concatenate(bottoms, axis=1)], axis=0))
    t = mi_ref[table] if im is not None else mi_ref[table, 0:128]
    yield dot(wide_table(t, 1), twice(hi, lo, 0))


def middle_kernel(
    y_hbm, base_hbm, cross_base_hbm, fwd_hbm, inv_hbm, filt_hbm, other_hbm, peak_ref, wave_ref, generic_ref, out_hbm, buf, obuf, *held
):
    y_ref, base_ref, cross_base_ref, fwd_ref, inv_ref, filt_ref, other_ref = held[:7]
    mf_ref, mi_ref, cross_ref, turn_ref, out_ref, sem = held[7:]
    blocks = [pl.ds(m * ROWS, ROWS) for m in range(STEPS)]
    sources = {"base": (base_hbm, base_ref), "cross": (cross_base_hbm, cross_base_ref)}
    for m, b in enumerate(blocks):
        sources["y", m] = (y_hbm.at[b], y_ref.at[b])
    sources["fwd"] = (fwd_hbm, fwd_ref)
    for ri in range(2):
        sources["filt", 0, ri] = (filt_hbm.at[0, ri], filt_ref.at[0, ri])
    sources["inv"] = (inv_hbm, inv_ref)
    for ri in range(2):
        sources["filt", 1, ri] = (filt_hbm.at[1, ri], filt_ref.at[1, ri])
    sources["filt", 2, 0] = (other_hbm, other_ref)
    copies = {k: pltpu.make_async_copy(*v, sem.at[i]) for i, (k, v) in enumerate(sources.items())}
    waiting = set(copies)

    def arrive(key):
        for k in list(copies):
            if k in waiting and (k == key or k[:2] == key):
                waiting.remove(k)
                copies[k].wait()

    for copy in copies.values():
        copy.start()
    peak = peak_ref[0:1, 0:1]
    tables = (mf_ref, mi_ref, cross_ref, turn_ref, fwd_ref, inv_ref)
    arrive("base")
    arrive("cross")
    for r in range(2):
        fill_tables(r, base_ref, cross_base_ref, wave_ref, *tables[:4])
    for m in range(STEPS):
        arrive(("y", m))
        y = decode(y_ref[blocks[m]].astype(f32), peak, FIELD_CODE).reshape(ROWS * 16, F)
        for g in range(2):
            buf[g, pl.ds(m * ROWS * 16, ROWS * 16), :] = y[:, g * 128 : (g + 1) * 128]

    def field(r, ri):
        return jnp.concatenate(
            [
                buf[g, pl.ds(h * 8 + r * 4 + c * 2 + ri, ND, stride=16), :]
                for c in range(2)
                for h in range(2)
                for g in range(2)
            ],
            axis=1,
        )

    def put(z, r, ri, part):
        for c in range(2):
            for h in range(2):
                for g in range(2):
                    at = c * 512 + h * 256 + g * 128
                    obuf[g, pl.ds(h * 8 + r * 4 + c * 2 + ri, ND, stride=16), :] = z[
                        part * 128 : (part + 1) * 128, at : at + 128
                    ]

    def filt_of(r):
        return lambda ri, c, odd: filt_ref[r, ri, c, :, odd * 128 : (odd + 1) * 128]

    running = []
    for r in range(2):
        im = field(r, 1)
        if r == 0:
            im = im * generic_ref[0]
        running.append(transform(field(r, 0), im, r, *tables, filt_of(r), arrive))
    for stage in range(4):
        for r in range(2):
            z = next(running[r])
            if stage == 3:
                put(z, r, 0, 0)
                put(z, r, 1, 1)

    arrive(("filt", 2))

    @pl.when(generic_ref[0] < 0.5)
    def _():
        fill_tables(2, base_ref, cross_base_ref, wave_ref, *tables[:4])
        *_, z = transform(
            field(0, 1),
            None,
            2,
            *tables,
            lambda ri, c, odd: other_ref[ri, c, :, odd * 128 : (odd + 1) * 128],
            arrive,
        )
        put(z, 0, 1, 0)

    writes = []
    for m in range(STEPS):
        y = jnp.concatenate([obuf[g, pl.ds(m * ROWS * 16, ROWS * 16), :] for g in range(2)], axis=1)
        out_ref[blocks[m]] = encode(y, peak, FILTERED_CODE).reshape(ROWS, 16, F).astype(bf16)
        writes.append(pltpu.make_async_copy(out_ref.at[blocks[m]], out_hbm.at[blocks[m]], sem.at[len(copies) + m]))
        writes[-1].start()
    for copy in writes:
        copy.wait()


def last_kernel(y_ref, table_ref, peak_ref, out_ref, acc, buf):
    peak = peak_ref[0:1, 0:1]
    step = pl.program_id(0)

    y = decode(y_ref[...].astype(f32), peak, FILTERED_CODE)
    t = table_ref[0]
    pair = step // (STEPS // 2)
    first = step % (STEPS // 2) == 0
    for h in range(2):
        hi, lo = split(y[:, h * 8 : h * 8 + 8, :].reshape(ROWS * 8, F))
        res = dot(t, twice(hi, lo, 0))
        acc[pair, h] = jnp.where(first, res, acc[pair, h] + res)

    @pl.when(step == STEPS - 1)
    def _():
        for pair in range(2):
            for h in range(2):
                for c in range(2):
                    for g in range(2):
                        buf[pl.ds(h * 8 + g * 4 + pair * 2 + c, ND, stride=16), :] = acc[
                            pair, h, c * ND : (c + 1) * ND, g * 128 : (g + 1) * 128
                        ]
        out_ref[...] = encode(buf[...], peak, CONV_CODE).reshape(ND, 16, 128).astype(bf16)


def finish_kernel(y_ref, sig_ref, gate_ref, skip_ref, peak_ref, out_ref, buf):
    peak = peak_ref[0:1, 0:1]
    buf[...] = decode(y_ref[...].astype(f32).reshape(ND * 16, 128), peak, CONV_CODE)
    skip = skip_ref[...]
    for q in range(ND):
        at = pl.ds(q * 512, 512)
        conv = jnp.concatenate([buf[pl.ds(q * 16 + i * 4, 4), :] for i in range(4)], axis=1)
        total = conv + skip * sig_ref[:, at].astype(f32)
        out_ref[:, at] = (gate_ref[:, at].astype(f32) * total).astype(bf16)


VMEM = pl.BlockSpec(memory_space=pltpu.VMEM)
SMEM = pl.BlockSpec(memory_space=pltpu.SMEM)
ANY = pl.BlockSpec(memory_space=pl.ANY)


def call(kernel, ins, outs, scratch, name, flops=0, limit=16, grid=(), in_specs=None, out_specs=None, scalars=0):
    size = sum(int(np.prod(x.shape)) * x.dtype.itemsize for x in (*ins, *outs))
    return pl.pallas_call(
        kernel,
        grid_spec=pltpu.PrefetchScalarGridSpec(
            num_scalar_prefetch=scalars,
            grid=grid,
            in_specs=in_specs or [VMEM] * len(ins),
            out_specs=out_specs or [VMEM] * len(outs),
            scratch_shapes=[d(s) if d is pltpu.SemaphoreType.DMA else pltpu.VMEM(s, d) for s, d in scratch],
        ),
        out_shape=outs,
        compiler_params=pltpu.CompilerParams(vmem_limit_bytes=limit * 2**20),
        cost_estimate=pl.CostEstimate(flops=flops, bytes_accessed=size, transcendentals=0),
        name=name,
    )(*ins)


def exchange(x):
    return lax.all_to_all(x, AXES, split_axis=0, concat_axis=0, tiled=True)


def shape(*dims, dtype=bf16):
    return jax.ShapeDtypeStruct(dims, dtype)


def per_device(signal, gate, skip, spectrum):
    place = lax.axis_index("wide") * lax.axis_size("narrow") + lax.axis_index("narrow")
    (packed,) = call(pack_kernel, (signal,), [shape(ND, 4, 640)], [], "pack")
    spread = exchange(packed)

    upper = (place >= ND // 2).astype(jnp.int32)
    special = place % (ND // 2) == 0
    generic = jnp.where(special, 0.0, 1.0).astype(f32)[None]
    plain, back = order_tables()
    block = (2, 2, 2, F, F)
    given = call(
        give_kernel,
        (jnp.stack([1 - upper, (place == 0).astype(jnp.int32)]), spectrum, jnp.asarray(np.stack([back, plain]))),
        [shape(4, F, F)] * 2,
        [],
        "give",
        limit=58,
        flops=2**30,
        grid=(1,),
        in_specs=[pl.BlockSpec(block, lambda i, flag: (0, flag[0], 0, 0, 0)), VMEM],
        out_specs=[pl.BlockSpec((4, F, F), lambda i, flag: (0, 0, 0))] * 2,
        scalars=1,
    )
    spread, *_ = lax.optimization_barrier((spread, *given))
    mirror = [(p, (ND // 2 - p) if p % (ND // 2) == 0 else ND - p) for p in range(ND)]
    got = [
        lax.ppermute(given[0], AXES, mirror),
        lax.ppermute(given[1], AXES, [(p, ND - 1 - p) for p in range(ND)]),
    ]

    k1 = jnp.stack([place * 2, place * 2 + 1, ND - place * 2])[:, None] % F
    lane = jnp.arange(F, dtype=jnp.int32)
    turns = jnp.stack([k1 * lane % (F * ND) * (F * 2), k1 * lane, (k1 + F * lane) % (F * F) * F], axis=1)
    angle = (2 * np.pi / F**3) * turns.astype(f32)
    wave = jnp.stack([jnp.cos(angle), jnp.sin(angle)], axis=2).reshape(3, 6, F)
    base, cross_base = (jnp.asarray(t) for t in base_tables())
    inner_fwd, inner_inv = (jnp.asarray(t) for t in inner_tables())

    field, peak = call(
        outer_kernel,
        (spread, jnp.asarray(outer_forward_table())),
        [shape(ND, 16, F), shape(8, 128, dtype=f32)],
        [((4, ND * 8, 128), f32), ((ND * 4, 512), bf16)],
        "outer",
        flops=2**29,
        grid=(STEPS,),
        in_specs=[VMEM, pl.BlockSpec((ROWS * 8, 512), lambda i: (i, 0))],
        out_specs=[pl.BlockSpec((ROWS, 16, F), lambda i: (i, 0, 0)), pl.BlockSpec((8, 128), lambda i: (0, 0))],
    )
    field = exchange(field)
    filt, other = call(
        combine_kernel,
        (upper[None], spectrum, jnp.asarray(plain), *got, generic),
        [shape(2, 2, 2, F, F, dtype=f32), shape(2, 2, F, F, dtype=f32)],
        [],
        "combine",
        limit=58,
        flops=2**34,
        grid=(1,),
        in_specs=[pl.BlockSpec(block, lambda i, half: (0, half[0], 0, 0, 0)), VMEM, VMEM, VMEM, SMEM],
        out_specs=[
            pl.BlockSpec((2, 2, 2, F, F), lambda i, half: (0, 0, 0, 0, 0)),
            pl.BlockSpec((2, 2, F, F), lambda i, half: (0, 0, 0, 0)),
        ],
        scalars=1,
    )
    loads = (field, base, cross_base, inner_fwd, inner_inv, filt, other)
    (filtered,) = call(
        middle_kernel,
        (*loads, peak, wave, generic),
        [shape(ND, 16, F)],
        [((2, ND * 16, 128), f32)] * 2
        + [(x.shape, x.dtype) for x in loads]
        + [((3, 256, 512), bf16)] * 2
        + [((3, 2, F, F), f32), ((3, 2, ND, ND), f32), ((ND, 16, F), bf16)]
        + [((9 + 2 * STEPS,), pltpu.SemaphoreType.DMA)],
        "middle",
        flops=4 * 2**30,
        limit=58,
        in_specs=[ANY] * 7 + [VMEM, VMEM, SMEM],
        out_specs=[ANY],
    )
    filtered = exchange(filtered)
    (conv,) = call(
        last_kernel,
        (filtered, jnp.asarray(outer_inverse_table()), peak),
        [shape(ND, 16, 128)],
        [((2, 2, 2 * ND, F), f32), ((ND * 16, 128), f32)],
        "last",
        flops=2**29,
        grid=(STEPS,),
        in_specs=[
            pl.BlockSpec((ROWS, 16, F), lambda i: (i, 0, 0)),
            pl.BlockSpec((1, 2 * ND, ROWS * 24), lambda i: (i, 0, 0)),
            VMEM,
        ],
        out_specs=[VMEM],
    )
    conv = exchange(conv)
    (mixed,) = call(
        finish_kernel,
        (conv, signal, gate, skip[:, None], peak),
        [shape(4, 65536)],
        [((ND * 16, 128), f32)],
        "finish",
    )
    return mixed


def solution(mesh):
    split_spec = P(None, AXES)
    return jax.shard_map(
        per_device,
        mesh=mesh,
        in_specs=(split_spec, split_spec, P(), P(None, None, AXES, None, None)),
        out_specs=split_spec,
        check_vma=False,
    )
```

```python
import jax
import jax.numpy as jnp
import ml_dtypes
import numpy as np
from jax import lax
from jax.experimental import pallas as pl
from jax.experimental.pallas import tpu as pltpu
from jax.sharding import PartitionSpec as P

F = 256
ND = 128
STEPS = 4
ROWS = ND // STEPS
AXES = ("wide", "narrow")
bf16 = jnp.bfloat16
f32 = jnp.float32

OFFSET = 120.0 * np.log(2.0)
SPAN = 240.0
FIELD_CODE = (2.0**-8, 15.1)
FILTERED_CODE = (2.0**-11, 22.2)
CONV_CODE = (2.0**-7, 21.7)
FILTER_TOP = 6.02


def split_np(x):
    hi = x.astype(ml_dtypes.bfloat16)
    lo = (x - hi.astype(np.float64)).astype(ml_dtypes.bfloat16)
    return hi, lo


def outer_waves():
    k1 = np.arange(F).reshape(ND, 2)
    ang = 2 * np.pi * (k1[:, :, None] * np.arange(ND) % F) / F
    wave = np.stack([np.cos(ang), -np.sin(ang)], axis=2)
    for p in (0, ND // 2):
        wave[p, 0, 1] = np.cos(np.pi * (1 - p // (ND // 2)) * np.arange(ND))
    return wave


def outer_forward_table():
    t = np.zeros((ND, 2, 2, 2, 2, ND))
    for c in range(2):
        t[:, :, c, :, c, :] = outer_waves()
    return np.concatenate(split_np(t.reshape(ND * 8, 2 * ND)), axis=1)


def outer_inverse_table():
    t = np.zeros((2, ND, ND, 2, 2, 2))
    for c in range(2):
        t[c, :, :, :, c, :] = outer_waves().transpose(3, 0, 1, 2)
    hi, lo = (x.reshape(2 * ND, STEPS, -1) for x in split_np(t.reshape(2 * ND, ND * 8)))
    return np.ascontiguousarray(np.concatenate([hi, hi, lo], axis=2).transpose(1, 0, 2))


def inner_tables():
    low = np.arange(ND)
    out = []
    for odd in range(2):
        ang = 2 * np.pi * (low[:, None] * (2 * low[None] + odd) % F) / F
        c, s = np.cos(ang), np.sin(ang)
        fwd = split_np(np.block([[c, -s], [s, c]]))
        inv = split_np(np.block([[c.T, s.T], [-s.T, c.T]]) / F)
        out.append([np.concatenate(x, axis=0) for x in (fwd, inv)])
    return np.stack([out[0][0], out[1][0]]), np.stack([out[0][1], out[1][1]])


def order_tables():
    eye = np.eye(F)
    even_odd = np.concatenate([np.arange(0, F, 2), np.arange(1, F, 2)])
    plain = np.stack([eye, eye[:, even_odd]])
    back = np.stack([eye[::-1], eye[:, 255 - even_odd]])
    return plain.astype(ml_dtypes.bfloat16), back.astype(ml_dtypes.bfloat16)


def base_tables():
    i = np.arange(F)
    half = np.arange(ND)
    a0 = 2 * np.pi * (half[:, None] * half[None] % ND) / ND
    a1 = 2 * np.pi * (i[:, None] * i[None]) / (F * F)
    return (
        np.stack([np.cos(a0), np.sin(a0)]).astype(np.float32),
        np.stack([np.cos(a1), np.sin(a1)]).astype(np.float32),
    )


def peak_of(peak_ref):
    return jnp.maximum(jnp.max(peak_ref[...], keepdims=True), 1e-30)


def encode(x, peak, code):
    knee, octaves = code
    beta = SPAN / octaves
    z = jnp.abs(x) * (1.0 / (peak * knee))
    y = jnp.exp(jnp.minimum(beta * jnp.log(1.0 + z) - OFFSET, OFFSET))
    return jnp.where(x < 0, -y, y)


def decode(y, peak, code):
    knee, octaves = code
    beta = SPAN / octaves
    z = jnp.exp(jnp.log(jnp.abs(y)) * (1.0 / beta) + OFFSET / beta) - 1.0
    z = z * (peak * knee)
    return jnp.where(y < 0, -z, z)


def encode_filter(x):
    y = jnp.exp(jnp.abs(x) * (SPAN * np.log(2.0) / FILTER_TOP) - OFFSET)
    return jnp.where(x < 0, -y, y)


def decode_filter(y):
    z = (jnp.log(jnp.abs(y)) + OFFSET) * (FILTER_TOP / (SPAN * np.log(2.0)))
    return jnp.where(y < 0, -z, z)


def split(x):
    hi = x.astype(bf16)
    return hi, (x - hi.astype(f32)).astype(bf16)


def dot(a, b):
    return jnp.dot(a, b, preferred_element_type=f32)


def twice(hi, lo, axis):
    return jnp.concatenate([hi, lo, hi], axis=axis)


def wide_table(t, axis):
    hi, lo = jnp.split(t, 2, axis=axis)
    return jnp.concatenate([hi, hi, lo], axis=axis)


def pack_kernel(sig_ref, out_ref):
    top = jnp.zeros((4, 128), f32)
    for q in range(ND):
        x = sig_ref[:, pl.ds(q * 512, 512)]
        out_ref[q, :, pl.ds(0, 512)] = x
        x = jnp.abs(x.astype(f32))
        for i in range(4):
            top = jnp.maximum(top, x[:, i * 128 : (i + 1) * 128])
    top = top.astype(bf16)
    for q in range(ND):
        out_ref[q, :, pl.ds(512, 128)] = top


def outer_kernel(x_ref, table_ref, out_ref, peak_ref, buf, xs):
    @pl.when(pl.program_id(0) == 0)
    def _():
        top = jnp.zeros((4, 128), f32)
        for n in range(ND):
            x = x_ref[n].astype(f32)
            top = jnp.maximum(top, x[:, 512:640])
            for i in range(4):
                buf[i, pl.ds(n * 8, 4), :] = x[:, i * 128 : (i + 1) * 128]
        peak_ref[...] = jnp.broadcast_to(jnp.maximum(jnp.max(top, keepdims=True), 1e-30), (8, 128))
        for c in range(4):
            parts = [buf[i, pl.ds(c, ND, stride=8), :] for i in range(4)]
            xs[pl.ds(c * ND, ND), :] = jnp.concatenate(parts, axis=1).astype(bf16)

    x = xs[pl.ds(pl.program_id(0) // (STEPS // 2) * 256, 256), :]
    res = encode(dot(table_ref[...], jnp.concatenate([x, x], axis=0)), peak_ref[0:1, 0:1], FIELD_CODE)
    parts = [res[:, h * F : (h + 1) * F].reshape(ROWS, 8, F) for h in range(2)]
    out_ref[...] = jnp.concatenate(parts, axis=1).astype(bf16)


def fill_tables(table, base_ref, cross_base_ref, wave_ref, mf_ref, mi_ref, cross_ref, turn_ref):
    def wave(row, lanes):
        return wave_ref[table, row : row + 1, 0:lanes]

    cb, sb = wave(0, ND), wave(1, ND)
    c0, s0 = base_ref[0:128, 0:128], base_ref[128:256, 0:128]
    c, s = c0 * cb - s0 * sb, s0 * cb + c0 * sb
    for out_ref, c, s in ((mf_ref, c, s), (mi_ref, c.T * (1.0 / F), s.T * (-1.0 / F))):
        (ch, cl), (sh, sl) = split(c), split(s)
        for part, (cc, ss) in enumerate(((ch, sh), (cl, sl))):
            at = part * 256
            out_ref[table, 0:128, at : at + 128] = cc
            out_ref[table, 0:128, at + 128 : at + 256] = ss
            out_ref[table, 128:256, at : at + 128] = -ss
            out_ref[table, 128:256, at + 128 : at + 256] = cc
    cb, sb = wave(2, F), wave(3, F)
    c1, s1 = cross_base_ref[0], cross_base_ref[1]
    cross_ref[table, 0] = c1 * cb - s1 * sb
    cross_ref[table, 1] = s1 * cb + c1 * sb
    for i in range(2):
        turn_ref[table, i] = jnp.broadcast_to(wave(4 + i, ND), (ND, ND)).T


def place_of():
    return lax.axis_index("wide") * lax.axis_size("narrow") + lax.axis_index("narrow")


def fetch_filter(r, pair, filt_hbm, held, sem):
    copies = []
    for i in range(4):
        source = filt_hbm.at[i // 2, pair * 2 + i % 2, r]
        copies.append(pltpu.make_async_copy(source, held.at[r, i], sem.at[r, i]))
        copies[-1].start()
    return copies


def give_kernel(r, order_ref, filt_hbm, out_ref, held, sem):
    place = place_of()
    copies = fetch_filter(r, 1 - place // (ND // 2), filt_hbm, held, sem)
    kind = jnp.where(place == 0, 1, 0) if r == 0 else 0
    left, right = order_ref[kind, 0], order_ref[kind, 1]
    sign = (2 * kind - 1) * jnp.float32(1.0)
    for copy in copies:
        copy.wait()
    for i in range(4):
        hi, lo = split(held[r, i])
        hi, lo = split(dot(hi, right) + dot(lo, right))
        x = dot(left, hi) + dot(left, lo)
        if i >= 2:
            x = x * sign
        out_ref[i] = encode_filter(x).astype(bf16)


def combine_kernel(filt_hbm, order_ref, cross_base_ref, base_ref, got0_ref, got1_ref, out_ref, held, sem):
    place = place_of()
    copies = [fetch_filter(r, place // (ND // 2), filt_hbm, held, sem) for r in range(2)]
    generic = jnp.where(place % (ND // 2) == 0, 0.0, 1.0)
    out_ref[12:14] = cross_base_ref[...]
    out_ref[14, 0:128, 0:128] = base_ref[0]
    out_ref[14, 128:256, 0:128] = base_ref[1]
    out_ref[14, :, 128:256] = jnp.zeros((F, 128), f32)
    for copy in (*copies[0], *copies[1]):
        copy.wait()
    for r, got_ref in enumerate((got0_ref, got1_ref)):
        for i in range(4):
            got = decode_filter(got_ref[i].astype(f32))
            if r == 0:
                out_ref[8 + i] = got
                got = got * generic
            hi, lo = split(held[r, i])
            out_ref[r * 4 + i] = dot(hi, order_ref[1]) + dot(lo, order_ref[1]) + got


def transform(re, im, table, mf_ref, mi_ref, cross_ref, turn_ref, inner_ref, filt, arrive):
    tc, ts = (jnp.concatenate([turn_ref[table, i]] * 2, axis=1) for i in range(2))
    if im is None:
        hi, lo = split(re)
        t = jnp.concatenate([mf_ref[table, :, 0:128], mf_ref[table, :, 256:384]], axis=1)
    else:
        hi, lo = split(jnp.concatenate([re, im], axis=0))
        t = mf_ref[table]
    z = dot(wide_table(t, 1), twice(hi, lo, 0))
    yield
    sums, diffs = [], []
    for c in range(2):
        at = c * 512
        dr, di = z[:128, at : at + 256], z[128:, at : at + 256]
        er, ei = z[:128, at + 256 : at + 512], z[128:, at + 256 : at + 512]
        pr, pi = er * tc + ei * ts, ei * tc - er * ts
        for zr, zi, e in ((dr + pr, di + pi, 0), (dr - pr, di - pi, 128)):
            cosine, sine = cross_ref[table, 0, e : e + 128], cross_ref[table, 1, e : e + 128]
            zr, zi = zr * cosine + zi * sine, zi * cosine - zr * sine
            sums.append(jnp.concatenate([zr[:, :128] + zr[:, 128:], zi[:, :128] + zi[:, 128:]], axis=1))
            diffs.append(jnp.concatenate([zr[:, :128] - zr[:, 128:], zi[:, :128] - zi[:, 128:]], axis=1))
    arrive("inner")
    spectra = []
    for odd, rows in enumerate((sums, diffs)):
        hi, lo = split(jnp.concatenate(rows, axis=0))
        spectra.append(dot(twice(hi, lo, 1), wide_table(inner_ref[0, odd], 0)))
    yield
    arrive(("filt", table))
    back = []
    for odd, z in enumerate(spectra):
        rows = []
        for c in range(2):
            zr, zi = z[c * F : (c + 1) * F, :128], z[c * F : (c + 1) * F, 128:]
            fr, fi = filt(0, c, odd), filt(1, c, odd)
            rows.append(jnp.concatenate([zr * fr - zi * fi, zi * fr + zr * fi], axis=1))
        hi, lo = split(jnp.concatenate(rows, axis=0))
        back.append(dot(twice(hi, lo, 1), wide_table(inner_ref[1, odd], 0)))
    yield
    even, odd = back
    tops, bottoms = [], []
    for c in range(2):
        both = []
        for e in (0, 128):
            at = c * F + e
            er, ei = even[at : at + 128, :128], even[at : at + 128, 128:]
            dr, di = odd[at : at + 128, :128], odd[at : at + 128, 128:]
            zr = jnp.concatenate([er + dr, er - dr], axis=1)
            zi = jnp.concatenate([ei + di, ei - di], axis=1)
            cosine = cross_ref[table, 0, e : e + 128] * (1.0 / F)
            sine = cross_ref[table, 1, e : e + 128] * (1.0 / F)
            both.append((zr * cosine - zi * sine, zi * cosine + zr * sine))
        (ar, ai), (br, bi) = both
        ur, ui = ar - br, ai - bi
        tops += [ar + br, ur * tc - ui * ts]
        bottoms += [ai + bi, ui * tc + ur * ts]
    hi, lo = split(jnp.concatenate([jnp.concatenate(tops, axis=1), jnp.concatenate(bottoms, axis=1)], axis=0))
    t = mi_ref[table] if im is not None else mi_ref[table, 0:128]
    yield dot(wide_table(t, 1), twice(hi, lo, 0))


def middle_kernel(y_ref, inner_hbm, bundle_hbm, peak_ref, wave_ref, out_hbm, buf, obuf, *held):
    inner_ref, base_ref, cross_base_ref, filt_ref, other_ref = held[:5]
    mf_ref, mi_ref, cross_ref, turn_ref, out_ref, sem = held[5:]
    special = place_of() % (ND // 2) == 0
    blocks = [pl.ds(m * ROWS, ROWS) for m in range(STEPS)]
    sources = {
        "base": (bundle_hbm.at[14], base_ref),
        "cross": (bundle_hbm.at[pl.ds(12, 2)], cross_base_ref),
        "inner": (inner_hbm, inner_ref),
    }
    for r in range(2):
        for ri in range(2):
            sources["filt", r, ri] = (bundle_hbm.at[pl.ds(r * 4 + ri * 2, 2)], filt_ref.at[r, ri])
    sources["filt", 2] = (bundle_hbm.at[pl.ds(8, 4)], other_ref)
    copies = {k: pltpu.make_async_copy(*v, sem.at[i]) for i, (k, v) in enumerate(sources.items())}
    waiting = set(copies)

    def arrive(key):
        for k in list(copies):
            if k in waiting and (k == key or k[:2] == key):
                waiting.remove(k)
                copies[k].wait()

    for copy in copies.values():
        copy.start()
    peak = peak_ref[0:1, 0:1]
    tables = (mf_ref, mi_ref, cross_ref, turn_ref, inner_ref)
    for m in range(STEPS):
        y = decode(y_ref[blocks[m]].astype(f32), peak, FIELD_CODE).reshape(ROWS * 16, F)
        for g in range(2):
            buf[g, pl.ds(m * ROWS * 16, ROWS * 16), :] = y[:, g * 128 : (g + 1) * 128]
    arrive("base")
    arrive("cross")
    for r in range(2):
        fill_tables(r, base_ref, cross_base_ref, wave_ref, *tables[:4])

    def field(r, ri):
        return jnp.concatenate(
            [
                buf[g, pl.ds(h * 8 + r * 4 + c * 2 + ri, ND, stride=16), :]
                for c in range(2)
                for h in range(2)
                for g in range(2)
            ],
            axis=1,
        )

    def put(z, r, ri, part):
        for c in range(2):
            for h in range(2):
                for g in range(2):
                    at = c * 512 + h * 256 + g * 128
                    obuf[g, pl.ds(h * 8 + r * 4 + c * 2 + ri, ND, stride=16), :] = z[
                        part * 128 : (part + 1) * 128, at : at + 128
                    ]

    def filt_of(r):
        return lambda ri, c, odd: filt_ref[r, ri, c, :, odd * 128 : (odd + 1) * 128]

    running = []
    for r in range(2):
        im = field(r, 1)
        if r == 0:
            im = im * jnp.where(special, 0.0, 1.0)
        running.append(transform(field(r, 0), im, r, *tables, filt_of(r), arrive))
    for stage in range(4):
        for r in range(2):
            z = next(running[r])
            if stage == 3:
                put(z, r, 0, 0)
                put(z, r, 1, 1)

    arrive(("filt", 2))

    @pl.when(special)
    def _():
        fill_tables(2, base_ref, cross_base_ref, wave_ref, *tables[:4])
        *_, z = transform(
            field(0, 1),
            None,
            2,
            *tables,
            lambda ri, c, odd: other_ref[ri * 2 + c, :, odd * 128 : (odd + 1) * 128],
            arrive,
        )
        put(z, 0, 1, 0)

    writes = []
    for m in range(STEPS):
        y = jnp.concatenate([obuf[g, pl.ds(m * ROWS * 16, ROWS * 16), :] for g in range(2)], axis=1)
        out_ref[blocks[m]] = encode(y, peak, FILTERED_CODE).reshape(ROWS, 16, F).astype(bf16)
        writes.append(pltpu.make_async_copy(out_ref.at[blocks[m]], out_hbm.at[blocks[m]], sem.at[len(copies) + m]))
        writes[-1].start()
    for copy in writes:
        copy.wait()


def last_kernel(y_ref, table_ref, peak_ref, out_ref, acc, buf):
    peak = peak_ref[0:1, 0:1]
    step = pl.program_id(0)

    y = decode(y_ref[...].astype(f32), peak, FILTERED_CODE)
    t = table_ref[0]
    pair = step // (STEPS // 2)
    first = step % (STEPS // 2) == 0
    for h in range(2):
        hi, lo = split(y[:, h * 8 : h * 8 + 8, :].reshape(ROWS * 8, F))
        res = dot(t, twice(hi, lo, 0))
        acc[pair, h] = jnp.where(first, res, acc[pair, h] + res)

    @pl.when(step == STEPS - 1)
    def _():
        for pair in range(2):
            for h in range(2):
                for c in range(2):
                    for g in range(2):
                        buf[pl.ds(h * 8 + g * 4 + pair * 2 + c, ND, stride=16), :] = acc[
                            pair, h, c * ND : (c + 1) * ND, g * 128 : (g + 1) * 128
                        ]
        out_ref[...] = encode(buf[...], peak, CONV_CODE).reshape(ND, 16, 128).astype(bf16)


def finish_kernel(y_ref, sig_ref, gate_ref, skip_ref, peak_ref, out_ref, buf):
    peak = peak_ref[0:1, 0:1]
    buf[...] = decode(y_ref[...].astype(f32).reshape(ND * 16, 128), peak, CONV_CODE)
    skip = skip_ref[...]
    for q in range(ND):
        at = pl.ds(q * 512, 512)
        conv = jnp.concatenate([buf[pl.ds(q * 16 + i * 4, 4), :] for i in range(4)], axis=1)
        total = conv + skip * sig_ref[:, at].astype(f32)
        out_ref[:, at] = (gate_ref[:, at].astype(f32) * total).astype(bf16)


VMEM = pl.BlockSpec(memory_space=pltpu.VMEM)
ANY = pl.BlockSpec(memory_space=pl.ANY)


def call(kernel, ins, outs, scratch, name, flops=0, limit=16, grid=(), in_specs=None, out_specs=None):
    size = sum(int(np.prod(x.shape)) * x.dtype.itemsize for x in (*ins, *outs))
    return pl.pallas_call(
        kernel,
        grid_spec=pltpu.PrefetchScalarGridSpec(
            num_scalar_prefetch=0,
            grid=grid,
            in_specs=in_specs or [VMEM] * len(ins),
            out_specs=out_specs or [VMEM] * len(outs),
            scratch_shapes=[pltpu.VMEM(s, d) if s else d for s, d in scratch],
        ),
        out_shape=outs,
        compiler_params=pltpu.CompilerParams(vmem_limit_bytes=limit * 2**20),
        cost_estimate=pl.CostEstimate(flops=flops, bytes_accessed=size, transcendentals=0),
        name=name,
    )(*ins)


def exchange(x):
    return lax.all_to_all(x, AXES, split_axis=0, concat_axis=0, tiled=True)


def shape(*dims, dtype=bf16):
    return jax.ShapeDtypeStruct(dims, dtype)


def per_device(signal, gate, skip, spectrum):
    (packed,) = call(pack_kernel, (signal,), [shape(ND, 4, 640)], [], "pack")
    spread = exchange(packed)

    plain, back = order_tables()
    held = [((2, 4, F, F), f32), (None, pltpu.SemaphoreType.DMA((2, 4)))]
    given = []
    for r, orders in enumerate(([back, plain], [back])):
        given += call(
            lambda *refs, r=r: give_kernel(r, *refs),
            (jnp.asarray(np.stack(orders)), spectrum),
            [shape(4, F, F)],
            held,
            "give",
            limit=58,
            flops=2**29,
            in_specs=[VMEM, ANY],
        )
    spread, *_ = lax.optimization_barrier((spread, *given))
    mirror = [(p, (ND // 2 - p) if p % (ND // 2) == 0 else ND - p) for p in range(ND)]
    got = [
        lax.ppermute(given[0], AXES, mirror),
        lax.ppermute(given[1], AXES, [(p, ND - 1 - p) for p in range(ND)]),
    ]

    place = place_of()
    k1 = jnp.stack([place * 2, place * 2 + 1, ND - place * 2])[:, None] % F
    lane = jnp.arange(F, dtype=jnp.int32)
    turns = jnp.stack([k1 * lane % (F * ND) * (F * 2), k1 * lane, (k1 + F * lane) % (F * F) * F], axis=1)
    angle = (2 * np.pi / F**3) * turns.astype(f32)
    wave = jnp.stack([jnp.cos(angle), jnp.sin(angle)], axis=2).reshape(3, 6, F)

    field, peak = call(
        outer_kernel,
        (spread, jnp.asarray(outer_forward_table())),
        [shape(ND, 16, F), shape(8, 128, dtype=f32)],
        [((4, ND * 8, 128), f32), ((ND * 4, 512), bf16)],
        "outer",
        flops=2**29,
        grid=(STEPS,),
        in_specs=[VMEM, pl.BlockSpec((ROWS * 8, 512), lambda i: (i, 0))],
        out_specs=[pl.BlockSpec((ROWS, 16, F), lambda i: (i, 0, 0)), pl.BlockSpec((8, 128), lambda i: (0, 0))],
    )
    field = exchange(field)
    base, cross_base = (jnp.asarray(t) for t in base_tables())
    (bundle,) = call(
        combine_kernel,
        (spectrum, jnp.asarray(plain), cross_base, base, *got),
        [shape(15, F, F, dtype=f32)],
        held,
        "combine",
        limit=58,
        flops=2**34,
        in_specs=[ANY] + [VMEM] * 5,
    )
    (filtered,) = call(
        middle_kernel,
        (field, jnp.asarray(np.stack(inner_tables())), bundle, peak, wave),
        [shape(ND, 16, F)],
        [((2, ND * 16, 128), f32)] * 2
        + [((2, 2, 512, F), bf16), ((F, F), f32), ((2, F, F), f32), ((2, 2, 2, F, F), f32), ((4, F, F), f32)]
        + [((3, 256, 512), bf16)] * 2
        + [((3, 2, F, F), f32), ((3, 2, ND, ND), f32), ((ND, 16, F), bf16)]
        + [(None, pltpu.SemaphoreType.DMA((8 + STEPS,)))],
        "middle",
        flops=4 * 2**30,
        limit=51,
        in_specs=[VMEM, ANY, ANY, VMEM, VMEM],
        out_specs=[ANY],
    )
    filtered = exchange(filtered)
    (conv,) = call(
        last_kernel,
        (filtered, jnp.asarray(outer_inverse_table()), peak),
        [shape(ND, 16, 128)],
        [((2, 2, 2 * ND, F), f32), ((ND * 16, 128), f32)],
        "last",
        flops=2**29,
        grid=(STEPS,),
        in_specs=[
            pl.BlockSpec((ROWS, 16, F), lambda i: (i, 0, 0)),
            pl.BlockSpec((1, 2 * ND, ROWS * 24), lambda i: (i, 0, 0)),
            VMEM,
        ],
        out_specs=[VMEM],
    )
    conv = exchange(conv)
    (mixed,) = call(
        finish_kernel,
        (conv, signal, gate, skip[:, None], peak),
        [shape(4, 65536)],
        [((ND * 16, 128), f32)],
        "finish",
    )
    return mixed


def solution(mesh):
    split_spec = P(None, AXES)
    return jax.shard_map(
        per_device,
        mesh=mesh,
        in_specs=(split_spec, split_spec, P(), P(None, None, AXES, None, None)),
        out_specs=split_spec,
        check_vma=False,
    )
```

```python
import jax
import jax.numpy as jnp
import ml_dtypes
import numpy as np
from jax import lax
from jax.experimental import pallas as pl
from jax.experimental.pallas import tpu as pltpu
from jax.sharding import PartitionSpec as P

F = 256
ND = 128
STEPS = 4
ROWS = ND // STEPS
AXES = ("wide", "narrow")
bf16 = jnp.bfloat16
f32 = jnp.float32

OFFSET = 120.0 * np.log(2.0)
SPAN = 240.0
FIELD_CODE = (2.0**-8, 15.1)
FILTERED_CODE = (2.0**-11, 22.2)
CONV_CODE = (2.0**-7, 21.7)
FILTER_TOP = 6.02


def split_np(x):
    hi = x.astype(ml_dtypes.bfloat16)
    lo = (x - hi.astype(np.float64)).astype(ml_dtypes.bfloat16)
    return hi, lo


def outer_waves():
    k1 = np.arange(F).reshape(ND, 2)
    ang = 2 * np.pi * (k1[:, :, None] * np.arange(ND) % F) / F
    wave = np.stack([np.cos(ang), -np.sin(ang)], axis=2)
    for p in (0, ND // 2):
        wave[p, 0, 1] = np.cos(np.pi * (1 - p // (ND // 2)) * np.arange(ND))
    return wave


def outer_forward_table():
    t = np.zeros((ND, 2, 2, 2, 2, ND))
    for c in range(2):
        t[:, :, c, :, c, :] = outer_waves()
    return np.concatenate(split_np(t.reshape(ND * 8, 2 * ND)), axis=1)


def outer_inverse_table():
    t = np.zeros((2, ND, ND, 2, 2, 2))
    for c in range(2):
        t[c, :, :, :, c, :] = outer_waves().transpose(3, 0, 1, 2)
    hi, lo = (x.reshape(2 * ND, STEPS, -1) for x in split_np(t.reshape(2 * ND, ND * 8)))
    return np.ascontiguousarray(np.concatenate([hi, hi, lo], axis=2).transpose(1, 0, 2))


def inner_tables():
    low = np.arange(ND)
    out = []
    for odd in range(2):
        ang = 2 * np.pi * (low[:, None] * (2 * low[None] + odd) % F) / F
        c, s = np.cos(ang), np.sin(ang)
        fwd = split_np(np.block([[c, -s], [s, c]]))
        inv = split_np(np.block([[c.T, s.T], [-s.T, c.T]]) / F)
        out.append([np.concatenate(x, axis=0) for x in (fwd, inv)])
    return np.stack([out[0][0], out[1][0]]), np.stack([out[0][1], out[1][1]])


def order_tables():
    eye = np.eye(F)
    even_odd = np.concatenate([np.arange(0, F, 2), np.arange(1, F, 2)])
    plain = np.stack([eye, eye[:, even_odd]])
    back = np.stack([eye[::-1], eye[:, 255 - even_odd]])
    return plain.astype(ml_dtypes.bfloat16), back.astype(ml_dtypes.bfloat16)


def base_tables():
    i = np.arange(F)
    half = np.arange(ND)
    a0 = 2 * np.pi * (half[:, None] * half[None] % ND) / ND
    a1 = 2 * np.pi * (i[:, None] * i[None]) / (F * F)
    return (
        np.stack([np.cos(a0), np.sin(a0)]).astype(np.float32),
        np.stack([np.cos(a1), np.sin(a1)]).astype(np.float32),
    )


def peak_of(peak_ref):
    return jnp.maximum(jnp.max(peak_ref[...], keepdims=True), 1e-30)


def encode(x, peak, code):
    knee, octaves = code
    beta = SPAN / octaves
    z = jnp.abs(x) * (1.0 / (peak * knee))
    y = jnp.exp(jnp.minimum(beta * jnp.log(1.0 + z) - OFFSET, OFFSET))
    return jnp.where(x < 0, -y, y)


def decode(y, peak, code):
    knee, octaves = code
    beta = SPAN / octaves
    z = jnp.exp(jnp.log(jnp.abs(y)) * (1.0 / beta) + OFFSET / beta) - 1.0
    z = z * (peak * knee)
    return jnp.where(y < 0, -z, z)


def encode_filter(x):
    y = jnp.exp(jnp.abs(x) * (SPAN * np.log(2.0) / FILTER_TOP) - OFFSET)
    return jnp.where(x < 0, -y, y)


def decode_filter(y):
    z = (jnp.log(jnp.abs(y)) + OFFSET) * (FILTER_TOP / (SPAN * np.log(2.0)))
    return jnp.where(y < 0, -z, z)


def split(x):
    hi = x.astype(bf16)
    return hi, (x - hi.astype(f32)).astype(bf16)


def dot(a, b):
    return jnp.dot(a, b, preferred_element_type=f32)


def twice(hi, lo, axis):
    return jnp.concatenate([hi, lo, hi], axis=axis)


def wide_table(t, axis):
    hi, lo = jnp.split(t, 2, axis=axis)
    return jnp.concatenate([hi, hi, lo], axis=axis)


def block(m):
    return pl.ds(m * ROWS, ROWS)


def send_block(out_ref, out_hbm, sem, m):
    copy = pltpu.make_async_copy(out_ref.at[block(m)], out_hbm.at[block(m)], sem.at[m])
    copy.start()
    return copy


def pack_kernel(sig_hbm, out_hbm, held, out_ref, sem):
    reads = []
    for m in range(STEPS):
        at = pl.ds(m * ROWS * 512, ROWS * 512)
        reads.append(pltpu.make_async_copy(sig_hbm.at[:, at], held.at[:, at], sem.at[m]))
        reads[-1].start()
    writes = []
    top = jnp.zeros((4, 128), f32)
    for m in range(STEPS):
        reads[m].wait()
        for q in range(m * ROWS, (m + 1) * ROWS):
            x = held[:, pl.ds(q * 512, 512)]
            out_ref[q, :, pl.ds(0, 512)] = x
            x = jnp.abs(x.astype(f32))
            for i in range(4):
                top = jnp.maximum(top, x[:, i * 128 : (i + 1) * 128])
        at = (block(m), slice(None), pl.ds(0, 512))
        writes.append(pltpu.make_async_copy(out_ref.at[at], out_hbm.at[at], sem.at[STEPS + m]))
        writes[-1].start()
    top = top.astype(bf16)
    for q in range(ND):
        out_ref[q, :, pl.ds(512, 128)] = top
    at = (slice(None), slice(None), pl.ds(512, 128))
    writes.append(pltpu.make_async_copy(out_ref.at[at], out_hbm.at[at], sem.at[2 * STEPS]))
    writes[-1].start()
    for copy in writes:
        copy.wait()


def outer_kernel(x_ref, table_ref, out_hbm, peak_ref, buf, out_ref, sem):
    top = jnp.zeros((4, 128), f32)
    for n in range(ND):
        x = x_ref[n].astype(f32)
        top = jnp.maximum(top, x[:, 512:640])
        for i in range(4):
            buf[i, pl.ds(n * 8, 4), :] = x[:, i * 128 : (i + 1) * 128]
    peak = jnp.maximum(jnp.max(top, keepdims=True), 1e-30)
    peak_ref[...] = jnp.broadcast_to(peak, (8, 128))
    writes = []
    for pair in range(2):
        rows = []
        for c in range(2):
            parts = [buf[i, pl.ds(pair * 2 + c, ND, stride=8), :] for i in range(4)]
            rows.append(jnp.concatenate(parts, axis=1).astype(bf16))
        x = jnp.concatenate(rows + rows, axis=0)
        for m in range(pair * STEPS // 2, (pair + 1) * STEPS // 2):
            res = encode(dot(table_ref[pl.ds(m * ROWS * 8, ROWS * 8), :], x), peak, FIELD_CODE)
            parts = [res[:, h * F : (h + 1) * F].reshape(ROWS, 8, F) for h in range(2)]
            out_ref[block(m)] = jnp.concatenate(parts, axis=1).astype(bf16)
            writes.append(send_block(out_ref, out_hbm, sem, m))
    for copy in writes:
        copy.wait()


def fill_tables(table, base_ref, cross_base_ref, wave_ref, mf_ref, mi_ref, cross_ref, turn_ref):
    def wave(row, lanes):
        return wave_ref[table, row : row + 1, 0:lanes]

    cb, sb = wave(0, ND), wave(1, ND)
    c0, s0 = base_ref[0:128, 0:128], base_ref[128:256, 0:128]
    c, s = c0 * cb - s0 * sb, s0 * cb + c0 * sb
    for out_ref, c, s in ((mf_ref, c, s), (mi_ref, c.T * (1.0 / F), s.T * (-1.0 / F))):
        (ch, cl), (sh, sl) = split(c), split(s)
        for part, (cc, ss) in enumerate(((ch, sh), (cl, sl))):
            at = part * 256
            out_ref[table, 0:128, at : at + 128] = cc
            out_ref[table, 0:128, at + 128 : at + 256] = ss
            out_ref[table, 128:256, at : at + 128] = -ss
            out_ref[table, 128:256, at + 128 : at + 256] = cc
    cb, sb = wave(2, F), wave(3, F)
    c1, s1 = cross_base_ref[0], cross_base_ref[1]
    cross_ref[table, 0] = c1 * cb - s1 * sb
    cross_ref[table, 1] = s1 * cb + c1 * sb
    for i in range(2):
        turn_ref[table, i] = jnp.broadcast_to(wave(4 + i, ND), (ND, ND)).T


def place_of():
    return lax.axis_index("wide") * lax.axis_size("narrow") + lax.axis_index("narrow")


def fetch_filter(slot, r, pair, filt_hbm, held, sem):
    copies = []
    for i in range(4):
        source = filt_hbm.at[i // 2, pair * 2 + i % 2, r]
        copies.append(pltpu.make_async_copy(source, held.at[slot, i], sem.at[slot, i]))
        copies[-1].start()
    return copies


def give_kernel(r, order_hbm, filt_hbm, out_hbm, held, order_ref, out_ref, sem, more):
    place = place_of()
    kind = jnp.where(place == 0, 1, 0) if r == 0 else 0
    order = pltpu.make_async_copy(order_hbm.at[kind], order_ref, more.at[4])
    order.start()
    copies = fetch_filter(0, r, 1 - place // (ND // 2), filt_hbm, held, sem)
    sign = (2 * kind - 1) * jnp.float32(1.0)
    order.wait()
    for copy in copies:
        copy.wait()
    left, right = order_ref[0], order_ref[1]
    writes = []
    for i in range(4):
        hi, lo = split(held[0, i])
        hi, lo = split(dot(hi, right) + dot(lo, right))
        x = dot(left, hi) + dot(left, lo)
        if i >= 2:
            x = x * sign
        out_ref[i] = encode_filter(x).astype(bf16)
        writes.append(pltpu.make_async_copy(out_ref.at[i], out_hbm.at[i], more.at[i]))
        writes[-1].start()
    for copy in writes:
        copy.wait()


def combine_kernel(filt_hbm, order_ref, cross_base_ref, base_ref, got0_ref, got1_ref, out_ref, held, sem):
    place = place_of()
    copies = [fetch_filter(r, r, place // (ND // 2), filt_hbm, held, sem) for r in range(2)]
    generic = jnp.where(place % (ND // 2) == 0, 0.0, 1.0)
    out_ref[12:14] = cross_base_ref[...]
    out_ref[14, 0:128, 0:128] = base_ref[0]
    out_ref[14, 128:256, 0:128] = base_ref[1]
    out_ref[14, :, 128:256] = jnp.zeros((F, 128), f32)
    for copy in (*copies[0], *copies[1]):
        copy.wait()
    for r, got_ref in enumerate((got0_ref, got1_ref)):
        for i in range(4):
            got = decode_filter(got_ref[i].astype(f32))
            if r == 0:
                out_ref[8 + i] = got
                got = got * generic
            hi, lo = split(held[r, i])
            out_ref[r * 4 + i] = dot(hi, order_ref[1]) + dot(lo, order_ref[1]) + got


def transform(re, im, table, mf_ref, mi_ref, cross_ref, turn_ref, inner_ref, filt, arrive):
    tc, ts = (jnp.concatenate([turn_ref[table, i]] * 2, axis=1) for i in range(2))
    if im is None:
        hi, lo = split(re)
        t = jnp.concatenate([mf_ref[table, :, 0:128], mf_ref[table, :, 256:384]], axis=1)
    else:
        hi, lo = split(jnp.concatenate([re, im], axis=0))
        t = mf_ref[table]
    z = dot(wide_table(t, 1), twice(hi, lo, 0))
    yield
    sums, diffs = [], []
    for c in range(2):
        at = c * 512
        dr, di = z[:128, at : at + 256], z[128:, at : at + 256]
        er, ei = z[:128, at + 256 : at + 512], z[128:, at + 256 : at + 512]
        pr, pi = er * tc + ei * ts, ei * tc - er * ts
        for zr, zi, e in ((dr + pr, di + pi, 0), (dr - pr, di - pi, 128)):
            cosine, sine = cross_ref[table, 0, e : e + 128], cross_ref[table, 1, e : e + 128]
            zr, zi = zr * cosine + zi * sine, zi * cosine - zr * sine
            sums.append(jnp.concatenate([zr[:, :128] + zr[:, 128:], zi[:, :128] + zi[:, 128:]], axis=1))
            diffs.append(jnp.concatenate([zr[:, :128] - zr[:, 128:], zi[:, :128] - zi[:, 128:]], axis=1))
    arrive("inner")
    spectra = []
    for odd, rows in enumerate((sums, diffs)):
        hi, lo = split(jnp.concatenate(rows, axis=0))
        spectra.append(dot(twice(hi, lo, 1), wide_table(inner_ref[0, odd], 0)))
    yield
    arrive(("filt", table))
    back = []
    for odd, z in enumerate(spectra):
        rows = []
        for c in range(2):
            zr, zi = z[c * F : (c + 1) * F, :128], z[c * F : (c + 1) * F, 128:]
            fr, fi = filt(0, c, odd), filt(1, c, odd)
            rows.append(jnp.concatenate([zr * fr - zi * fi, zi * fr + zr * fi], axis=1))
        hi, lo = split(jnp.concatenate(rows, axis=0))
        back.append(dot(twice(hi, lo, 1), wide_table(inner_ref[1, odd], 0)))
    yield
    even, odd = back
    tops, bottoms = [], []
    for c in range(2):
        both = []
        for e in (0, 128):
            at = c * F + e
            er, ei = even[at : at + 128, :128], even[at : at + 128, 128:]
            dr, di = odd[at : at + 128, :128], odd[at : at + 128, 128:]
            zr = jnp.concatenate([er + dr, er - dr], axis=1)
            zi = jnp.concatenate([ei + di, ei - di], axis=1)
            cosine = cross_ref[table, 0, e : e + 128] * (1.0 / F)
            sine = cross_ref[table, 1, e : e + 128] * (1.0 / F)
            both.append((zr * cosine - zi * sine, zi * cosine + zr * sine))
        (ar, ai), (br, bi) = both
        ur, ui = ar - br, ai - bi
        tops += [ar + br, ur * tc - ui * ts]
        bottoms += [ai + bi, ui * tc + ur * ts]
    hi, lo = split(jnp.concatenate([jnp.concatenate(tops, axis=1), jnp.concatenate(bottoms, axis=1)], axis=0))
    t = mi_ref[table] if im is not None else mi_ref[table, 0:128]
    yield dot(wide_table(t, 1), twice(hi, lo, 0))


def middle_kernel(y_ref, inner_hbm, bundle_hbm, peak_ref, wave_ref, out_hbm, buf, obuf, *held):
    inner_ref, base_ref, cross_base_ref, filt_ref, other_ref = held[:5]
    mf_ref, mi_ref, cross_ref, turn_ref, out_ref, sem = held[5:]
    special = place_of() % (ND // 2) == 0
    blocks = [pl.ds(m * ROWS, ROWS) for m in range(STEPS)]
    sources = {
        "base": (bundle_hbm.at[14], base_ref),
        "cross": (bundle_hbm.at[pl.ds(12, 2)], cross_base_ref),
        "inner": (inner_hbm, inner_ref),
    }
    for r in range(2):
        for ri in range(2):
            sources["filt", r, ri] = (bundle_hbm.at[pl.ds(r * 4 + ri * 2, 2)], filt_ref.at[r, ri])
    sources["filt", 2] = (bundle_hbm.at[pl.ds(8, 4)], other_ref)
    copies = {k: pltpu.make_async_copy(*v, sem.at[i]) for i, (k, v) in enumerate(sources.items())}
    waiting = set(copies)

    def arrive(key):
        for k in list(copies):
            if k in waiting and (k == key or k[:2] == key):
                waiting.remove(k)
                copies[k].wait()

    for copy in copies.values():
        copy.start()
    peak = peak_ref[0:1, 0:1]
    tables = (mf_ref, mi_ref, cross_ref, turn_ref, inner_ref)
    for m in range(STEPS):
        y = decode(y_ref[blocks[m]].astype(f32), peak, FIELD_CODE).reshape(ROWS * 16, F)
        for g in range(2):
            buf[g, pl.ds(m * ROWS * 16, ROWS * 16), :] = y[:, g * 128 : (g + 1) * 128]
    arrive("base")
    arrive("cross")
    for r in range(2):
        fill_tables(r, base_ref, cross_base_ref, wave_ref, *tables[:4])

    def field(r, ri):
        return jnp.concatenate(
            [
                buf[g, pl.ds(h * 8 + r * 4 + c * 2 + ri, ND, stride=16), :]
                for c in range(2)
                for h in range(2)
                for g in range(2)
            ],
            axis=1,
        )

    def put(z, r, ri, part):
        for c in range(2):
            for h in range(2):
                for g in range(2):
                    at = c * 512 + h * 256 + g * 128
                    obuf[g, pl.ds(h * 8 + r * 4 + c * 2 + ri, ND, stride=16), :] = z[
                        part * 128 : (part + 1) * 128, at : at + 128
                    ]

    def filt_of(r):
        return lambda ri, c, odd: filt_ref[r, ri, c, :, odd * 128 : (odd + 1) * 128]

    running = []
    for r in range(2):
        im = field(r, 1)
        if r == 0:
            im = im * jnp.where(special, 0.0, 1.0)
        running.append(transform(field(r, 0), im, r, *tables, filt_of(r), arrive))
    for stage in range(4):
        for r in range(2):
            z = next(running[r])
            if stage == 3:
                put(z, r, 0, 0)
                put(z, r, 1, 1)

    arrive(("filt", 2))

    @pl.when(special)
    def _():
        fill_tables(2, base_ref, cross_base_ref, wave_ref, *tables[:4])
        *_, z = transform(
            field(0, 1),
            None,
            2,
            *tables,
            lambda ri, c, odd: other_ref[ri * 2 + c, :, odd * 128 : (odd + 1) * 128],
            arrive,
        )
        put(z, 0, 1, 0)

    writes = []
    for m in range(STEPS):
        y = jnp.concatenate([obuf[g, pl.ds(m * ROWS * 16, ROWS * 16), :] for g in range(2)], axis=1)
        out_ref[blocks[m]] = encode(y, peak, FILTERED_CODE).reshape(ROWS, 16, F).astype(bf16)
        writes.append(pltpu.make_async_copy(out_ref.at[blocks[m]], out_hbm.at[blocks[m]], sem.at[len(copies) + m]))
        writes[-1].start()
    for copy in writes:
        copy.wait()


def last_kernel(y_ref, table_ref, peak_ref, out_hbm, buf, out_ref, sem):
    peak = peak_ref[0:1, 0:1]
    for pair in range(2):
        acc = [None, None]
        for step in range(pair * STEPS // 2, (pair + 1) * STEPS // 2):
            y = decode(y_ref[block(step)].astype(f32), peak, FILTERED_CODE)
            for h in range(2):
                hi, lo = split(y[:, h * 8 : h * 8 + 8, :].reshape(ROWS * 8, F))
                res = dot(table_ref[step], twice(hi, lo, 0))
                acc[h] = res if acc[h] is None else acc[h] + res
        for h in range(2):
            for c in range(2):
                for g in range(2):
                    buf[pl.ds(h * 8 + g * 4 + pair * 2 + c, ND, stride=16), :] = acc[h][
                        c * ND : (c + 1) * ND, g * 128 : (g + 1) * 128
                    ]
    writes = []
    for m in range(STEPS):
        y = encode(buf[pl.ds(m * ROWS * 16, ROWS * 16), :], peak, CONV_CODE)
        out_ref[block(m)] = y.reshape(ROWS, 16, 128).astype(bf16)
        writes.append(send_block(out_ref, out_hbm, sem, m))
    for copy in writes:
        copy.wait()


def finish_kernel(y_ref, sig_ref, gate_ref, skip_ref, peak_ref, out_ref, buf):
    peak = peak_ref[0:1, 0:1]
    buf[...] = decode(y_ref[...].astype(f32).reshape(ND * 16, 128), peak, CONV_CODE)
    skip = skip_ref[...]
    for q in range(ND):
        at = pl.ds(q * 512, 512)
        conv = jnp.concatenate([buf[pl.ds(q * 16 + i * 4, 4), :] for i in range(4)], axis=1)
        total = conv + skip * sig_ref[:, at].astype(f32)
        out_ref[:, at] = (gate_ref[:, at].astype(f32) * total).astype(bf16)


VMEM = pl.BlockSpec(memory_space=pltpu.VMEM)
ANY = pl.BlockSpec(memory_space=pl.ANY)


def call(kernel, ins, outs, scratch, name, flops=0, limit=16, grid=(), in_specs=None, out_specs=None):
    size = sum(int(np.prod(x.shape)) * x.dtype.itemsize for x in (*ins, *outs))
    return pl.pallas_call(
        kernel,
        grid_spec=pltpu.PrefetchScalarGridSpec(
            num_scalar_prefetch=0,
            grid=grid,
            in_specs=in_specs or [VMEM] * len(ins),
            out_specs=out_specs or [VMEM] * len(outs),
            scratch_shapes=[pltpu.VMEM(s, d) if s else d for s, d in scratch],
        ),
        out_shape=outs,
        compiler_params=pltpu.CompilerParams(vmem_limit_bytes=limit * 2**20),
        cost_estimate=pl.CostEstimate(flops=flops, bytes_accessed=size, transcendentals=0),
        name=name,
    )(*ins)


def exchange(x):
    return lax.all_to_all(x, AXES, split_axis=0, concat_axis=0, tiled=True)


def shape(*dims, dtype=bf16):
    return jax.ShapeDtypeStruct(dims, dtype)


def per_device(signal, gate, skip, spectrum):
    (packed,) = call(
        pack_kernel,
        (signal,),
        [shape(ND, 4, 640)],
        [(signal.shape, bf16), ((ND, 4, 640), bf16), (None, pltpu.SemaphoreType.DMA((2 * STEPS + 1,)))],
        "pack",
        limit=58,
        in_specs=[ANY],
        out_specs=[ANY],
    )
    spread = exchange(packed)

    plain, back = order_tables()
    held = [((2, 4, F, F), f32), (None, pltpu.SemaphoreType.DMA((2, 4)))]
    given = []
    for r, orders in enumerate(([back, plain], [back])):
        given += call(
            lambda *refs, r=r: give_kernel(r, *refs),
            (jnp.asarray(np.stack(orders)), spectrum),
            [shape(4, F, F)],
            [((1, 4, F, F), f32), ((2, F, F), bf16), ((4, F, F), bf16)]
            + [(None, pltpu.SemaphoreType.DMA((1, 4))), (None, pltpu.SemaphoreType.DMA((5,)))],
            "give",
            limit=58,
            flops=2**29,
            in_specs=[ANY, ANY],
            out_specs=[ANY],
        )
    spread, *_ = lax.optimization_barrier((spread, *given))
    mirror = [(p, (ND // 2 - p) if p % (ND // 2) == 0 else ND - p) for p in range(ND)]
    got = [
        lax.ppermute(given[0], AXES, mirror),
        lax.ppermute(given[1], AXES, [(p, ND - 1 - p) for p in range(ND)]),
    ]

    place = place_of()
    k1 = jnp.stack([place * 2, place * 2 + 1, ND - place * 2])[:, None] % F
    lane = jnp.arange(F, dtype=jnp.int32)
    turns = jnp.stack([k1 * lane % (F * ND) * (F * 2), k1 * lane, (k1 + F * lane) % (F * F) * F], axis=1)
    angle = (2 * np.pi / F**3) * turns.astype(f32)
    wave = jnp.stack([jnp.cos(angle), jnp.sin(angle)], axis=2).reshape(3, 6, F)

    field, peak = call(
        outer_kernel,
        (spread, jnp.asarray(outer_forward_table())),
        [shape(ND, 16, F), shape(8, 128, dtype=f32)],
        [((4, ND * 8, 128), f32), ((ND, 16, F), bf16), (None, pltpu.SemaphoreType.DMA((STEPS,)))],
        "outer",
        flops=2**29,
        out_specs=[ANY, VMEM],
    )
    field = exchange(field)
    base, cross_base = (jnp.asarray(t) for t in base_tables())
    (bundle,) = call(
        combine_kernel,
        (spectrum, jnp.asarray(plain), cross_base, base, *got),
        [shape(15, F, F, dtype=f32)],
        held,
        "combine",
        limit=58,
        flops=2**34,
        in_specs=[ANY] + [VMEM] * 5,
    )
    (filtered,) = call(
        middle_kernel,
        (field, jnp.asarray(np.stack(inner_tables())), bundle, peak, wave),
        [shape(ND, 16, F)],
        [((2, ND * 16, 128), f32)] * 2
        + [((2, 2, 512, F), bf16), ((F, F), f32), ((2, F, F), f32), ((2, 2, 2, F, F), f32), ((4, F, F), f32)]
        + [((3, 256, 512), bf16)] * 2
        + [((3, 2, F, F), f32), ((3, 2, ND, ND), f32), ((ND, 16, F), bf16)]
        + [(None, pltpu.SemaphoreType.DMA((8 + STEPS,)))],
        "middle",
        flops=4 * 2**30,
        limit=51,
        in_specs=[VMEM, ANY, ANY, VMEM, VMEM],
        out_specs=[ANY],
    )
    filtered = exchange(filtered)
    (conv,) = call(
        last_kernel,
        (filtered, jnp.asarray(outer_inverse_table()), peak),
        [shape(ND, 16, 128)],
        [((ND * 16, 128), f32), ((ND, 16, 128), bf16), (None, pltpu.SemaphoreType.DMA((STEPS,)))],
        "last",
        flops=2**29,
        out_specs=[ANY],
    )
    conv = exchange(conv)
    (mixed,) = call(
        finish_kernel,
        (conv, signal, gate, skip[:, None], peak),
        [shape(4, 65536)],
        [((ND * 16, 128), f32)],
        "finish",
    )
    return mixed


def solution(mesh):
    split_spec = P(None, AXES)
    return jax.shard_map(
        per_device,
        mesh=mesh,
        in_specs=(split_spec, split_spec, P(), P(None, None, AXES, None, None)),
        out_specs=split_spec,
        check_vma=False,
    )
```

```python
import jax
import jax.numpy as jnp
import ml_dtypes
import numpy as np
from jax import lax
from jax.experimental import pallas as pl
from jax.experimental.pallas import tpu as pltpu
from jax.sharding import PartitionSpec as P

F = 256
ND = 128
STEPS = 4
ROWS = ND // STEPS
AXES = ("wide", "narrow")
bf16 = jnp.bfloat16
f32 = jnp.float32

OFFSET = 120.0 * np.log(2.0)
SPAN = 240.0
FIELD_CODE = (2.0**-8, 15.1)
FILTERED_CODE = (2.0**-11, 22.2)
CONV_CODE = (2.0**-7, 21.7)
FILTER_TOP = 6.02


def split_np(x):
    hi = x.astype(ml_dtypes.bfloat16)
    lo = (x - hi.astype(np.float64)).astype(ml_dtypes.bfloat16)
    return hi, lo


def outer_waves():
    k1 = np.arange(F).reshape(ND, 2)
    ang = 2 * np.pi * (k1[:, :, None] * np.arange(ND) % F) / F
    wave = np.stack([np.cos(ang), -np.sin(ang)], axis=2)
    for p in (0, ND // 2):
        wave[p, 0, 1] = np.cos(np.pi * (1 - p // (ND // 2)) * np.arange(ND))
    return wave


def outer_forward_table():
    t = np.zeros((ND, 2, 2, 2, 2, ND))
    for c in range(2):
        t[:, :, c, :, c, :] = outer_waves()
    return np.concatenate(split_np(t.reshape(ND * 8, 2 * ND)), axis=1)


def outer_inverse_table():
    t = np.zeros((2, ND, ND, 2, 2, 2))
    for c in range(2):
        t[c, :, :, :, c, :] = outer_waves().transpose(3, 0, 1, 2)
    hi, lo = (x.reshape(2 * ND, STEPS, -1) for x in split_np(t.reshape(2 * ND, ND * 8)))
    return np.ascontiguousarray(np.concatenate([hi, hi, lo], axis=2).transpose(1, 0, 2))


def inner_tables():
    low = np.arange(ND)
    out = []
    for odd in range(2):
        ang = 2 * np.pi * (low[:, None] * (2 * low[None] + odd) % F) / F
        c, s = np.cos(ang), np.sin(ang)
        fwd = split_np(np.block([[c, -s], [s, c]]))
        inv = split_np(np.block([[c.T, s.T], [-s.T, c.T]]) / F)
        out.append([np.concatenate(x, axis=0) for x in (fwd, inv)])
    return np.stack([out[0][0], out[1][0]]), np.stack([out[0][1], out[1][1]])


def order_tables():
    eye = np.eye(F)
    even_odd = np.concatenate([np.arange(0, F, 2), np.arange(1, F, 2)])
    plain = np.stack([eye, eye[:, even_odd]])
    back = np.stack([eye[::-1], eye[:, 255 - even_odd]])
    return plain.astype(ml_dtypes.bfloat16), back.astype(ml_dtypes.bfloat16)


def base_tables():
    i = np.arange(F)
    half = np.arange(ND)
    a0 = 2 * np.pi * (half[:, None] * half[None] % ND) / ND
    a1 = 2 * np.pi * (i[:, None] * i[None]) / (F * F)
    return (
        np.stack([np.cos(a0), np.sin(a0)]).astype(np.float32),
        np.stack([np.cos(a1), np.sin(a1)]).astype(np.float32),
    )


def peak_of(peak_ref):
    return jnp.maximum(jnp.max(peak_ref[...], keepdims=True), 1e-30)


def encode(x, peak, code):
    knee, octaves = code
    beta = SPAN / octaves
    z = jnp.abs(x) * (1.0 / (peak * knee))
    y = jnp.exp(jnp.minimum(beta * jnp.log(1.0 + z) - OFFSET, OFFSET))
    return jnp.where(x < 0, -y, y)


def decode(y, peak, code):
    knee, octaves = code
    beta = SPAN / octaves
    z = jnp.exp(jnp.log(jnp.abs(y)) * (1.0 / beta) + OFFSET / beta) - 1.0
    z = z * (peak * knee)
    return jnp.where(y < 0, -z, z)


def encode_filter(x):
    y = jnp.exp(jnp.abs(x) * (SPAN * np.log(2.0) / FILTER_TOP) - OFFSET)
    return jnp.where(x < 0, -y, y)


def decode_filter(y):
    z = (jnp.log(jnp.abs(y)) + OFFSET) * (FILTER_TOP / (SPAN * np.log(2.0)))
    return jnp.where(y < 0, -z, z)


def split(x):
    hi = x.astype(bf16)
    return hi, (x - hi.astype(f32)).astype(bf16)


def dot(a, b):
    return jnp.dot(a, b, preferred_element_type=f32)


def twice(hi, lo, axis):
    return jnp.concatenate([hi, lo, hi], axis=axis)


def wide_table(t, axis):
    hi, lo = jnp.split(t, 2, axis=axis)
    return jnp.concatenate([hi, hi, lo], axis=axis)


def block(m):
    return pl.ds(m * ROWS, ROWS)


def send_block(out_ref, out_hbm, sem, m):
    copy = pltpu.make_async_copy(out_ref.at[block(m)], out_hbm.at[block(m)], sem.at[m])
    copy.start()
    return copy


def pack_kernel(sig_hbm, out_hbm, held, out_ref, sem):
    reads = []
    for m in range(STEPS):
        at = pl.ds(m * ROWS * 512, ROWS * 512)
        reads.append(pltpu.make_async_copy(sig_hbm.at[:, at], held.at[:, at], sem.at[m]))
        reads[-1].start()
    writes = []
    top = jnp.zeros((4, 128), f32)
    for m in range(STEPS):
        reads[m].wait()
        for q in range(m * ROWS, (m + 1) * ROWS):
            x = held[:, pl.ds(q * 512, 512)]
            out_ref[q, :, pl.ds(0, 512)] = x
            x = jnp.abs(x.astype(f32))
            for i in range(4):
                top = jnp.maximum(top, x[:, i * 128 : (i + 1) * 128])
        at = (block(m), slice(None), pl.ds(0, 512))
        writes.append(pltpu.make_async_copy(out_ref.at[at], out_hbm.at[at], sem.at[STEPS + m]))
        writes[-1].start()
    top = top.astype(bf16)
    for q in range(ND):
        out_ref[q, :, pl.ds(512, 128)] = top
    at = (slice(None), slice(None), pl.ds(512, 128))
    writes.append(pltpu.make_async_copy(out_ref.at[at], out_hbm.at[at], sem.at[2 * STEPS]))
    writes[-1].start()
    for copy in writes:
        copy.wait()


def outer_kernel(x_ref, table_ref, out_hbm, peak_ref, buf, out_ref, sem):
    top = jnp.zeros((4, 128), f32)
    for n in range(ND):
        x = x_ref[n].astype(f32)
        top = jnp.maximum(top, x[:, 512:640])
        for i in range(4):
            buf[i, pl.ds(n * 8, 4), :] = x[:, i * 128 : (i + 1) * 128]
    peak = jnp.maximum(jnp.max(top, keepdims=True), 1e-30)
    peak_ref[...] = jnp.broadcast_to(peak, (8, 128))
    writes = []
    for pair in range(2):
        rows = []
        for c in range(2):
            parts = [buf[i, pl.ds(pair * 2 + c, ND, stride=8), :] for i in range(4)]
            rows.append(jnp.concatenate(parts, axis=1).astype(bf16))
        x = jnp.concatenate(rows + rows, axis=0)
        for m in range(pair * STEPS // 2, (pair + 1) * STEPS // 2):
            res = encode(dot(table_ref[pl.ds(m * ROWS * 8, ROWS * 8), :], x), peak, FIELD_CODE)
            parts = [res[:, h * F : (h + 1) * F].reshape(ROWS, 8, F) for h in range(2)]
            out_ref[block(m)] = jnp.concatenate(parts, axis=1).astype(bf16)
            writes.append(send_block(out_ref, out_hbm, sem, m))
    for copy in writes:
        copy.wait()


def fill_tables(table, base_ref, cross_base_ref, wave_ref, mf_ref, mi_ref, cross_ref, turn_ref):
    def wave(row, lanes):
        return wave_ref[table, row : row + 1, 0:lanes]

    cb, sb = wave(0, ND), wave(1, ND)
    c0, s0 = base_ref[0:128, 0:128], base_ref[128:256, 0:128]
    c, s = c0 * cb - s0 * sb, s0 * cb + c0 * sb
    for out_ref, c, s in ((mf_ref, c, s), (mi_ref, c.T * (1.0 / F), s.T * (-1.0 / F))):
        (ch, cl), (sh, sl) = split(c), split(s)
        for part, (cc, ss) in enumerate(((ch, sh), (cl, sl))):
            at = part * 256
            out_ref[table, 0:128, at : at + 128] = cc
            out_ref[table, 0:128, at + 128 : at + 256] = ss
            out_ref[table, 128:256, at : at + 128] = -ss
            out_ref[table, 128:256, at + 128 : at + 256] = cc
    cb, sb = wave(2, F), wave(3, F)
    c1, s1 = cross_base_ref[0], cross_base_ref[1]
    cross_ref[table, 0] = c1 * cb - s1 * sb
    cross_ref[table, 1] = s1 * cb + c1 * sb
    for i in range(2):
        turn_ref[table, i] = jnp.broadcast_to(wave(4 + i, ND), (ND, ND)).T


def place_of():
    return lax.axis_index("wide") * lax.axis_size("narrow") + lax.axis_index("narrow")


def fetch_filter(slot, r, pair, filt_hbm, held, sem):
    copies = []
    for i in range(4):
        source = filt_hbm.at[i // 2, pair * 2 + i % 2, r]
        copies.append(pltpu.make_async_copy(source, held.at[slot, i], sem.at[slot, i]))
        copies[-1].start()
    return copies


def give_kernel(r, order_hbm, filt_hbm, out_hbm, held, order_ref, out_ref, sem, more):
    place = place_of()
    kind = jnp.where(place == 0, 1, 0) if r == 0 else 0
    order = pltpu.make_async_copy(order_hbm.at[kind], order_ref, more.at[4])
    order.start()
    copies = fetch_filter(0, r, 1 - place // (ND // 2), filt_hbm, held, sem)
    sign = (2 * kind - 1) * jnp.float32(1.0)
    order.wait()
    for copy in copies:
        copy.wait()
    left, right = order_ref[0], order_ref[1]
    writes = []
    for i in range(4):
        hi, lo = split(held[0, i])
        hi, lo = split(dot(hi, right) + dot(lo, right))
        x = dot(left, hi) + dot(left, lo)
        if i >= 2:
            x = x * sign
        out_ref[i] = encode_filter(x).astype(bf16)
        writes.append(pltpu.make_async_copy(out_ref.at[i], out_hbm.at[i], more.at[i]))
        writes[-1].start()
    for copy in writes:
        copy.wait()


def combine_kernel(filt_hbm, order_ref, cross_base_ref, base_ref, got0_ref, got1_ref, out_hbm, held, out_ref, sem, out_sem):
    place = place_of()
    copies = [fetch_filter(r, r, place // (ND // 2), filt_hbm, held, sem) for r in range(2)]
    generic = jnp.where(place % (ND // 2) == 0, 0.0, 1.0)
    out_ref[12:14] = cross_base_ref[...]
    out_ref[14, 0:128, 0:128] = base_ref[0]
    out_ref[14, 128:256, 0:128] = base_ref[1]
    out_ref[14, :, 128:256] = jnp.zeros((F, 128), f32)
    writes = []

    def write(i):
        writes.append(pltpu.make_async_copy(out_ref.at[i], out_hbm.at[i], out_sem.at[i]))
        writes[-1].start()

    for i in (12, 13, 14):
        write(i)
    for copy in (*copies[0], *copies[1]):
        copy.wait()
    for r, got_ref in enumerate((got0_ref, got1_ref)):
        for i in range(4):
            got = decode_filter(got_ref[i].astype(f32))
            if r == 0:
                out_ref[8 + i] = got
                write(8 + i)
                got = got * generic
            hi, lo = split(held[r, i])
            out_ref[r * 4 + i] = dot(hi, order_ref[1]) + dot(lo, order_ref[1]) + got
            write(r * 4 + i)
    for copy in writes:
        copy.wait()


def transform(re, im, table, mf_ref, mi_ref, cross_ref, turn_ref, inner_ref, filt, arrive):
    tc, ts = (jnp.concatenate([turn_ref[table, i]] * 2, axis=1) for i in range(2))
    if im is None:
        hi, lo = split(re)
        t = jnp.concatenate([mf_ref[table, :, 0:128], mf_ref[table, :, 256:384]], axis=1)
    else:
        hi, lo = split(jnp.concatenate([re, im], axis=0))
        t = mf_ref[table]
    z = dot(wide_table(t, 1), twice(hi, lo, 0))
    yield
    sums, diffs = [], []
    for c in range(2):
        at = c * 512
        dr, di = z[:128, at : at + 256], z[128:, at : at + 256]
        er, ei = z[:128, at + 256 : at + 512], z[128:, at + 256 : at + 512]
        pr, pi = er * tc + ei * ts, ei * tc - er * ts
        for zr, zi, e in ((dr + pr, di + pi, 0), (dr - pr, di - pi, 128)):
            cosine, sine = cross_ref[table, 0, e : e + 128], cross_ref[table, 1, e : e + 128]
            zr, zi = zr * cosine + zi * sine, zi * cosine - zr * sine
            sums.append(jnp.concatenate([zr[:, :128] + zr[:, 128:], zi[:, :128] + zi[:, 128:]], axis=1))
            diffs.append(jnp.concatenate([zr[:, :128] - zr[:, 128:], zi[:, :128] - zi[:, 128:]], axis=1))
    arrive("inner")
    spectra = []
    for odd, rows in enumerate((sums, diffs)):
        hi, lo = split(jnp.concatenate(rows, axis=0))
        spectra.append(dot(twice(hi, lo, 1), wide_table(inner_ref[0, odd], 0)))
    yield
    arrive(("filt", table))
    back = []
    for odd, z in enumerate(spectra):
        rows = []
        for c in range(2):
            zr, zi = z[c * F : (c + 1) * F, :128], z[c * F : (c + 1) * F, 128:]
            fr, fi = filt(0, c, odd), filt(1, c, odd)
            rows.append(jnp.concatenate([zr * fr - zi * fi, zi * fr + zr * fi], axis=1))
        hi, lo = split(jnp.concatenate(rows, axis=0))
        back.append(dot(twice(hi, lo, 1), wide_table(inner_ref[1, odd], 0)))
    yield
    even, odd = back
    tops, bottoms = [], []
    for c in range(2):
        both = []
        for e in (0, 128):
            at = c * F + e
            er, ei = even[at : at + 128, :128], even[at : at + 128, 128:]
            dr, di = odd[at : at + 128, :128], odd[at : at + 128, 128:]
            zr = jnp.concatenate([er + dr, er - dr], axis=1)
            zi = jnp.concatenate([ei + di, ei - di], axis=1)
            cosine = cross_ref[table, 0, e : e + 128] * (1.0 / F)
            sine = cross_ref[table, 1, e : e + 128] * (1.0 / F)
            both.append((zr * cosine - zi * sine, zi * cosine + zr * sine))
        (ar, ai), (br, bi) = both
        ur, ui = ar - br, ai - bi
        tops += [ar + br, ur * tc - ui * ts]
        bottoms += [ai + bi, ui * tc + ur * ts]
    hi, lo = split(jnp.concatenate([jnp.concatenate(tops, axis=1), jnp.concatenate(bottoms, axis=1)], axis=0))
    t = mi_ref[table] if im is not None else mi_ref[table, 0:128]
    yield dot(wide_table(t, 1), twice(hi, lo, 0))


def middle_kernel(y_ref, inner_hbm, bundle_hbm, peak_ref, wave_ref, out_hbm, buf, obuf, *held):
    inner_ref, base_ref, cross_base_ref, filt_ref, other_ref = held[:5]
    mf_ref, mi_ref, cross_ref, turn_ref, out_ref, sem = held[5:]
    special = place_of() % (ND // 2) == 0
    blocks = [pl.ds(m * ROWS, ROWS) for m in range(STEPS)]
    sources = {
        "base": (bundle_hbm.at[14], base_ref),
        "cross": (bundle_hbm.at[pl.ds(12, 2)], cross_base_ref),
        "inner": (inner_hbm, inner_ref),
    }
    for r in range(2):
        for ri in range(2):
            sources["filt", r, ri] = (bundle_hbm.at[pl.ds(r * 4 + ri * 2, 2)], filt_ref.at[r, ri])
    sources["filt", 2] = (bundle_hbm.at[pl.ds(8, 4)], other_ref)
    copies = {k: pltpu.make_async_copy(*v, sem.at[i]) for i, (k, v) in enumerate(sources.items())}
    waiting = set(copies)

    def arrive(key):
        for k in list(copies):
            if k in waiting and (k == key or k[:2] == key):
                waiting.remove(k)
                copies[k].wait()

    for copy in copies.values():
        copy.start()
    peak = peak_ref[0:1, 0:1]
    tables = (mf_ref, mi_ref, cross_ref, turn_ref, inner_ref)
    for m in range(STEPS):
        y = decode(y_ref[blocks[m]].astype(f32), peak, FIELD_CODE).reshape(ROWS * 16, F)
        for g in range(2):
            buf[g, pl.ds(m * ROWS * 16, ROWS * 16), :] = y[:, g * 128 : (g + 1) * 128]
    arrive("base")
    arrive("cross")
    for r in range(2):
        fill_tables(r, base_ref, cross_base_ref, wave_ref, *tables[:4])

    def field(r, ri):
        return jnp.concatenate(
            [
                buf[g, pl.ds(h * 8 + r * 4 + c * 2 + ri, ND, stride=16), :]
                for c in range(2)
                for h in range(2)
                for g in range(2)
            ],
            axis=1,
        )

    def put(z, r, ri, part):
        for c in range(2):
            for h in range(2):
                for g in range(2):
                    at = c * 512 + h * 256 + g * 128
                    obuf[g, pl.ds(h * 8 + r * 4 + c * 2 + ri, ND, stride=16), :] = z[
                        part * 128 : (part + 1) * 128, at : at + 128
                    ]

    def filt_of(r):
        return lambda ri, c, odd: filt_ref[r, ri, c, :, odd * 128 : (odd + 1) * 128]

    running = []
    for r in range(2):
        im = field(r, 1)
        if r == 0:
            im = im * jnp.where(special, 0.0, 1.0)
        running.append(transform(field(r, 0), im, r, *tables, filt_of(r), arrive))
    for stage in range(4):
        for r in range(2):
            z = next(running[r])
            if stage == 3:
                put(z, r, 0, 0)
                put(z, r, 1, 1)

    arrive(("filt", 2))

    @pl.when(special)
    def _():
        fill_tables(2, base_ref, cross_base_ref, wave_ref, *tables[:4])
        *_, z = transform(
            field(0, 1),
            None,
            2,
            *tables,
            lambda ri, c, odd: other_ref[ri * 2 + c, :, odd * 128 : (odd + 1) * 128],
            arrive,
        )
        put(z, 0, 1, 0)

    writes = []
    for m in range(STEPS):
        y = jnp.concatenate([obuf[g, pl.ds(m * ROWS * 16, ROWS * 16), :] for g in range(2)], axis=1)
        out_ref[blocks[m]] = encode(y, peak, FILTERED_CODE).reshape(ROWS, 16, F).astype(bf16)
        writes.append(pltpu.make_async_copy(out_ref.at[blocks[m]], out_hbm.at[blocks[m]], sem.at[len(copies) + m]))
        writes[-1].start()
    for copy in writes:
        copy.wait()


def last_kernel(y_ref, table_ref, peak_ref, out_hbm, buf, out_ref, sem):
    peak = peak_ref[0:1, 0:1]
    for pair in range(2):
        acc = [None, None]
        for step in range(pair * STEPS // 2, (pair + 1) * STEPS // 2):
            y = decode(y_ref[block(step)].astype(f32), peak, FILTERED_CODE)
            for h in range(2):
                hi, lo = split(y[:, h * 8 : h * 8 + 8, :].reshape(ROWS * 8, F))
                res = dot(table_ref[step], twice(hi, lo, 0))
                acc[h] = res if acc[h] is None else acc[h] + res
        for h in range(2):
            for c in range(2):
                for g in range(2):
                    buf[pl.ds(h * 8 + g * 4 + pair * 2 + c, ND, stride=16), :] = acc[h][
                        c * ND : (c + 1) * ND, g * 128 : (g + 1) * 128
                    ]
    writes = []
    for m in range(STEPS):
        y = encode(buf[pl.ds(m * ROWS * 16, ROWS * 16), :], peak, CONV_CODE)
        out_ref[block(m)] = y.reshape(ROWS, 16, 128).astype(bf16)
        writes.append(send_block(out_ref, out_hbm, sem, m))
    for copy in writes:
        copy.wait()


def finish_kernel(y_ref, sig_ref, gate_ref, skip_ref, peak_ref, out_ref, buf):
    peak = peak_ref[0:1, 0:1]
    buf[...] = decode(y_ref[...].astype(f32).reshape(ND * 16, 128), peak, CONV_CODE)
    skip = skip_ref[...]
    for q in range(ND):
        at = pl.ds(q * 512, 512)
        conv = jnp.concatenate([buf[pl.ds(q * 16 + i * 4, 4), :] for i in range(4)], axis=1)
        total = conv + skip * sig_ref[:, at].astype(f32)
        out_ref[:, at] = (gate_ref[:, at].astype(f32) * total).astype(bf16)


VMEM = pl.BlockSpec(memory_space=pltpu.VMEM)
ANY = pl.BlockSpec(memory_space=pl.ANY)


def call(kernel, ins, outs, scratch, name, flops=0, limit=16, grid=(), in_specs=None, out_specs=None):
    size = sum(int(np.prod(x.shape)) * x.dtype.itemsize for x in (*ins, *outs))
    return pl.pallas_call(
        kernel,
        grid_spec=pltpu.PrefetchScalarGridSpec(
            num_scalar_prefetch=0,
            grid=grid,
            in_specs=in_specs or [VMEM] * len(ins),
            out_specs=out_specs or [VMEM] * len(outs),
            scratch_shapes=[pltpu.VMEM(s, d) if s else d for s, d in scratch],
        ),
        out_shape=outs,
        compiler_params=pltpu.CompilerParams(vmem_limit_bytes=limit * 2**20),
        cost_estimate=pl.CostEstimate(flops=flops, bytes_accessed=size, transcendentals=0),
        name=name,
    )(*ins)


def exchange(x):
    return lax.all_to_all(x, AXES, split_axis=0, concat_axis=0, tiled=True)


def shape(*dims, dtype=bf16):
    return jax.ShapeDtypeStruct(dims, dtype)


def per_device(signal, gate, skip, spectrum):
    (packed,) = call(
        pack_kernel,
        (signal,),
        [shape(ND, 4, 640)],
        [(signal.shape, bf16), ((ND, 4, 640), bf16), (None, pltpu.SemaphoreType.DMA((2 * STEPS + 1,)))],
        "pack",
        limit=58,
        in_specs=[ANY],
        out_specs=[ANY],
    )
    spread = exchange(packed)

    plain, back = order_tables()
    given = []
    for r, orders in enumerate(([back, plain], [back])):
        given += call(
            lambda *refs, r=r: give_kernel(r, *refs),
            (jnp.asarray(np.stack(orders)), spectrum),
            [shape(4, F, F)],
            [((1, 4, F, F), f32), ((2, F, F), bf16), ((4, F, F), bf16)]
            + [(None, pltpu.SemaphoreType.DMA((1, 4))), (None, pltpu.SemaphoreType.DMA((5,)))],
            "give",
            limit=58,
            flops=2**29,
            in_specs=[ANY, ANY],
            out_specs=[ANY],
        )
    spread, *_ = lax.optimization_barrier((spread, *given))
    mirror = [(p, (ND // 2 - p) if p % (ND // 2) == 0 else ND - p) for p in range(ND)]
    got = [
        lax.ppermute(given[0], AXES, mirror),
        lax.ppermute(given[1], AXES, [(p, ND - 1 - p) for p in range(ND)]),
    ]

    place = place_of()
    k1 = jnp.stack([place * 2, place * 2 + 1, ND - place * 2])[:, None] % F
    lane = jnp.arange(F, dtype=jnp.int32)
    turns = jnp.stack([k1 * lane % (F * ND) * (F * 2), k1 * lane, (k1 + F * lane) % (F * F) * F], axis=1)
    angle = (2 * np.pi / F**3) * turns.astype(f32)
    wave = jnp.stack([jnp.cos(angle), jnp.sin(angle)], axis=2).reshape(3, 6, F)

    field, peak = call(
        outer_kernel,
        (spread, jnp.asarray(outer_forward_table())),
        [shape(ND, 16, F), shape(8, 128, dtype=f32)],
        [((4, ND * 8, 128), f32), ((ND, 16, F), bf16), (None, pltpu.SemaphoreType.DMA((STEPS,)))],
        "outer",
        flops=2**29,
        out_specs=[ANY, VMEM],
    )
    field = exchange(field)
    base, cross_base = (jnp.asarray(t) for t in base_tables())
    (bundle,) = call(
        combine_kernel,
        (spectrum, jnp.asarray(plain), cross_base, base, *got),
        [shape(15, F, F, dtype=f32)],
        [((2, 4, F, F), f32), ((15, F, F), f32)]
        + [(None, pltpu.SemaphoreType.DMA((2, 4))), (None, pltpu.SemaphoreType.DMA((15,)))],
        "combine",
        limit=51,
        flops=2**34,
        in_specs=[ANY] + [VMEM] * 5,
        out_specs=[ANY],
    )
    (filtered,) = call(
        middle_kernel,
        (field, jnp.asarray(np.stack(inner_tables())), bundle, peak, wave),
        [shape(ND, 16, F)],
        [((2, ND * 16, 128), f32)] * 2
        + [((2, 2, 512, F), bf16), ((F, F), f32), ((2, F, F), f32), ((2, 2, 2, F, F), f32), ((4, F, F), f32)]
        + [((3, 256, 512), bf16)] * 2
        + [((3, 2, F, F), f32), ((3, 2, ND, ND), f32), ((ND, 16, F), bf16)]
        + [(None, pltpu.SemaphoreType.DMA((8 + STEPS,)))],
        "middle",
        flops=4 * 2**30,
        limit=51,
        in_specs=[VMEM, ANY, ANY, VMEM, VMEM],
        out_specs=[ANY],
    )
    filtered = exchange(filtered)
    (conv,) = call(
        last_kernel,
        (filtered, jnp.asarray(outer_inverse_table()), peak),
        [shape(ND, 16, 128)],
        [((ND * 16, 128), f32), ((ND, 16, 128), bf16), (None, pltpu.SemaphoreType.DMA((STEPS,)))],
        "last",
        flops=2**29,
        out_specs=[ANY],
    )
    conv = exchange(conv)
    (mixed,) = call(
        finish_kernel,
        (conv, signal, gate, skip[:, None], peak),
        [shape(4, 65536)],
        [((ND * 16, 128), f32)],
        "finish",
    )
    return mixed


def solution(mesh):
    split_spec = P(None, AXES)
    return jax.shard_map(
        per_device,
        mesh=mesh,
        in_specs=(split_spec, split_spec, P(), P(None, None, AXES, None, None)),
        out_specs=split_spec,
        check_vma=False,
    )
```

```python
import jax
import jax.numpy as jnp
import ml_dtypes
import numpy as np
from jax import lax
from jax.experimental import pallas as pl
from jax.experimental.pallas import tpu as pltpu
from jax.sharding import PartitionSpec as P

F = 256
ND = 128
STEPS = 4
ROWS = ND // STEPS
AXES = ("wide", "narrow")
bf16 = jnp.bfloat16
f32 = jnp.float32

OFFSET = 120.0 * np.log(2.0)
SPAN = 240.0
FIELD_CODE = (2.0**-8, 15.1)
FILTERED_CODE = (2.0**-11, 22.2)
CONV_CODE = (2.0**-7, 21.7)
FILTER_TOP = 6.02


def split_np(x):
    hi = x.astype(ml_dtypes.bfloat16)
    lo = (x - hi.astype(np.float64)).astype(ml_dtypes.bfloat16)
    return hi, lo


def outer_waves():
    k1 = np.arange(F).reshape(ND, 2)
    ang = 2 * np.pi * (k1[:, :, None] * np.arange(ND) % F) / F
    wave = np.stack([np.cos(ang), -np.sin(ang)], axis=2)
    for p in (0, ND // 2):
        wave[p, 0, 1] = np.cos(np.pi * (1 - p // (ND // 2)) * np.arange(ND))
    return wave


def outer_forward_table():
    t = np.zeros((ND, 2, 2, 2, 2, ND))
    for c in range(2):
        t[:, :, c, :, c, :] = outer_waves()
    return np.concatenate(split_np(t.reshape(ND * 8, 2 * ND)), axis=1)


def outer_inverse_table():
    t = np.zeros((2, ND, ND, 2, 2, 2))
    for c in range(2):
        t[c, :, :, :, c, :] = outer_waves().transpose(3, 0, 1, 2)
    hi, lo = (x.reshape(2 * ND, STEPS, -1) for x in split_np(t.reshape(2 * ND, ND * 8)))
    return np.ascontiguousarray(np.concatenate([hi, hi, lo], axis=2).transpose(1, 0, 2))


def inner_tables():
    low = np.arange(ND)
    out = []
    for odd in range(2):
        ang = 2 * np.pi * (low[:, None] * (2 * low[None] + odd) % F) / F
        c, s = np.cos(ang), np.sin(ang)
        fwd = split_np(np.block([[c, -s], [s, c]]))
        inv = split_np(np.block([[c.T, s.T], [-s.T, c.T]]) / F)
        out.append([np.concatenate(x, axis=0) for x in (fwd, inv)])
    return np.stack([out[0][0], out[1][0]]), np.stack([out[0][1], out[1][1]])


def order_tables():
    eye = np.eye(F)
    even_odd = np.concatenate([np.arange(0, F, 2), np.arange(1, F, 2)])
    plain = np.stack([eye, eye[:, even_odd]])
    back = np.stack([eye[::-1], eye[:, 255 - even_odd]])
    return plain.astype(ml_dtypes.bfloat16), back.astype(ml_dtypes.bfloat16)


def base_tables():
    i = np.arange(F)
    half = np.arange(ND)
    a0 = 2 * np.pi * (half[:, None] * half[None] % ND) / ND
    a1 = 2 * np.pi * (i[:, None] * i[None]) / (F * F)
    return (
        np.stack([np.cos(a0), np.sin(a0)]).astype(np.float32),
        np.stack([np.cos(a1), np.sin(a1)]).astype(np.float32),
    )


def peak_of(peak_ref):
    return jnp.maximum(jnp.max(peak_ref[...], keepdims=True), 1e-30)


def encode(x, peak, code):
    knee, octaves = code
    beta = SPAN / octaves
    z = jnp.abs(x) * (1.0 / (peak * knee))
    y = jnp.exp(jnp.minimum(beta * jnp.log(1.0 + z) - OFFSET, OFFSET))
    return jnp.where(x < 0, -y, y)


def decode(y, peak, code):
    knee, octaves = code
    beta = SPAN / octaves
    z = jnp.exp(jnp.log(jnp.abs(y)) * (1.0 / beta) + OFFSET / beta) - 1.0
    z = z * (peak * knee)
    return jnp.where(y < 0, -z, z)


def encode_filter(x):
    y = jnp.exp(jnp.abs(x) * (SPAN * np.log(2.0) / FILTER_TOP) - OFFSET)
    return jnp.where(x < 0, -y, y)


def decode_filter(y):
    z = (jnp.log(jnp.abs(y)) + OFFSET) * (FILTER_TOP / (SPAN * np.log(2.0)))
    return jnp.where(y < 0, -z, z)


def split(x):
    hi = x.astype(bf16)
    return hi, (x - hi.astype(f32)).astype(bf16)


def dot(a, b):
    return jnp.dot(a, b, preferred_element_type=f32)


def twice(hi, lo, axis):
    return jnp.concatenate([hi, lo, hi], axis=axis)


def wide_table(t, axis):
    hi, lo = jnp.split(t, 2, axis=axis)
    return jnp.concatenate([hi, hi, lo], axis=axis)


def block(m):
    return pl.ds(m * ROWS, ROWS)


def send_block(out_ref, out_hbm, sem, m):
    copy = pltpu.make_async_copy(out_ref.at[block(m)], out_hbm.at[block(m)], sem.at[m])
    copy.start()
    return copy


def pack_kernel(sig_hbm, out_hbm, held, out_ref, sem):
    reads = []
    for m in range(STEPS):
        at = pl.ds(m * ROWS * 512, ROWS * 512)
        reads.append(pltpu.make_async_copy(sig_hbm.at[:, at], held.at[:, at], sem.at[m]))
        reads[-1].start()
    writes = []
    top = jnp.zeros((4, 128), f32)
    for m in range(STEPS):
        reads[m].wait()
        for q in range(m * ROWS, (m + 1) * ROWS):
            x = held[:, pl.ds(q * 512, 512)]
            out_ref[q, :, pl.ds(0, 512)] = x
            x = jnp.abs(x.astype(f32))
            for i in range(4):
                top = jnp.maximum(top, x[:, i * 128 : (i + 1) * 128])
        at = (block(m), slice(None), pl.ds(0, 512))
        writes.append(pltpu.make_async_copy(out_ref.at[at], out_hbm.at[at], sem.at[STEPS + m]))
        writes[-1].start()
    top = top.astype(bf16)
    for q in range(ND):
        out_ref[q, :, pl.ds(512, 128)] = top
    at = (slice(None), slice(None), pl.ds(512, 128))
    writes.append(pltpu.make_async_copy(out_ref.at[at], out_hbm.at[at], sem.at[2 * STEPS]))
    writes[-1].start()
    for copy in writes:
        copy.wait()


def outer_kernel(x_ref, table_hbm, out_hbm, peak_ref, buf, out_ref, table_ref, sem):
    load = pltpu.make_async_copy(table_hbm, table_ref, sem.at[STEPS])
    load.start()
    top = jnp.zeros((4, 128), f32)
    for n in range(ND):
        x = x_ref[n].astype(f32)
        top = jnp.maximum(top, x[:, 512:640])
        for i in range(4):
            buf[i, pl.ds(n * 8, 4), :] = x[:, i * 128 : (i + 1) * 128]
    peak = jnp.maximum(jnp.max(top, keepdims=True), 1e-30)
    peak_ref[...] = jnp.broadcast_to(peak, (8, 128))
    load.wait()
    writes = []
    for pair in range(2):
        rows = []
        for c in range(2):
            parts = [buf[i, pl.ds(pair * 2 + c, ND, stride=8), :] for i in range(4)]
            rows.append(jnp.concatenate(parts, axis=1).astype(bf16))
        x = jnp.concatenate(rows + rows, axis=0)
        for m in range(pair * STEPS // 2, (pair + 1) * STEPS // 2):
            res = encode(dot(table_ref[pl.ds(m * ROWS * 8, ROWS * 8), :], x), peak, FIELD_CODE)
            parts = [res[:, h * F : (h + 1) * F].reshape(ROWS, 8, F) for h in range(2)]
            out_ref[block(m)] = jnp.concatenate(parts, axis=1).astype(bf16)
            writes.append(send_block(out_ref, out_hbm, sem, m))
    for copy in writes:
        copy.wait()


def fill_tables(table, base_ref, cross_base_ref, wave_ref, mf_ref, mi_ref, cross_ref, turn_ref):
    def wave(row, lanes):
        return wave_ref[table, row : row + 1, 0:lanes]

    cb, sb = wave(0, ND), wave(1, ND)
    c0, s0 = base_ref[0:128, 0:128], base_ref[128:256, 0:128]
    c, s = c0 * cb - s0 * sb, s0 * cb + c0 * sb
    for out_ref, c, s in ((mf_ref, c, s), (mi_ref, c.T * (1.0 / F), s.T * (-1.0 / F))):
        (ch, cl), (sh, sl) = split(c), split(s)
        for part, (cc, ss) in enumerate(((ch, sh), (cl, sl))):
            at = part * 256
            out_ref[table, 0:128, at : at + 128] = cc
            out_ref[table, 0:128, at + 128 : at + 256] = ss
            out_ref[table, 128:256, at : at + 128] = -ss
            out_ref[table, 128:256, at + 128 : at + 256] = cc
    cb, sb = wave(2, F), wave(3, F)
    c1, s1 = cross_base_ref[0], cross_base_ref[1]
    cross_ref[table, 0] = c1 * cb - s1 * sb
    cross_ref[table, 1] = s1 * cb + c1 * sb
    for i in range(2):
        turn_ref[table, i] = jnp.broadcast_to(wave(4 + i, ND), (ND, ND)).T


def place_of():
    return lax.axis_index("wide") * lax.axis_size("narrow") + lax.axis_index("narrow")


def fetch_filter(slot, r, pair, filt_hbm, held, sem):
    copies = []
    for i in range(4):
        source = filt_hbm.at[i // 2, pair * 2 + i % 2, r]
        copies.append(pltpu.make_async_copy(source, held.at[slot, i], sem.at[slot, i]))
        copies[-1].start()
    return copies


def give_kernel(r, order_hbm, filt_hbm, out_hbm, held, order_ref, out_ref, sem, more):
    place = place_of()
    kind = jnp.where(place == 0, 1, 0) if r == 0 else 0
    order = pltpu.make_async_copy(order_hbm.at[kind], order_ref, more.at[4])
    order.start()
    copies = fetch_filter(0, r, 1 - place // (ND // 2), filt_hbm, held, sem)
    sign = (2 * kind - 1) * jnp.float32(1.0)
    order.wait()
    for copy in copies:
        copy.wait()
    left, right = order_ref[0], order_ref[1]
    writes = []
    for i in range(4):
        hi, lo = split(held[0, i])
        hi, lo = split(dot(hi, right) + dot(lo, right))
        x = dot(left, hi) + dot(left, lo)
        if i >= 2:
            x = x * sign
        out_ref[i] = encode_filter(x).astype(bf16)
        writes.append(pltpu.make_async_copy(out_ref.at[i], out_hbm.at[i], more.at[i]))
        writes[-1].start()
    for copy in writes:
        copy.wait()


def combine_kernel(filt_hbm, order_ref, cross_base_ref, base_ref, got0_ref, got1_ref, out_hbm, held, out_ref, sem, out_sem):
    place = place_of()
    copies = [fetch_filter(r, r, place // (ND // 2), filt_hbm, held, sem) for r in range(2)]
    generic = jnp.where(place % (ND // 2) == 0, 0.0, 1.0)
    out_ref[12:14] = cross_base_ref[...]
    out_ref[14, 0:128, 0:128] = base_ref[0]
    out_ref[14, 128:256, 0:128] = base_ref[1]
    out_ref[14, :, 128:256] = jnp.zeros((F, 128), f32)
    writes = []

    def write(i):
        writes.append(pltpu.make_async_copy(out_ref.at[i], out_hbm.at[i], out_sem.at[i]))
        writes[-1].start()

    for i in (12, 13, 14):
        write(i)
    for copy in (*copies[0], *copies[1]):
        copy.wait()
    for r, got_ref in enumerate((got0_ref, got1_ref)):
        for i in range(4):
            got = decode_filter(got_ref[i].astype(f32))
            if r == 0:
                out_ref[8 + i] = got
                write(8 + i)
                got = got * generic
            hi, lo = split(held[r, i])
            out_ref[r * 4 + i] = dot(hi, order_ref[1]) + dot(lo, order_ref[1]) + got
            write(r * 4 + i)
    for copy in writes:
        copy.wait()


def transform(re, im, table, mf_ref, mi_ref, cross_ref, turn_ref, inner_ref, filt, arrive):
    tc, ts = (jnp.concatenate([turn_ref[table, i]] * 2, axis=1) for i in range(2))
    if im is None:
        hi, lo = split(re)
        t = jnp.concatenate([mf_ref[table, :, 0:128], mf_ref[table, :, 256:384]], axis=1)
    else:
        hi, lo = split(jnp.concatenate([re, im], axis=0))
        t = mf_ref[table]
    z = dot(wide_table(t, 1), twice(hi, lo, 0))
    yield
    sums, diffs = [], []
    for c in range(2):
        at = c * 512
        dr, di = z[:128, at : at + 256], z[128:, at : at + 256]
        er, ei = z[:128, at + 256 : at + 512], z[128:, at + 256 : at + 512]
        pr, pi = er * tc + ei * ts, ei * tc - er * ts
        for zr, zi, e in ((dr + pr, di + pi, 0), (dr - pr, di - pi, 128)):
            cosine, sine = cross_ref[table, 0, e : e + 128], cross_ref[table, 1, e : e + 128]
            zr, zi = zr * cosine + zi * sine, zi * cosine - zr * sine
            sums.append(jnp.concatenate([zr[:, :128] + zr[:, 128:], zi[:, :128] + zi[:, 128:]], axis=1))
            diffs.append(jnp.concatenate([zr[:, :128] - zr[:, 128:], zi[:, :128] - zi[:, 128:]], axis=1))
    arrive("inner")
    spectra = []
    for odd, rows in enumerate((sums, diffs)):
        hi, lo = split(jnp.concatenate(rows, axis=0))
        spectra.append(dot(twice(hi, lo, 1), wide_table(inner_ref[0, odd], 0)))
    yield
    arrive(("filt", table))
    back = []
    for odd, z in enumerate(spectra):
        rows = []
        for c in range(2):
            zr, zi = z[c * F : (c + 1) * F, :128], z[c * F : (c + 1) * F, 128:]
            fr, fi = filt(0, c, odd), filt(1, c, odd)
            rows.append(jnp.concatenate([zr * fr - zi * fi, zi * fr + zr * fi], axis=1))
        hi, lo = split(jnp.concatenate(rows, axis=0))
        back.append(dot(twice(hi, lo, 1), wide_table(inner_ref[1, odd], 0)))
    yield
    even, odd = back
    tops, bottoms = [], []
    for c in range(2):
        both = []
        for e in (0, 128):
            at = c * F + e
            er, ei = even[at : at + 128, :128], even[at : at + 128, 128:]
            dr, di = odd[at : at + 128, :128], odd[at : at + 128, 128:]
            zr = jnp.concatenate([er + dr, er - dr], axis=1)
            zi = jnp.concatenate([ei + di, ei - di], axis=1)
            cosine = cross_ref[table, 0, e : e + 128] * (1.0 / F)
            sine = cross_ref[table, 1, e : e + 128] * (1.0 / F)
            both.append((zr * cosine - zi * sine, zi * cosine + zr * sine))
        (ar, ai), (br, bi) = both
        ur, ui = ar - br, ai - bi
        tops += [ar + br, ur * tc - ui * ts]
        bottoms += [ai + bi, ui * tc + ur * ts]
    hi, lo = split(jnp.concatenate([jnp.concatenate(tops, axis=1), jnp.concatenate(bottoms, axis=1)], axis=0))
    t = mi_ref[table] if im is not None else mi_ref[table, 0:128]
    yield dot(wide_table(t, 1), twice(hi, lo, 0))


def middle_kernel(y_ref, inner_hbm, bundle_hbm, peak_ref, wave_ref, out_hbm, buf, obuf, *held):
    inner_ref, base_ref, cross_base_ref, filt_ref, other_ref = held[:5]
    mf_ref, mi_ref, cross_ref, turn_ref, out_ref, sem = held[5:]
    special = place_of() % (ND // 2) == 0
    blocks = [pl.ds(m * ROWS, ROWS) for m in range(STEPS)]
    sources = {
        "base": (bundle_hbm.at[14], base_ref),
        "cross": (bundle_hbm.at[pl.ds(12, 2)], cross_base_ref),
        "inner": (inner_hbm, inner_ref),
    }
    for r in range(2):
        for ri in range(2):
            sources["filt", r, ri] = (bundle_hbm.at[pl.ds(r * 4 + ri * 2, 2)], filt_ref.at[r, ri])
    sources["filt", 2] = (bundle_hbm.at[pl.ds(8, 4)], other_ref)
    copies = {k: pltpu.make_async_copy(*v, sem.at[i]) for i, (k, v) in enumerate(sources.items())}
    waiting = set(copies)

    def arrive(key):
        for k in list(copies):
            if k in waiting and (k == key or k[:2] == key):
                waiting.remove(k)
                copies[k].wait()

    for copy in copies.values():
        copy.start()
    peak = peak_ref[0:1, 0:1]
    tables = (mf_ref, mi_ref, cross_ref, turn_ref, inner_ref)
    for m in range(STEPS):
        y = decode(y_ref[blocks[m]].astype(f32), peak, FIELD_CODE).reshape(ROWS * 16, F)
        for g in range(2):
            buf[g, pl.ds(m * ROWS * 16, ROWS * 16), :] = y[:, g * 128 : (g + 1) * 128]
    arrive("base")
    arrive("cross")
    for r in range(2):
        fill_tables(r, base_ref, cross_base_ref, wave_ref, *tables[:4])

    def field(r, ri):
        return jnp.concatenate(
            [
                buf[g, pl.ds(h * 8 + r * 4 + c * 2 + ri, ND, stride=16), :]
                for c in range(2)
                for h in range(2)
                for g in range(2)
            ],
            axis=1,
        )

    def put(z, r, ri, part):
        for c in range(2):
            for h in range(2):
                for g in range(2):
                    at = c * 512 + h * 256 + g * 128
                    obuf[g, pl.ds(h * 8 + r * 4 + c * 2 + ri, ND, stride=16), :] = z[
                        part * 128 : (part + 1) * 128, at : at + 128
                    ]

    def filt_of(r):
        return lambda ri, c, odd: filt_ref[r, ri, c, :, odd * 128 : (odd + 1) * 128]

    running = []
    for r in range(2):
        im = field(r, 1)
        if r == 0:
            im = im * jnp.where(special, 0.0, 1.0)
        running.append(transform(field(r, 0), im, r, *tables, filt_of(r), arrive))
    for stage in range(4):
        for r in range(2):
            z = next(running[r])
            if stage == 3:
                put(z, r, 0, 0)
                put(z, r, 1, 1)

    arrive(("filt", 2))

    @pl.when(special)
    def _():
        fill_tables(2, base_ref, cross_base_ref, wave_ref, *tables[:4])
        *_, z = transform(
            field(0, 1),
            None,
            2,
            *tables,
            lambda ri, c, odd: other_ref[ri * 2 + c, :, odd * 128 : (odd + 1) * 128],
            arrive,
        )
        put(z, 0, 1, 0)

    writes = []
    for m in range(STEPS):
        y = jnp.concatenate([obuf[g, pl.ds(m * ROWS * 16, ROWS * 16), :] for g in range(2)], axis=1)
        out_ref[blocks[m]] = encode(y, peak, FILTERED_CODE).reshape(ROWS, 16, F).astype(bf16)
        writes.append(pltpu.make_async_copy(out_ref.at[blocks[m]], out_hbm.at[blocks[m]], sem.at[len(copies) + m]))
        writes[-1].start()
    for copy in writes:
        copy.wait()


def last_kernel(y_ref, table_ref, peak_ref, out_hbm, buf, out_ref, sem):
    peak = peak_ref[0:1, 0:1]
    for pair in range(2):
        acc = [None, None]
        for step in range(pair * STEPS // 2, (pair + 1) * STEPS // 2):
            y = decode(y_ref[block(step)].astype(f32), peak, FILTERED_CODE)
            for h in range(2):
                hi, lo = split(y[:, h * 8 : h * 8 + 8, :].reshape(ROWS * 8, F))
                res = dot(table_ref[step], twice(hi, lo, 0))
                acc[h] = res if acc[h] is None else acc[h] + res
        for h in range(2):
            for c in range(2):
                for g in range(2):
                    buf[pl.ds(h * 8 + g * 4 + pair * 2 + c, ND, stride=16), :] = acc[h][
                        c * ND : (c + 1) * ND, g * 128 : (g + 1) * 128
                    ]
    writes = []
    for m in range(STEPS):
        y = encode(buf[pl.ds(m * ROWS * 16, ROWS * 16), :], peak, CONV_CODE)
        out_ref[block(m)] = y.reshape(ROWS, 16, 128).astype(bf16)
        writes.append(send_block(out_ref, out_hbm, sem, m))
    for copy in writes:
        copy.wait()


def finish_kernel(y_ref, sig_ref, gate_ref, skip_ref, peak_ref, out_ref, buf):
    peak = peak_ref[0:1, 0:1]
    buf[...] = decode(y_ref[...].astype(f32).reshape(ND * 16, 128), peak, CONV_CODE)
    skip = skip_ref[...]
    for q in range(ND):
        at = pl.ds(q * 512, 512)
        conv = jnp.concatenate([buf[pl.ds(q * 16 + i * 4, 4), :] for i in range(4)], axis=1)
        total = conv + skip * sig_ref[:, at].astype(f32)
        out_ref[:, at] = (gate_ref[:, at].astype(f32) * total).astype(bf16)


VMEM = pl.BlockSpec(memory_space=pltpu.VMEM)
ANY = pl.BlockSpec(memory_space=pl.ANY)


def call(kernel, ins, outs, scratch, name, flops=0, limit=16, grid=(), in_specs=None, out_specs=None):
    size = sum(int(np.prod(x.shape)) * x.dtype.itemsize for x in (*ins, *outs))
    return pl.pallas_call(
        kernel,
        grid_spec=pltpu.PrefetchScalarGridSpec(
            num_scalar_prefetch=0,
            grid=grid,
            in_specs=in_specs or [VMEM] * len(ins),
            out_specs=out_specs or [VMEM] * len(outs),
            scratch_shapes=[pltpu.VMEM(s, d) if s else d for s, d in scratch],
        ),
        out_shape=outs,
        compiler_params=pltpu.CompilerParams(vmem_limit_bytes=limit * 2**20),
        cost_estimate=pl.CostEstimate(flops=flops, bytes_accessed=size, transcendentals=0),
        name=name,
    )(*ins)


def exchange(x):
    return lax.all_to_all(x, AXES, split_axis=0, concat_axis=0, tiled=True)


def shape(*dims, dtype=bf16):
    return jax.ShapeDtypeStruct(dims, dtype)


def per_device(signal, gate, skip, spectrum):
    (packed,) = call(
        pack_kernel,
        (signal,),
        [shape(ND, 4, 640)],
        [(signal.shape, bf16), ((ND, 4, 640), bf16), (None, pltpu.SemaphoreType.DMA((2 * STEPS + 1,)))],
        "pack",
        limit=58,
        in_specs=[ANY],
        out_specs=[ANY],
    )
    spread = exchange(packed)

    plain, back = order_tables()
    given = []
    for r, orders in enumerate(([back, plain], [back])):
        given += call(
            lambda *refs, r=r: give_kernel(r, *refs),
            (jnp.asarray(np.stack(orders)), spectrum),
            [shape(4, F, F)],
            [((1, 4, F, F), f32), ((2, F, F), bf16), ((4, F, F), bf16)]
            + [(None, pltpu.SemaphoreType.DMA((1, 4))), (None, pltpu.SemaphoreType.DMA((5,)))],
            "give",
            limit=58,
            flops=2**29,
            in_specs=[ANY, ANY],
            out_specs=[ANY],
        )
    spread, *_ = lax.optimization_barrier((spread, *given))
    mirror = [(p, (ND // 2 - p) if p % (ND // 2) == 0 else ND - p) for p in range(ND)]
    got = [
        lax.ppermute(given[0], AXES, mirror),
        lax.ppermute(given[1], AXES, [(p, ND - 1 - p) for p in range(ND)]),
    ]

    place = place_of()
    k1 = jnp.stack([place * 2, place * 2 + 1, ND - place * 2])[:, None] % F
    lane = jnp.arange(F, dtype=jnp.int32)
    turns = jnp.stack([k1 * lane % (F * ND) * (F * 2), k1 * lane, (k1 + F * lane) % (F * F) * F], axis=1)
    angle = (2 * np.pi / F**3) * turns.astype(f32)
    wave = jnp.stack([jnp.cos(angle), jnp.sin(angle)], axis=2).reshape(3, 6, F)

    field, peak = call(
        outer_kernel,
        (spread, jnp.asarray(outer_forward_table())),
        [shape(ND, 16, F), shape(8, 128, dtype=f32)],
        [((4, ND * 8, 128), f32), ((ND, 16, F), bf16), ((ND * 8, 512), bf16)]
        + [(None, pltpu.SemaphoreType.DMA((STEPS + 1,)))],
        "outer",
        limit=53,
        flops=2**29,
        in_specs=[VMEM, ANY],
        out_specs=[ANY, VMEM],
    )
    field = exchange(field)
    base, cross_base = (jnp.asarray(t) for t in base_tables())
    (bundle,) = call(
        combine_kernel,
        (spectrum, jnp.asarray(plain), cross_base, base, *got),
        [shape(15, F, F, dtype=f32)],
        [((2, 4, F, F), f32), ((15, F, F), f32)]
        + [(None, pltpu.SemaphoreType.DMA((2, 4))), (None, pltpu.SemaphoreType.DMA((15,)))],
        "combine",
        limit=51,
        flops=2**34,
        in_specs=[ANY] + [VMEM] * 5,
        out_specs=[ANY],
    )
    (filtered,) = call(
        middle_kernel,
        (field, jnp.asarray(np.stack(inner_tables())), bundle, peak, wave),
        [shape(ND, 16, F)],
        [((2, ND * 16, 128), f32)] * 2
        + [((2, 2, 512, F), bf16), ((F, F), f32), ((2, F, F), f32), ((2, 2, 2, F, F), f32), ((4, F, F), f32)]
        + [((3, 256, 512), bf16)] * 2
        + [((3, 2, F, F), f32), ((3, 2, ND, ND), f32), ((ND, 16, F), bf16)]
        + [(None, pltpu.SemaphoreType.DMA((8 + STEPS,)))],
        "middle",
        flops=4 * 2**30,
        limit=51,
        in_specs=[VMEM, ANY, ANY, VMEM, VMEM],
        out_specs=[ANY],
    )
    filtered = exchange(filtered)
    (conv,) = call(
        last_kernel,
        (filtered, jnp.asarray(outer_inverse_table()), peak),
        [shape(ND, 16, 128)],
        [((ND * 16, 128), f32), ((ND, 16, 128), bf16), (None, pltpu.SemaphoreType.DMA((STEPS,)))],
        "last",
        flops=2**29,
        out_specs=[ANY],
    )
    conv = exchange(conv)
    (mixed,) = call(
        finish_kernel,
        (conv, signal, gate, skip[:, None], peak),
        [shape(4, 65536)],
        [((ND * 16, 128), f32)],
        "finish",
    )
    return mixed


def solution(mesh):
    split_spec = P(None, AXES)
    return jax.shard_map(
        per_device,
        mesh=mesh,
        in_specs=(split_spec, split_spec, P(), P(None, None, AXES, None, None)),
        out_specs=split_spec,
        check_vma=False,
    )
```

```python
import jax
import jax.numpy as jnp
import ml_dtypes
import numpy as np
from jax import lax
from jax.experimental import pallas as pl
from jax.experimental.pallas import tpu as pltpu
from jax.sharding import PartitionSpec as P

F = 256
ND = 128
STEPS = 4
ROWS = ND // STEPS
AXES = ("wide", "narrow")
bf16 = jnp.bfloat16
f32 = jnp.float32

OFFSET = 120.0 * np.log(2.0)
SPAN = 240.0
FIELD_CODE = (2.0**-8, 15.1)
FILTERED_CODE = (2.0**-11, 22.2)
CONV_CODE = (2.0**-7, 21.7)
FILTER_TOP = 6.02


def split_np(x):
    hi = x.astype(ml_dtypes.bfloat16)
    lo = (x - hi.astype(np.float64)).astype(ml_dtypes.bfloat16)
    return hi, lo


def outer_waves():
    k1 = np.arange(F).reshape(ND, 2)
    ang = 2 * np.pi * (k1[:, :, None] * np.arange(ND) % F) / F
    wave = np.stack([np.cos(ang), -np.sin(ang)], axis=2)
    for p in (0, ND // 2):
        wave[p, 0, 1] = np.cos(np.pi * (1 - p // (ND // 2)) * np.arange(ND))
    return wave


def outer_forward_table():
    t = np.zeros((ND, 2, 2, 2, 2, ND))
    for c in range(2):
        t[:, :, c, :, c, :] = outer_waves()
    return np.concatenate(split_np(t.reshape(ND * 8, 2 * ND)), axis=1)


def outer_inverse_table():
    t = np.zeros((2, ND, ND, 2, 2, 2))
    for c in range(2):
        t[c, :, :, :, c, :] = outer_waves().transpose(3, 0, 1, 2)
    hi, lo = (x.reshape(2 * ND, STEPS, -1) for x in split_np(t.reshape(2 * ND, ND * 8)))
    return np.ascontiguousarray(np.concatenate([hi, hi, lo], axis=2).transpose(1, 0, 2))


def inner_tables():
    low = np.arange(ND)
    out = []
    for odd in range(2):
        ang = 2 * np.pi * (low[:, None] * (2 * low[None] + odd) % F) / F
        c, s = np.cos(ang), np.sin(ang)
        fwd = split_np(np.block([[c, -s], [s, c]]))
        inv = split_np(np.block([[c.T, s.T], [-s.T, c.T]]) / F)
        out.append([np.concatenate(x, axis=0) for x in (fwd, inv)])
    return np.stack([out[0][0], out[1][0]]), np.stack([out[0][1], out[1][1]])


def order_tables():
    eye = np.eye(F)
    even_odd = np.concatenate([np.arange(0, F, 2), np.arange(1, F, 2)])
    plain = np.stack([eye, eye[:, even_odd]])
    back = np.stack([eye[::-1], eye[:, 255 - even_odd]])
    return plain.astype(ml_dtypes.bfloat16), back.astype(ml_dtypes.bfloat16)


def base_tables():
    i = np.arange(F)
    half = np.arange(ND)
    a0 = 2 * np.pi * (half[:, None] * half[None] % ND) / ND
    a1 = 2 * np.pi * (i[:, None] * i[None]) / (F * F)
    return (
        np.stack([np.cos(a0), np.sin(a0)]).astype(np.float32),
        np.stack([np.cos(a1), np.sin(a1)]).astype(np.float32),
    )


def peak_of(peak_ref):
    return jnp.maximum(jnp.max(peak_ref[...], keepdims=True), 1e-30)


def encode(x, peak, code):
    knee, octaves = code
    beta = SPAN / octaves
    z = jnp.abs(x) * (1.0 / (peak * knee))
    y = jnp.exp(jnp.minimum(beta * jnp.log(1.0 + z) - OFFSET, OFFSET))
    return jnp.where(x < 0, -y, y)


def decode(y, peak, code):
    knee, octaves = code
    beta = SPAN / octaves
    z = jnp.exp(jnp.log(jnp.abs(y)) * (1.0 / beta) + OFFSET / beta) - 1.0
    z = z * (peak * knee)
    return jnp.where(y < 0, -z, z)


def encode_filter(x):
    y = jnp.exp(jnp.abs(x) * (SPAN * np.log(2.0) / FILTER_TOP) - OFFSET)
    return jnp.where(x < 0, -y, y)


def decode_filter(y):
    z = (jnp.log(jnp.abs(y)) + OFFSET) * (FILTER_TOP / (SPAN * np.log(2.0)))
    return jnp.where(y < 0, -z, z)


def split(x):
    hi = x.astype(bf16)
    return hi, (x - hi.astype(f32)).astype(bf16)


def dot(a, b):
    return jnp.dot(a, b, preferred_element_type=f32)


def twice(hi, lo, axis):
    return jnp.concatenate([hi, lo, hi], axis=axis)


def wide_table(t, axis):
    hi, lo = jnp.split(t, 2, axis=axis)
    return jnp.concatenate([hi, hi, lo], axis=axis)


def block(m):
    return pl.ds(m * ROWS, ROWS)


def send_block(out_ref, out_hbm, sem, m):
    copy = pltpu.make_async_copy(out_ref.at[block(m)], out_hbm.at[block(m)], sem.at[m])
    copy.start()
    return copy


def pack_kernel(sig_hbm, out_hbm, held, out_ref, sem):
    reads = []
    for m in range(STEPS):
        at = pl.ds(m * ROWS * 512, ROWS * 512)
        reads.append(pltpu.make_async_copy(sig_hbm.at[:, at], held.at[:, at], sem.at[m]))
        reads[-1].start()
    writes = []
    top = jnp.zeros((4, 128), f32)
    for m in range(STEPS):
        reads[m].wait()
        for q in range(m * ROWS, (m + 1) * ROWS):
            x = held[:, pl.ds(q * 512, 512)]
            out_ref[q, :, pl.ds(0, 512)] = x
            x = jnp.abs(x.astype(f32))
            for i in range(4):
                top = jnp.maximum(top, x[:, i * 128 : (i + 1) * 128])
        at = (block(m), slice(None), pl.ds(0, 512))
        writes.append(pltpu.make_async_copy(out_ref.at[at], out_hbm.at[at], sem.at[STEPS + m]))
        writes[-1].start()
    top = top.astype(bf16)
    for q in range(ND):
        out_ref[q, :, pl.ds(512, 128)] = top
    at = (slice(None), slice(None), pl.ds(512, 128))
    writes.append(pltpu.make_async_copy(out_ref.at[at], out_hbm.at[at], sem.at[2 * STEPS]))
    writes[-1].start()
    for copy in writes:
        copy.wait()


def outer_kernel(x_ref, table_ref, out_hbm, peak_ref, buf, out_ref, sem):
    top = jnp.zeros((4, 128), f32)
    for n in range(ND):
        x = x_ref[n].astype(f32)
        top = jnp.maximum(top, x[:, 512:640])
        for i in range(4):
            buf[i, pl.ds(n * 8, 4), :] = x[:, i * 128 : (i + 1) * 128]
    peak = jnp.maximum(jnp.max(top, keepdims=True), 1e-30)
    peak_ref[...] = jnp.broadcast_to(peak, (8, 128))
    writes = []
    for pair in range(2):
        rows = []
        for c in range(2):
            parts = [buf[i, pl.ds(pair * 2 + c, ND, stride=8), :] for i in range(4)]
            rows.append(jnp.concatenate(parts, axis=1).astype(bf16))
        x = jnp.concatenate(rows + rows, axis=0)
        for m in range(pair * STEPS // 2, (pair + 1) * STEPS // 2):
            res = encode(dot(table_ref[pl.ds(m * ROWS * 8, ROWS * 8), :], x), peak, FIELD_CODE)
            parts = [res[:, h * F : (h + 1) * F].reshape(ROWS, 8, F) for h in range(2)]
            out_ref[block(m)] = jnp.concatenate(parts, axis=1).astype(bf16)
            writes.append(send_block(out_ref, out_hbm, sem, m))
    for copy in writes:
        copy.wait()


def fill_tables(table, base_ref, cross_base_ref, wave_ref, mf_ref, mi_ref, cross_ref, turn_ref):
    def wave(row, lanes):
        return wave_ref[table, row : row + 1, 0:lanes]

    cb, sb = wave(0, ND), wave(1, ND)
    c0, s0 = base_ref[0:128, 0:128], base_ref[128:256, 0:128]
    c, s = c0 * cb - s0 * sb, s0 * cb + c0 * sb
    for out_ref, c, s in ((mf_ref, c, s), (mi_ref, c.T * (1.0 / F), s.T * (-1.0 / F))):
        (ch, cl), (sh, sl) = split(c), split(s)
        for part, (cc, ss) in enumerate(((ch, sh), (cl, sl))):
            at = part * 256
            out_ref[table, 0:128, at : at + 128] = cc
            out_ref[table, 0:128, at + 128 : at + 256] = ss
            out_ref[table, 128:256, at : at + 128] = -ss
            out_ref[table, 128:256, at + 128 : at + 256] = cc
    cb, sb = wave(2, F), wave(3, F)
    c1, s1 = cross_base_ref[0], cross_base_ref[1]
    cross_ref[table, 0] = c1 * cb - s1 * sb
    cross_ref[table, 1] = s1 * cb + c1 * sb
    for i in range(2):
        turn_ref[table, i] = jnp.broadcast_to(wave(4 + i, ND), (ND, ND)).T


def place_of():
    return lax.axis_index("wide") * lax.axis_size("narrow") + lax.axis_index("narrow")


def fetch_filter(slot, r, pair, filt_hbm, held, sem):
    copies = []
    for i in range(4):
        source = filt_hbm.at[i // 2, pair * 2 + i % 2, r]
        copies.append(pltpu.make_async_copy(source, held.at[slot, i], sem.at[slot, i]))
        copies[-1].start()
    return copies


def give_kernel(r, order_hbm, filt_hbm, out_hbm, held, order_ref, out_ref, sem, more):
    place = place_of()
    kind = jnp.where(place == 0, 1, 0) if r == 0 else 0
    order = pltpu.make_async_copy(order_hbm.at[kind], order_ref, more.at[4])
    order.start()
    copies = fetch_filter(0, r, 1 - place // (ND // 2), filt_hbm, held, sem)
    sign = (2 * kind - 1) * jnp.float32(1.0)
    order.wait()
    for copy in copies:
        copy.wait()
    left, right = order_ref[0], order_ref[1]
    writes = []
    for i in range(4):
        hi, lo = split(held[0, i])
        hi, lo = split(dot(hi, right) + dot(lo, right))
        x = dot(left, hi) + dot(left, lo)
        if i >= 2:
            x = x * sign
        out_ref[i] = encode_filter(x).astype(bf16)
        writes.append(pltpu.make_async_copy(out_ref.at[i], out_hbm.at[i], more.at[i]))
        writes[-1].start()
    for copy in writes:
        copy.wait()


def combine_kernel(filt_hbm, order_ref, cross_base_ref, base_ref, got0_ref, got1_ref, out_hbm, held, out_ref, sem, out_sem):
    place = place_of()
    copies = [fetch_filter(r, r, place // (ND // 2), filt_hbm, held, sem) for r in range(2)]
    generic = jnp.where(place % (ND // 2) == 0, 0.0, 1.0)
    out_ref[12:14] = cross_base_ref[...]
    out_ref[14, 0:128, 0:128] = base_ref[0]
    out_ref[14, 128:256, 0:128] = base_ref[1]
    out_ref[14, :, 128:256] = jnp.zeros((F, 128), f32)
    writes = []

    def write(i):
        writes.append(pltpu.make_async_copy(out_ref.at[i], out_hbm.at[i], out_sem.at[i]))
        writes[-1].start()

    for i in (12, 13, 14):
        write(i)
    for copy in (*copies[0], *copies[1]):
        copy.wait()
    for r, got_ref in enumerate((got0_ref, got1_ref)):
        for i in range(4):
            got = decode_filter(got_ref[i].astype(f32))
            if r == 0:
                out_ref[8 + i] = got
                write(8 + i)
                got = got * generic
            hi, lo = split(held[r, i])
            out_ref[r * 4 + i] = dot(hi, order_ref[1]) + dot(lo, order_ref[1]) + got
            write(r * 4 + i)
    for copy in writes:
        copy.wait()


def transform(re, im, table, mf_ref, mi_ref, cross_ref, turn_ref, inner_ref, filt, arrive):
    tc, ts = (jnp.concatenate([turn_ref[table, i]] * 2, axis=1) for i in range(2))
    if im is None:
        hi, lo = split(re)
        t = jnp.concatenate([mf_ref[table, :, 0:128], mf_ref[table, :, 256:384]], axis=1)
    else:
        hi, lo = split(jnp.concatenate([re, im], axis=0))
        t = mf_ref[table]
    z = dot(wide_table(t, 1), twice(hi, lo, 0))
    yield
    sums, diffs = [], []
    for c in range(2):
        at = c * 512
        dr, di = z[:128, at : at + 256], z[128:, at : at + 256]
        er, ei = z[:128, at + 256 : at + 512], z[128:, at + 256 : at + 512]
        pr, pi = er * tc + ei * ts, ei * tc - er * ts
        for zr, zi, e in ((dr + pr, di + pi, 0), (dr - pr, di - pi, 128)):
            cosine, sine = cross_ref[table, 0, e : e + 128], cross_ref[table, 1, e : e + 128]
            zr, zi = zr * cosine + zi * sine, zi * cosine - zr * sine
            sums.append(jnp.concatenate([zr[:, :128] + zr[:, 128:], zi[:, :128] + zi[:, 128:]], axis=1))
            diffs.append(jnp.concatenate([zr[:, :128] - zr[:, 128:], zi[:, :128] - zi[:, 128:]], axis=1))
    arrive("inner")
    spectra = []
    for odd, rows in enumerate((sums, diffs)):
        hi, lo = split(jnp.concatenate(rows, axis=0))
        spectra.append(dot(twice(hi, lo, 1), wide_table(inner_ref[0, odd], 0)))
    yield
    arrive(("filt", table))
    back = []
    for odd, z in enumerate(spectra):
        rows = []
        for c in range(2):
            zr, zi = z[c * F : (c + 1) * F, :128], z[c * F : (c + 1) * F, 128:]
            fr, fi = filt(0, c, odd), filt(1, c, odd)
            rows.append(jnp.concatenate([zr * fr - zi * fi, zi * fr + zr * fi], axis=1))
        hi, lo = split(jnp.concatenate(rows, axis=0))
        back.append(dot(twice(hi, lo, 1), wide_table(inner_ref[1, odd], 0)))
    yield
    even, odd = back
    tops, bottoms = [], []
    for c in range(2):
        both = []
        for e in (0, 128):
            at = c * F + e
            er, ei = even[at : at + 128, :128], even[at : at + 128, 128:]
            dr, di = odd[at : at + 128, :128], odd[at : at + 128, 128:]
            zr = jnp.concatenate([er + dr, er - dr], axis=1)
            zi = jnp.concatenate([ei + di, ei - di], axis=1)
            cosine = cross_ref[table, 0, e : e + 128] * (1.0 / F)
            sine = cross_ref[table, 1, e : e + 128] * (1.0 / F)
            both.append((zr * cosine - zi * sine, zi * cosine + zr * sine))
        (ar, ai), (br, bi) = both
        ur, ui = ar - br, ai - bi
        tops += [ar + br, ur * tc - ui * ts]
        bottoms += [ai + bi, ui * tc + ur * ts]
    hi, lo = split(jnp.concatenate([jnp.concatenate(tops, axis=1), jnp.concatenate(bottoms, axis=1)], axis=0))
    t = mi_ref[table] if im is not None else mi_ref[table, 0:128]
    yield dot(wide_table(t, 1), twice(hi, lo, 0))


def middle_kernel(y_ref, inner_hbm, bundle_hbm, peak_ref, wave_ref, out_hbm, buf, obuf, *held):
    inner_ref, base_ref, cross_base_ref, filt_ref, other_ref = held[:5]
    mf_ref, mi_ref, cross_ref, turn_ref, out_ref, sem = held[5:]
    special = place_of() % (ND // 2) == 0
    blocks = [pl.ds(m * ROWS, ROWS) for m in range(STEPS)]
    sources = {
        "base": (bundle_hbm.at[14], base_ref),
        "cross": (bundle_hbm.at[pl.ds(12, 2)], cross_base_ref),
        "inner": (inner_hbm, inner_ref),
    }
    for r in range(2):
        for ri in range(2):
            sources["filt", r, ri] = (bundle_hbm.at[pl.ds(r * 4 + ri * 2, 2)], filt_ref.at[r, ri])
    sources["filt", 2] = (bundle_hbm.at[pl.ds(8, 4)], other_ref)
    copies = {k: pltpu.make_async_copy(*v, sem.at[i]) for i, (k, v) in enumerate(sources.items())}
    waiting = set(copies)

    def arrive(key):
        for k in list(copies):
            if k in waiting and (k == key or k[:2] == key):
                waiting.remove(k)
                copies[k].wait()

    for copy in copies.values():
        copy.start()
    peak = peak_ref[0:1, 0:1]
    tables = (mf_ref, mi_ref, cross_ref, turn_ref, inner_ref)
    for m in range(STEPS):
        y = decode(y_ref[blocks[m]].astype(f32), peak, FIELD_CODE).reshape(ROWS * 16, F)
        for g in range(2):
            buf[g, pl.ds(m * ROWS * 16, ROWS * 16), :] = y[:, g * 128 : (g + 1) * 128]
    arrive("base")
    arrive("cross")
    for r in range(2):
        fill_tables(r, base_ref, cross_base_ref, wave_ref, *tables[:4])

    def field(r, ri):
        return jnp.concatenate(
            [
                buf[g, pl.ds(h * 8 + r * 4 + c * 2 + ri, ND, stride=16), :]
                for c in range(2)
                for h in range(2)
                for g in range(2)
            ],
            axis=1,
        )

    def put(z, r, ri, part):
        for c in range(2):
            for h in range(2):
                for g in range(2):
                    at = c * 512 + h * 256 + g * 128
                    obuf[g, pl.ds(h * 8 + r * 4 + c * 2 + ri, ND, stride=16), :] = z[
                        part * 128 : (part + 1) * 128, at : at + 128
                    ]

    def filt_of(r):
        return lambda ri, c, odd: filt_ref[r, ri, c, :, odd * 128 : (odd + 1) * 128]

    running = []
    for r in range(2):
        im = field(r, 1)
        if r == 0:
            im = im * jnp.where(special, 0.0, 1.0)
        running.append(transform(field(r, 0), im, r, *tables, filt_of(r), arrive))
    for stage in range(4):
        for r in range(2):
            z = next(running[r])
            if stage == 3:
                put(z, r, 0, 0)
                put(z, r, 1, 1)

    arrive(("filt", 2))

    @pl.when(special)
    def _():
        fill_tables(2, base_ref, cross_base_ref, wave_ref, *tables[:4])
        *_, z = transform(
            field(0, 1),
            None,
            2,
            *tables,
            lambda ri, c, odd: other_ref[ri * 2 + c, :, odd * 128 : (odd + 1) * 128],
            arrive,
        )
        put(z, 0, 1, 0)

    writes = []
    for m in range(STEPS):
        y = jnp.concatenate([obuf[g, pl.ds(m * ROWS * 16, ROWS * 16), :] for g in range(2)], axis=1)
        out_ref[blocks[m]] = encode(y, peak, FILTERED_CODE).reshape(ROWS, 16, F).astype(bf16)
        writes.append(pltpu.make_async_copy(out_ref.at[blocks[m]], out_hbm.at[blocks[m]], sem.at[len(copies) + m]))
        writes[-1].start()
    for copy in writes:
        copy.wait()


def last_kernel(y_ref, table_ref, peak_ref, out_hbm, buf, out_ref, sem):
    peak = peak_ref[0:1, 0:1]
    for pair in range(2):
        acc = [None, None]
        for step in range(pair * STEPS // 2, (pair + 1) * STEPS // 2):
            y = decode(y_ref[block(step)].astype(f32), peak, FILTERED_CODE)
            for h in range(2):
                hi, lo = split(y[:, h * 8 : h * 8 + 8, :].reshape(ROWS * 8, F))
                res = dot(table_ref[step], twice(hi, lo, 0))
                acc[h] = res if acc[h] is None else acc[h] + res
        for h in range(2):
            for c in range(2):
                for g in range(2):
                    buf[pl.ds(h * 8 + g * 4 + pair * 2 + c, ND, stride=16), :] = acc[h][
                        c * ND : (c + 1) * ND, g * 128 : (g + 1) * 128
                    ]
    writes = []
    for m in range(STEPS):
        y = encode(buf[pl.ds(m * ROWS * 16, ROWS * 16), :], peak, CONV_CODE)
        out_ref[block(m)] = y.reshape(ROWS, 16, 128).astype(bf16)
        writes.append(send_block(out_ref, out_hbm, sem, m))
    for copy in writes:
        copy.wait()


def finish_kernel(y_ref, sig_ref, gate_ref, skip_ref, peak_ref, out_hbm, buf, out_ref, sem):
    peak = peak_ref[0:1, 0:1]
    buf[...] = decode(y_ref[...].astype(f32).reshape(ND * 16, 128), peak, CONV_CODE)
    skip = skip_ref[...]
    writes = []
    for q in range(ND):
        at = pl.ds(q * 512, 512)
        conv = jnp.concatenate([buf[pl.ds(q * 16 + i * 4, 4), :] for i in range(4)], axis=1)
        total = conv + skip * sig_ref[:, at].astype(f32)
        out_ref[:, at] = (gate_ref[:, at].astype(f32) * total).astype(bf16)
        if q % ROWS == ROWS - 1:
            at = pl.ds((q + 1 - ROWS) * 512, ROWS * 512)
            writes.append(pltpu.make_async_copy(out_ref.at[:, at], out_hbm.at[:, at], sem.at[q // ROWS]))
            writes[-1].start()
    for copy in writes:
        copy.wait()


VMEM = pl.BlockSpec(memory_space=pltpu.VMEM)
ANY = pl.BlockSpec(memory_space=pl.ANY)


def call(kernel, ins, outs, scratch, name, flops=0, limit=16, grid=(), in_specs=None, out_specs=None):
    size = sum(int(np.prod(x.shape)) * x.dtype.itemsize for x in (*ins, *outs))
    return pl.pallas_call(
        kernel,
        grid_spec=pltpu.PrefetchScalarGridSpec(
            num_scalar_prefetch=0,
            grid=grid,
            in_specs=in_specs or [VMEM] * len(ins),
            out_specs=out_specs or [VMEM] * len(outs),
            scratch_shapes=[pltpu.VMEM(s, d) if s else d for s, d in scratch],
        ),
        out_shape=outs,
        compiler_params=pltpu.CompilerParams(vmem_limit_bytes=limit * 2**20),
        cost_estimate=pl.CostEstimate(flops=flops, bytes_accessed=size, transcendentals=0),
        name=name,
    )(*ins)


def exchange(x):
    return lax.all_to_all(x, AXES, split_axis=0, concat_axis=0, tiled=True)


def shape(*dims, dtype=bf16):
    return jax.ShapeDtypeStruct(dims, dtype)


def per_device(signal, gate, skip, spectrum):
    (packed,) = call(
        pack_kernel,
        (signal,),
        [shape(ND, 4, 640)],
        [(signal.shape, bf16), ((ND, 4, 640), bf16), (None, pltpu.SemaphoreType.DMA((2 * STEPS + 1,)))],
        "pack",
        limit=58,
        in_specs=[ANY],
        out_specs=[ANY],
    )
    spread = exchange(packed)

    plain, back = order_tables()
    given = []
    for r, orders in enumerate(([back, plain], [back])):
        given += call(
            lambda *refs, r=r: give_kernel(r, *refs),
            (jnp.asarray(np.stack(orders)), spectrum),
            [shape(4, F, F)],
            [((1, 4, F, F), f32), ((2, F, F), bf16), ((4, F, F), bf16)]
            + [(None, pltpu.SemaphoreType.DMA((1, 4))), (None, pltpu.SemaphoreType.DMA((5,)))],
            "give",
            limit=58,
            flops=2**29,
            in_specs=[ANY, ANY],
            out_specs=[ANY],
        )
    spread, *_ = lax.optimization_barrier((spread, *given))
    mirror = [(p, (ND // 2 - p) if p % (ND // 2) == 0 else ND - p) for p in range(ND)]
    got = [
        lax.ppermute(given[0], AXES, mirror),
        lax.ppermute(given[1], AXES, [(p, ND - 1 - p) for p in range(ND)]),
    ]

    place = place_of()
    k1 = jnp.stack([place * 2, place * 2 + 1, ND - place * 2])[:, None] % F
    lane = jnp.arange(F, dtype=jnp.int32)
    turns = jnp.stack([k1 * lane % (F * ND) * (F * 2), k1 * lane, (k1 + F * lane) % (F * F) * F], axis=1)
    angle = (2 * np.pi / F**3) * turns.astype(f32)
    wave = jnp.stack([jnp.cos(angle), jnp.sin(angle)], axis=2).reshape(3, 6, F)

    field, peak = call(
        outer_kernel,
        (spread, jnp.asarray(outer_forward_table())),
        [shape(ND, 16, F), shape(8, 128, dtype=f32)],
        [((4, ND * 8, 128), f32), ((ND, 16, F), bf16), (None, pltpu.SemaphoreType.DMA((STEPS,)))],
        "outer",
        flops=2**29,
        out_specs=[ANY, VMEM],
    )
    field = exchange(field)
    base, cross_base = (jnp.asarray(t) for t in base_tables())
    (bundle,) = call(
        combine_kernel,
        (spectrum, jnp.asarray(plain), cross_base, base, *got),
        [shape(15, F, F, dtype=f32)],
        [((2, 4, F, F), f32), ((15, F, F), f32)]
        + [(None, pltpu.SemaphoreType.DMA((2, 4))), (None, pltpu.SemaphoreType.DMA((15,)))],
        "combine",
        limit=51,
        flops=2**34,
        in_specs=[ANY] + [VMEM] * 5,
        out_specs=[ANY],
    )
    (filtered,) = call(
        middle_kernel,
        (field, jnp.asarray(np.stack(inner_tables())), bundle, peak, wave),
        [shape(ND, 16, F)],
        [((2, ND * 16, 128), f32)] * 2
        + [((2, 2, 512, F), bf16), ((F, F), f32), ((2, F, F), f32), ((2, 2, 2, F, F), f32), ((4, F, F), f32)]
        + [((3, 256, 512), bf16)] * 2
        + [((3, 2, F, F), f32), ((3, 2, ND, ND), f32), ((ND, 16, F), bf16)]
        + [(None, pltpu.SemaphoreType.DMA((8 + STEPS,)))],
        "middle",
        flops=4 * 2**30,
        limit=51,
        in_specs=[VMEM, ANY, ANY, VMEM, VMEM],
        out_specs=[ANY],
    )
    filtered = exchange(filtered)
    (conv,) = call(
        last_kernel,
        (filtered, jnp.asarray(outer_inverse_table()), peak),
        [shape(ND, 16, 128)],
        [((ND * 16, 128), f32), ((ND, 16, 128), bf16), (None, pltpu.SemaphoreType.DMA((STEPS,)))],
        "last",
        flops=2**29,
        out_specs=[ANY],
    )
    conv = exchange(conv)
    (mixed,) = call(
        finish_kernel,
        (conv, signal, gate, skip[:, None], peak),
        [shape(4, 65536)],
        [((ND * 16, 128), f32), (signal.shape, bf16), (None, pltpu.SemaphoreType.DMA((STEPS,)))],
        "finish",
        out_specs=[ANY],
    )
    return mixed


def solution(mesh):
    split_spec = P(None, AXES)
    return jax.shard_map(
        per_device,
        mesh=mesh,
        in_specs=(split_spec, split_spec, P(), P(None, None, AXES, None, None)),
        out_specs=split_spec,
        check_vma=False,
    )
```
